256 devices in a mesh: xy: 64 (over y, x, z_lo, core), gz: 4 (over z_hi).
Axes of the slice: x: 4, y: 4, z: 8 (z_hi: 4, z_lo: 2; z = z_hi * 2 + z_lo), core: 2. Of those that a mesh axis runs over, the one named last changes fastest.
Arguments:
- target: bfloat16 [4096, 256, 1024], P('xy', None, 'gz'), may hold values from -6 to 6
- plane_xy: bfloat16 [32, 4096, 256], P(None, 'xy'), may hold values from -1.796875 to 1.796875
- plane_xz: bfloat16 [32, 4096, 1024], P(None, 'xy', 'gz'), may hold values from -1.796875 to 1.796875
- plane_yz: bfloat16 [32, 256, 1024], P(None, 'xy', 'gz'), may hold values from -1.796875 to 1.796875
- line_x: bfloat16 [32, 4096], P(None, 'xy'), may hold values from -2.09375 to 2.09375
- line_y: bfloat16 [32, 256], replicated, may hold values from -2.09375 to 2.09375
- line_z: bfloat16 [32, 1024], P(None, 'gz'), may hold values from -2.09375 to 2.09375
Outputs:
- new_plane_xy: bfloat16 [32, 4096, 256], P(None, 'xy')
- new_plane_xz: bfloat16 [32, 4096, 1024], P(None, 'xy', 'gz')
- new_plane_yz: bfloat16 [32, 256, 1024], P(None, 'xy', 'gz')
- new_line_x: bfloat16 [32, 4096], P(None, 'xy')
- new_line_y: bfloat16 [32, 256], replicated
- new_line_z: bfloat16 [32, 1024], P(None, 'gz')
The draws below stay inside these ranges and needn't reach their ends.
All inputs are finite; a program needn't handle non-finite values.
Results may differ from the reference program's by a relative error of at most 0.0056.
Values may be sent and summed in bfloat16 or wider, within the bound.
No kernel may reach another device: no remote copies, remote signals or barrier semaphores. Data moves between devices by JAX's collectives and lax.ppermute only.
A program may use at most 192 MiB of HBM per device.

```python
import jax
import jax.numpy as jnp
from jax import lax

R = 32
CX = 64
NY = 256
NX = 4096
NZ = 1024


def levels(rng, shape, pieces, low, high):
    factor_of, own = 1.0, jax.random.fold_in(rng, 6)
    for dim, parts in pieces:
        heights = jnp.exp(jax.random.uniform(jax.random.fold_in(own, dim), (parts,), jnp.float32, low / len(pieces), high / len(pieces)))
        factor_of = factor_of * jnp.repeat(heights, shape[dim] // parts).reshape([-1 if axis == dim else 1 for axis in range(len(shape))])
    return factor_of


def centred(key, dims, scale, limit, shards=(), kind=jnp.bfloat16):
    array = scale * jax.random.normal(key, dims, jnp.float32)
    if shards:
        array = array * levels(key, dims, shards, -0.22, 0.18)
    return jnp.clip(array, -limit, limit).astype(kind)


def setup_inputs(seed: int = 0) -> dict:
    splits = jax.random.split(jax.random.key(seed), 8)
    target = centred(splits[0], (NX, NY, NZ), 1.0, 6.0, ((0, 64), (2, 4)))
    plane_xy = centred(splits[1], (R, NX, NY), 0.3, 1.796875, ((1, 64),))
    plane_xz = centred(splits[2], (R, NX, NZ), 0.3, 1.796875, ((1, 64), (2, 4)))
    plane_yz = centred(splits[3], (R, NY, NZ), 0.3, 1.796875, ((1, 64), (2, 4)))
    line_x = centred(splits[4], (R, NX), 0.35, 2.09375, ((1, 64),))
    line_y = centred(splits[5], (R, NY), 0.35, 2.09375)
    line_z = centred(splits[6], (R, NZ), 0.35, 2.09375, ((1, 4),))
    return {"target": target, "plane_xy": plane_xy, "plane_xz": plane_xz, "plane_yz": plane_yz, "line_x": line_x, "line_y": line_y, "line_z": line_z}


ridge = 1.0

def solve_normal(gram, rhs):
    size = gram.shape[0]
    shape = rhs.shape
    chol = jnp.linalg.cholesky(gram + ridge * jnp.eye(size, dtype=jnp.float32))
    flat = rhs.reshape(size, -1)
    inner = lax.linalg.triangular_solve(chol, flat, left_side=True, lower=True, transpose_a=False)
    outer = lax.linalg.triangular_solve(chol, inner, left_side=True, lower=True, transpose_a=True)
    return outer.reshape(shape)

def with_old(gram, old):
    size = gram.shape[0]
    return jnp.dot(gram, old.reshape(size, -1), precision=lax.Precision.HIGHEST).reshape(old.shape)

def reference(target, plane_xy, plane_xz, plane_yz, line_x, line_y, line_z):
    fl = jnp.float32
    xy_full = plane_xy.astype(fl)
    xz_full = plane_xz.astype(fl)
    yz_full = plane_yz.astype(fl)
    lx_full = line_x.astype(fl)
    ly_full = line_y.astype(fl)
    lz_full = line_z.astype(fl)
    count = NX // CX

    def block(carry, index):
        yz_acc, z_acc, y_acc = carry
        start = index * CX
        target_rows = lax.dynamic_slice_in_dim(target, start, CX, 0).astype(fl)
        xy_rows = lax.dynamic_slice_in_dim(xy_full, start, CX, 1)
        xz_rows = lax.dynamic_slice_in_dim(xz_full, start, CX, 1)
        lx_rows = lax.dynamic_slice_in_dim(lx_full, start, CX, 1)
        model = jnp.einsum('rxy,rz->xyz', xy_rows, lz_full)
        model = model + jnp.einsum('rxz,ry->xyz', xz_rows, ly_full)
        model = model + jnp.einsum('rx,ryz->xyz', lx_rows, yz_full)
        rounded = lax.optimization_barrier((target_rows - model).astype(jnp.bfloat16))
        misfit = rounded.astype(fl)
        xy_term = jnp.einsum('xyz,rz->rxy', misfit, lz_full)
        xz_term = jnp.einsum('xyz,ry->rxz', misfit, ly_full)
        x_term = jnp.einsum('xyz,ryz->rx', misfit, yz_full)
        yz_acc = yz_acc + jnp.einsum('xyz,rx->ryz', misfit, lx_rows)
        z_acc = z_acc + jnp.einsum('xyz,rxy->rz', misfit, xy_rows)
        y_acc = y_acc + jnp.einsum('xyz,rxz->ry', misfit, xz_rows)
        return ((yz_acc, z_acc, y_acc), (xy_term, xz_term, x_term))
    start_carry = (jnp.zeros((R, NY, NZ), fl), jnp.zeros((R, NZ), fl), jnp.zeros((R, NY), fl))
    sums, stacked = lax.scan(block, start_carry, jnp.arange(count, dtype=jnp.int32))
    yz_side, z_side, y_side = sums
    xy_side = jnp.moveaxis(stacked[0], 0, 1).reshape(R, NX, NY)
    xz_side = jnp.moveaxis(stacked[1], 0, 1).reshape(R, NX, NZ)
    x_side = jnp.moveaxis(stacked[2], 0, 1).reshape(R, NX)
    gram_z = jnp.einsum('rz,sz->rs', lz_full, lz_full)
    gram_y = jnp.einsum('ry,sy->rs', ly_full, ly_full)
    gram_x = jnp.einsum('rx,sx->rs', lx_full, lx_full)
    gram_xy = jnp.einsum('rxy,sxy->rs', xy_full, xy_full)
    gram_xz = jnp.einsum('rxz,sxz->rs', xz_full, xz_full)
    gram_yz = jnp.einsum('ryz,syz->rs', yz_full, yz_full)
    bf = jnp.bfloat16
    new_xy = solve_normal(gram_z, xy_side + with_old(gram_z, xy_full)).astype(bf)
    new_xz = solve_normal(gram_y, xz_side + with_old(gram_y, xz_full)).astype(bf)
    new_yz = solve_normal(gram_x, yz_side + with_old(gram_x, yz_full)).astype(bf)
    new_x = solve_normal(gram_yz, x_side + with_old(gram_yz, lx_full)).astype(bf)
    new_y = solve_normal(gram_xz, y_side + with_old(gram_xz, ly_full)).astype(bf)
    new_z = solve_normal(gram_xy, z_side + with_old(gram_xy, lz_full)).astype(bf)
    return (new_xy, new_xz, new_yz, new_x, new_y, new_z)
```

```python
import functools

import jax
import jax.numpy as jnp
from jax import lax
from jax.experimental import pallas as pl
from jax.experimental.pallas import tpu as pltpu
from jax.sharding import Mesh, PartitionSpec as P

ridge = 1.0
f32 = jnp.float32
bf16 = jnp.bfloat16
sizes = {"y": 4, "x": 4, "zl": 2, "c": 2, "gz": 4}
HIGH = lax.Precision.HIGHEST
MB = 2**20


def hop(value, axis, shift):
    count = sizes[axis]
    return lax.ppermute(value, axis, [(i, (i + shift) % count) for i in range(count)])


def nn(left, right, **kw):
    return lax.dot_general(left, right, (((1,), (0,)), ((), ())), preferred_element_type=f32, **kw)


def nt(left, right, **kw):
    return lax.dot_general(left, right, (((1,), (1,)), ((), ())), preferred_element_type=f32, **kw)


def tn(left, right):
    return lax.dot_general(left, right, (((0,), (0,)), ((), ())), preferred_element_type=f32)


def iota(shape, axis):
    return lax.broadcasted_iota(jnp.int32, shape, axis)


def one_where(mask, kind=f32):
    return jnp.where(mask, 1.0, 0.0).astype(kind)


def call(kernel, name, scalars, grid, in_specs, out_specs, out_shape, scratch, args, flops, limit=50, moved=20 * MB):
    return pl.pallas_call(
        kernel,
        name=name,
        out_shape=out_shape,
        grid_spec=pltpu.PrefetchScalarGridSpec(
            num_scalar_prefetch=1, grid=grid, in_specs=in_specs, out_specs=out_specs, scratch_shapes=scratch
        ),
        compiler_params=pltpu.CompilerParams(vmem_limit_bytes=limit * MB),
        cost_estimate=pl.CostEstimate(flops=flops, bytes_accessed=moved, transcendentals=0),
    )(scalars, *args)


def whole(shape):
    return pl.BlockSpec(shape, lambda *_: (0,) * len(shape))


def inverse_kernel(s_ref, gram_ref, out_ref):
    shape = gram_ref.shape
    rows, cols = iota(shape, 1), iota(shape, 2)
    work = gram_ref[...] + ridge * one_where(rows == cols)
    for k in range(shape[1]):
        row, col = work[:, k : k + 1, :], work[:, :, k : k + 1]
        pivot = 1.0 / work[:, k : k + 1, k : k + 1]
        scaled = row * pivot
        work = jnp.where(cols == k, 0.0, work) - col * jnp.where(cols == k, pivot, scaled)
        work = jnp.where(rows == k, jnp.where(cols == k, pivot, scaled), work)
    out_ref[...] = work


def inverses(scalars, grams):
    shape = grams.shape
    return call(
        inverse_kernel, "inverse", scalars, (1,), [whole(shape)], whole(shape), jax.ShapeDtypeStruct(shape, f32), [], (grams,), 3000000, 16, MB
    )


def flat_row(matrix):
    spread = one_where(iota((32, 1024), 1) % 32 == iota((32, 1024), 0))
    wide = nn(matrix, spread, precision=HIGH)
    return jnp.sum(jnp.where(iota((32, 1024), 1) // 32 == iota((32, 1024), 0), wide, 0.0), axis=0, keepdims=True)


def small_kernel(s_ref, px_ref, pz_ref, own_ref, lx_ref, ly_ref, lz_ref, gz_ref, xy_ref, gy_ref):
    def step(x, carry):
        xy, xz = carry
        return xy + nt(px_ref[x], px_ref[x]), xz + nt(pz_ref[x], pz_ref[x])

    zero = jnp.zeros((32, 32), f32)
    gram_xy, gram_xz = lax.fori_loop(0, 64, step, (zero, zero), unroll=8)
    line_x, line_y, line_z = lx_ref[...], ly_ref[...], lz_ref[...]
    gram_yz = zero
    for y in range(4):
        gram_yz = gram_yz + nt(own_ref[y], own_ref[y])
        gz_ref[y : y + 1] = flat_row(nt(own_ref[y], line_z))
    gz_ref[4:5] = flat_row(gram_xz)
    gz_ref[5:6] = flat_row(gram_yz)
    gz_ref[6:7] = flat_row(nt(line_z, line_z))
    gz_ref[7:8] = jnp.zeros((1, 1024), f32)
    xy_ref[0:1] = flat_row(gram_xy)
    xy_ref[1:2] = flat_row(nt(line_x, line_x))
    xy_ref[2:8] = jnp.zeros((6, 1024), f32)
    gy_ref[...] = nt(line_y, line_y)


def rho_kernel(s_ref, t_ref, px_ref, pz_ref, ly_ref, lz_ref, rho_ref, ty_ref, xy0_ref, xy1_ref, xy2_ref, xy3_ref, yp_ref, zp_ref):
    k = pl.program_id(0)
    line_y, line_z = ly_ref[...], lz_ref[...]

    @pl.when(k == 0)
    def _():
        yp_ref[...] = jnp.zeros_like(yp_ref)
        zp_ref[...] = jnp.zeros_like(zp_ref)

    def step(x, _):
        over_y = jnp.concatenate([line_y, px_ref[x]], axis=0)
        over_z = jnp.concatenate([pz_ref[x], line_z], axis=0)
        rho = (t_ref[x].astype(f32) - tn(over_y, over_z)).astype(bf16)
        rho_ref[x] = rho
        from_z = nt(over_z, rho)
        from_y = nn(over_y, rho)
        ty_ref[x] = from_y[:32]
        zp_ref[...] += from_y[32:]
        yp_ref[...] += from_z[:32]
        xy0_ref[k, x] = from_z[32:]
        return 0

    lax.fori_loop(0, 16, step, 0, unroll=4)
    for which, ref in ((1, xy1_ref), (2, xy2_ref), (3, xy3_ref)):

        @pl.when(k == which)
        def _(ref=ref, which=which):
            ref[...] = xy0_ref[which].astype(bf16)


def yz_kernel(s_ref, lx_ref, rho_ref, keep_ref, send_ref, kron):
    @pl.when(pl.program_id(0) == 0)
    def _():
        spread = one_where(iota((64, 1024), 1) // 16 == iota((64, 1024), 0), bf16)
        wide = nn(lx_ref[...], spread)
        mask = iota((16, 1024), 1) % 16 == iota((16, 1024), 0)
        for r in range(32):
            kron[16 * r : 16 * r + 16] = jnp.where(mask, wide[r : r + 1], 0.0).astype(bf16)

    out = nn(kron[...], rho_ref[...].reshape(1024, 256)).astype(bf16)
    keep_ref[...] = out[:256].reshape(1, 1, 16, 16, 256)
    send_ref[...] = out[256:].reshape(1, 1, 16, 16, 256)


def spread_x(lines):
    count = lines.shape[0]
    wide = nn(lines, one_where(iota((32, 1024), 1) // 32 == iota((32, 1024), 0), bf16))
    mask = iota((32, 1024), 1) % 32 == iota((32, 1024), 0)
    return jnp.where(mask[None], wide[:, None, :], 0.0).astype(bf16).reshape(count * 32, 1024)


def apply_inverse(inverse, rows):
    tall = one_where(iota((256, 32), 0) % 32 == iota((256, 32), 1))
    wide = nt(nn(tall, inverse, precision=HIGH), tall, precision=HIGH)
    wide = jnp.where(iota((256, 256), 0) // 32 == iota((256, 256), 1) // 32, wide, 0.0)
    count = rows.shape[0] // 256
    return jnp.concatenate([nn(wide, rows[256 * i : 256 * i + 256], precision=HIGH) for i in range(count)], axis=0)


def row_of(s_ref, i, j):
    return pl.multiple_of((((s_ref[0] + 4 - j) % 4) * 4 + (s_ref[1] + 4 - i) % 4) * 16, 16)


def xy_kernel(s_ref, lx_ref, inv_ref, old_ref, own_ref, g1_ref, g2_ref, g3_ref, near_ref, far_ref, new_ref, w_all):
    for i in range(4):
        for j in range(4):
            rows = pl.ds(row_of(s_ref, i, j), 16)
            for half, ref in ((0, near_ref), (1, far_ref)):
                for part in range(2):
                    w_all[rows, 512 * half + 256 * part : 512 * half + 256 * part + 256] = ref[4 * i + j, part]
    total = own_ref[0] + g1_ref[...].astype(f32) + g2_ref[...].astype(f32) + g3_ref[...].astype(f32)
    total = total.reshape(512, 256) - nt(spread_x(lx_ref[...]), w_all[...])
    old = old_ref[...].astype(f32).reshape(512, 256)
    new = old + apply_inverse(inv_ref[...], total - old)
    new_ref[...] = new.astype(bf16).reshape(16, 32, 256)


def halves(value):
    high = value.astype(bf16)
    return high, (value - high.astype(f32)).astype(bf16)


def plane_kernel(
    s_ref, near_ref, far_ref, rho_ref, ty_ref, pz_ref, lx_ref, ly_ref, q_ref, b_ref, inv_ref, new_ref, xp_ref, yc_ref, zc_ref, plane, u_high, u_low
):
    @pl.when(pl.program_id(0) == 0)
    def _():
        for i in range(4):
            for j in range(4):
                rows = pl.ds(row_of(s_ref, i, j), 16)
                for r in range(16):
                    plane[r, rows] = near_ref[4 * i + j, r]
                    plane[16 + r, rows] = far_ref[4 * i + j, r]
        line_y = ly_ref[...]

        def step(s, carry):
            y_cross, z_cross = carry
            mine = plane[s]
            b_high, b_low = halves(b_ref[s])
            q_high, q_low = halves(q_ref[s])
            over_y = nn(jnp.concatenate([line_y, b_high, b_low], axis=0), mine)
            over_z = nt(jnp.concatenate([q_high, q_low], axis=0), mine)
            rows = pl.ds(pl.multiple_of(s * 32, 32), 32)
            u_high[rows], u_low[rows] = halves(over_y[:32])
            return y_cross + over_z[:32] + over_z[32:], z_cross + over_y[32:64] + over_y[64:]

        zero = jnp.zeros((32, 256), f32)
        yc_ref[...], zc_ref[...] = lax.fori_loop(0, 32, step, (zero, zero), unroll=2)

    kron = spread_x(lx_ref[...])
    total = ty_ref[...].reshape(512, 256) - nn(kron, u_high[...]) - nn(kron, u_low[...])
    old = pz_ref[...].astype(f32).reshape(512, 256)
    new_ref[...] = (old + apply_inverse(inv_ref[...], total - old)).astype(bf16).reshape(16, 32, 256)

    def block(j, total):
        rows = pl.ds(pl.multiple_of(16 * j, 16), 16)
        return total + nt(rho_ref[:, rows, :].reshape(256, 256), plane[:, rows, :].reshape(512, 256))

    total = lax.fori_loop(0, 16, block, jnp.zeros((256, 512), f32))
    total = jnp.where(iota((256, 512), 0) % 16 == iota((256, 512), 1) % 16, total, 0.0)
    over_x = nn(one_where(iota((16, 256), 1) // 16 == iota((16, 256), 0)), total, precision=HIGH)
    xp_ref[...] = nn(over_x, one_where(iota((512, 32), 0) // 16 == iota((512, 32), 1)), precision=HIGH)


def contract(form, left, right):
    return jnp.einsum(form, left, right, preferred_element_type=f32)


def exact(form, left, right):
    return jnp.einsum(form, left, right, precision=HIGH, preferred_element_type=f32)


def split(value, terms):
    parts = []
    for _ in range(terms):
        part = lax.reduce_precision(value, 8, 7)
        parts.append(part.astype(bf16))
        value = value - part
    return parts


def ordered(mine, other, second, axis):
    return jnp.concatenate([jnp.where(second, other, mine), jnp.where(second, mine, other)], axis=axis)


def all_sum(value, axis):
    total = value
    for shift in range(1, sizes[axis]):
        total = total + hop(value, axis, shift)
    return total


def update(inverse, part, old):
    old = old.astype(f32)
    shape = part.shape
    step = jnp.dot(inverse, (part - old).reshape(32, -1), precision=HIGH)
    return (old + step.reshape(shape)).astype(bf16)


def shards(target, plane_xy, plane_xz, plane_yz, line_x, line_y, line_z):
    at = {name: lax.axis_index(name) for name in sizes}
    scalars = jnp.stack([at["y"], at["x"], at["zl"], at["c"], at["gz"]]).astype(jnp.int32)
    px, pz = plane_xy.transpose(1, 0, 2), plane_xz.transpose(1, 0, 2)
    second_c, second_z = at["c"] == 1, at["zl"] == 1
    shape = jax.ShapeDtypeStruct

    half = lambda value, which: lax.dynamic_slice_in_dim(value, which * 16, 16, 0)
    block = ordered(half(plane_yz, at["c"]), hop(half(plane_yz, 1 - at["c"]), "c", 1), second_c, 1)
    block = ordered(block, hop(block, "zl", 1), second_z, 1)

    gz_sums, xy_sums, gram_y = call(
        small_kernel, "small", scalars, (1,),
        [whole((64, 32, 256))] * 2 + [whole((4, 32, 256)), whole((32, 64))] + [whole((32, 256))] * 2,
        [whole((8, 1024))] * 2 + [whole((32, 32))],
        [shape((8, 1024), f32)] * 2 + [shape((32, 32), f32)],
        [], (px, pz, plane_yz.transpose(1, 0, 2), line_x, line_y, line_z), 40000000, 30, 3 * MB,
    )
    gz_sums = all_sum(gz_sums, "gz")
    early = inverses(scalars, jnp.stack([gz_sums[6].reshape(32, 32), gram_y]))
    sums = jnp.concatenate([gz_sums[:6], xy_sums[:2]])
    got = hop(sums, "c", 1)
    sums = jnp.concatenate([ordered(sums[:4], got[:4], second_c, 0), sums[4:] + got[4:], jnp.zeros((4, 1024), f32)])
    got = hop(sums, "zl", 1)
    w_rows = ordered(sums[:8], got[:8], second_z, 0)
    grams = sums[8:12] + got[8:12]
    w_rows = lax.dynamic_slice_in_dim(w_rows, at["c"] * 512, 512, 1).astype(bf16)
    block = jnp.concatenate([block, jnp.stack([w_rows[:, :256], w_rows[:, 256:]])])

    def coded(value):
        tall = jnp.concatenate(split(value, 3) + [jnp.zeros((4, 1024), bf16)])
        return jnp.stack([tall[:, 256 * i : 256 * i + 256] for i in range(4)])

    def decoded(tiles):
        tall = jnp.concatenate([tiles[i] for i in range(4)], axis=1).astype(f32)
        return tall[:4] + (tall[4:8] + tall[8:12])

    for axis in ("y", "x"):
        rows = block.shape[0]
        message = jnp.concatenate([block, coded(grams)])
        got = [hop(message, axis, shift) for shift in range(1, 4)]
        for piece in got:
            grams = grams + decoded(piece[rows:])
        block = jnp.concatenate([block] + [piece[:rows] for piece in got])
    near = block.reshape(16, 18, 16, 256)
    far = hop(near, "c", 1)
    late = inverses(scalars, grams.reshape(4, 32, 32))

    by_quarter = lambda k, s: ((s[4] + k) % 4, 0, 0)
    lines = [whole((32, 256))] * 2
    rho, ty, xy0, xy1, xy2, xy3, y_part, z_part = call(
        rho_kernel, "rho", scalars, (4,),
        [pl.BlockSpec((16, 256, 256), by_quarter)] + [pl.BlockSpec((16, 32, 256), by_quarter)] * 2 + lines,
        [pl.BlockSpec((16, 256, 256), by_quarter), pl.BlockSpec((16, 32, 256), by_quarter), whole((4, 16, 32, 256))]
        + [whole((16, 32, 256))] * 3 + lines,
        [shape((64, 256, 256), bf16), shape((64, 32, 256), f32), shape((4, 16, 32, 256), f32)]
        + [shape((16, 32, 256), bf16)] * 3 + [shape((32, 256), f32)] * 2,
        [], (target, px, pz, line_y, line_z), 6000000000,
    )
    xy_got = [hop(send, "gz", shift) for shift, send in ((1, xy1), (2, xy2), (3, xy3))]

    back = jnp.roll(line_x, -16 * at["c"], axis=0)
    to_block = lambda j, s: ((j // 4 + 4 - s[0]) % 4, (j % 4 + 4 - s[1]) % 4, 0, 0, 0)
    keep, send = call(
        yz_kernel, "yz", scalars, (16,),
        [whole((32, 64)), pl.BlockSpec((64, 16, 256), lambda j, s: (0, j, 0))],
        [pl.BlockSpec((1, 1, 16, 16, 256), to_block)] * 2,
        [shape((4, 4, 16, 16, 256), bf16)] * 2,
        [pltpu.VMEM((512, 1024), bf16)], (back, rho), 5000000000,
    )
    got = hop(send, "c", 1)
    pieces = [keep[i].astype(f32) + got[i].astype(f32) for i in range(4)]
    total = pieces[0]
    for shift in range(1, 4):
        total = total + hop(pieces[shift].astype(bf16), "y", shift).astype(f32)
    pieces = [total[i] for i in range(4)]
    total = pieces[0]
    for shift in range(1, 4):
        total = total + hop(pieces[shift], "x", shift)
    region = lambda which: lax.dynamic_slice_in_dim(total, which * 8, 8, 1)
    total = region(at["zl"]) + hop(region(1 - at["zl"]), "zl", 1)
    region = lambda which: lax.dynamic_slice_in_dim(total, which * 4, 4, 1)
    yz_side = ordered(region(at["c"]), hop(region(1 - at["c"]), "c", 1), second_c, 0)

    back_t = back.T
    tiles = pl.BlockSpec((16, 2, 16, 256), lambda k, s: (0, 8, 0, 0))
    mine = call(
        xy_kernel, "xy", scalars, (1,),
        [pl.BlockSpec((16, 32), lambda k, s: (s[4], 0)), whole((32, 32)), pl.BlockSpec((16, 32, 256), lambda k, s: (s[4], 0, 0))]
        + [pl.BlockSpec((1, 16, 32, 256), lambda k, s: (0, 0, 0, 0))] + [whole((16, 32, 256))] * 3 + [tiles] * 2,
        whole((16, 32, 256)),
        shape((16, 32, 256), bf16),
        [pltpu.VMEM((256, 1024), bf16)], (back_t, early[0], px, xy0, *xy_got, near, far), 800000000, 50, 5 * MB,
    )
    quarters = [mine] + [hop(mine, "gz", shift) for shift in range(1, 4)]
    new_xy = jnp.zeros((32, 64, 256), bf16)
    for shift, piece in enumerate(quarters):
        new_xy = lax.dynamic_update_slice_in_dim(new_xy, piece.transpose(1, 0, 2), ((at["gz"] + 4 - shift) % 4) * 16, 1)

    q_part = contract("sx,xrz->srz", back, pz)
    b_part = contract("sx,xry->sry", back, px)
    blocks = lambda k, s: (k, 0, 0)
    new_xz, x_part, y_cross, z_cross = call(
        plane_kernel, "plane", scalars, (4,),
        [whole((16, 18, 16, 256))] * 2
        + [pl.BlockSpec((16, 256, 256), blocks)] + [pl.BlockSpec((16, 32, 256), blocks)] * 2
        + [pl.BlockSpec((16, 32), lambda k, s: (k, 0)), whole((32, 256))] + [whole((32, 32, 256))] * 2 + [whole((32, 32))],
        [pl.BlockSpec((16, 32, 256), blocks), pl.BlockSpec((16, 32), lambda k, s: (k, 0))] + lines,
        [shape((64, 32, 256), bf16), shape((64, 32), f32)] + [shape((32, 256), f32)] * 2,
        [pltpu.VMEM((32, 256, 256), bf16)] + [pltpu.VMEM((1024, 256), bf16)] * 2,
        (near, far, rho, ty, pz, back_t, line_y, q_part, b_part, early[1]), 9000000000, 56,
    )
    x_side = jnp.roll(x_part.T, 16 * at["c"], axis=0)
    both = all_sum(jnp.concatenate([y_part - y_cross, x_side], axis=1), "gz")
    x_side = both[:, 256:]
    both = jnp.concatenate([both[:, :256], z_part - z_cross])
    for axis in ("c", "zl", "y", "x"):
        both = all_sum(both, axis)
    y_side, z_side = both[:32], both[32:]

    gram_xz, gram_yz, gram_xy, gram_x = (grams[i].reshape(32, 32) for i in range(4))
    new_yz = update(late[3], yz_side - exact("rs,syz->ryz", gram_x, plane_yz.astype(f32)), plane_yz)
    new_x = update(late[1], x_side - exact("rs,sx->rx", gram_yz, line_x.astype(f32)), line_x)
    new_y = update(late[0], y_side, line_y)
    new_z = update(late[2], z_side, line_z)
    return (new_xy, new_xz.transpose(1, 0, 2), new_yz, new_x, new_y, new_z)


def solution(mesh):
    shape = tuple(sizes.values())
    mesh = Mesh(mesh.devices.reshape(shape), tuple(sizes))
    xy = ("y", "x", "zl", "c")
    outs = (
        P(None, xy, None),
        P(None, xy, "gz"),
        P(None, xy, "gz"),
        P(None, xy),
        P(),
        P(None, "gz"),
    )
    return jax.shard_map(
        shards,
        mesh=mesh,
        in_specs=(P(xy, None, "gz"),) + outs,
        out_specs=outs,
        check_vma=False,
    )
```

```python
import functools

import jax
import jax.numpy as jnp
from jax import lax
from jax.experimental import pallas as pl
from jax.experimental.pallas import tpu as pltpu
from jax.sharding import Mesh, PartitionSpec as P

ridge = 1.0
f32 = jnp.float32
bf16 = jnp.bfloat16
sizes = {"y": 4, "x": 4, "zl": 2, "c": 2, "gz": 4}
HIGH = lax.Precision.HIGHEST
MB = 2**20


def hop(value, axis, shift):
    count = sizes[axis]
    return lax.ppermute(value, axis, [(i, (i + shift) % count) for i in range(count)])


def pair_hop(value, flip):
    return lax.ppermute(value, ("zl", "c"), [(i, i ^ flip) for i in range(4)])


def nn(left, right, **kw):
    return lax.dot_general(left, right, (((1,), (0,)), ((), ())), preferred_element_type=f32, **kw)


def nt(left, right, **kw):
    return lax.dot_general(left, right, (((1,), (1,)), ((), ())), preferred_element_type=f32, **kw)


def tn(left, right):
    return lax.dot_general(left, right, (((0,), (0,)), ((), ())), preferred_element_type=f32)


def iota(shape, axis):
    return lax.broadcasted_iota(jnp.int32, shape, axis)


def one_where(mask, kind=f32):
    return jnp.where(mask, 1.0, 0.0).astype(kind)


def call(kernel, name, scalars, grid, in_specs, out_specs, out_shape, scratch, args, limit=50):
    return pl.pallas_call(
        kernel,
        name=name,
        out_shape=out_shape,
        grid_spec=pltpu.PrefetchScalarGridSpec(
            num_scalar_prefetch=1, grid=grid, in_specs=in_specs, out_specs=out_specs, scratch_shapes=scratch
        ),
        compiler_params=pltpu.CompilerParams(vmem_limit_bytes=limit * MB),
        cost_estimate=pl.CostEstimate(flops=1000, bytes_accessed=1000, transcendentals=0),
    )(scalars, *args)


def whole(shape):
    return pl.BlockSpec(shape, lambda *_: (0,) * len(shape))


def inverse_kernel(s_ref, gram_ref, out_ref):
    shape = gram_ref.shape
    rows, cols = iota(shape, 1), iota(shape, 2)
    work = gram_ref[...] + ridge * one_where(rows == cols)
    for k in range(shape[1]):
        row, col = work[:, k : k + 1, :], work[:, :, k : k + 1]
        pivot = 1.0 / work[:, k : k + 1, k : k + 1]
        scaled = row * pivot
        work = jnp.where(cols == k, 0.0, work) - col * jnp.where(cols == k, pivot, scaled)
        work = jnp.where(rows == k, jnp.where(cols == k, pivot, scaled), work)
    out_ref[...] = work


def inverses(scalars, grams):
    shape = grams.shape
    return call(
        inverse_kernel, "inverse", scalars, (1,), [whole(shape)], whole(shape), jax.ShapeDtypeStruct(shape, f32), [], (grams,), 16
    )


def small_kernel(s_ref, px_ref, pz_ref, own_ref, lx_ref, ly_ref, lz_ref, sums_ref, gz_ref, gy_ref):
    def step(x, carry):
        xy, xz = carry
        return xy + nt(px_ref[x], px_ref[x]), xz + nt(pz_ref[x], pz_ref[x])

    zero = jnp.zeros((32, 32), f32)
    gram_xy, gram_xz = lax.fori_loop(0, 64, step, (zero, zero), unroll=8)
    gram_yz = zero
    for y in range(4):
        gram_yz = gram_yz + nt(own_ref[y], own_ref[y])
    sums_ref[0] = gram_xz
    sums_ref[1] = gram_yz
    sums_ref[2] = gram_xy
    sums_ref[3] = nt(lx_ref[...], lx_ref[...])
    gz_ref[...] = nt(lz_ref[...], lz_ref[...])
    gy_ref[...] = nt(ly_ref[...], ly_ref[...])


def rho_kernel(s_ref, t_ref, px_ref, pz_ref, ly_ref, lz_ref, rho_ref, ty_ref, xy_ref, yp_ref, zp_ref):
    line_y, line_z = ly_ref[...], lz_ref[...]

    @pl.when(pl.program_id(0) == 0)
    def _():
        yp_ref[...] = jnp.zeros_like(yp_ref)
        zp_ref[...] = jnp.zeros_like(zp_ref)

    def step(x, _):
        over_y = jnp.concatenate([line_y, px_ref[x]], axis=0)
        over_z = jnp.concatenate([pz_ref[x], line_z], axis=0)
        rho = (t_ref[x].astype(f32) - tn(over_y, over_z)).astype(bf16)
        rho_ref[x] = rho
        from_z = nt(over_z, rho)
        from_y = nn(over_y, rho)
        ty_ref[x] = from_y[:32]
        zp_ref[...] += from_y[32:]
        yp_ref[...] += from_z[:32]
        xy_ref[x] = from_z[32:]
        return 0

    lax.fori_loop(0, 8, step, 0, unroll=8)


def yz_kernel(s_ref, lx_ref, low_ref, high_ref, keep_ref, send_ref, kron):
    @pl.when(pl.program_id(0) == 0)
    def _():
        spread = one_where(iota((64, 1024), 1) // 16 == iota((64, 1024), 0), bf16)
        wide = nn(lx_ref[...], spread)
        mask = iota((16, 1024), 1) % 16 == iota((16, 1024), 0)
        for r in range(32):
            kron[16 * r : 16 * r + 16] = jnp.where(mask, wide[r : r + 1], 0.0).astype(bf16)

    rows = jnp.concatenate([low_ref[...].reshape(512, 256), high_ref[...].reshape(512, 256)], axis=0)
    out = nn(kron[...], rows).astype(bf16)
    keep_ref[...] = out[:256].reshape(1, 1, 16, 16, 256)
    send_ref[...] = out[256:].reshape(1, 1, 16, 16, 256)


def spread_x(lines):
    count = lines.shape[0]
    wide = nn(lines, one_where(iota((32, 1024), 1) // 32 == iota((32, 1024), 0), bf16))
    mask = iota((32, 1024), 1) % 32 == iota((32, 1024), 0)
    return jnp.where(mask[None], wide[:, None, :], 0.0).astype(bf16).reshape(count * 32, 1024)


def apply_inverse(inverse, rows):
    tall = one_where(iota((256, 32), 0) % 32 == iota((256, 32), 1))
    wide = nt(nn(tall, inverse, precision=HIGH), tall, precision=HIGH)
    wide = jnp.where(iota((256, 256), 0) // 32 == iota((256, 256), 1) // 32, wide, 0.0)
    count = rows.shape[0] // 256
    return jnp.concatenate([nn(wide, rows[256 * i : 256 * i + 256], precision=HIGH) for i in range(count)], axis=0)


def row_of(s_ref, i, j):
    return pl.multiple_of((((s_ref[0] + 4 - j) % 4) * 4 + (s_ref[1] + 4 - i) % 4) * 16, 16)


def halves(value):
    high = value.astype(bf16)
    return high, (value - high.astype(f32)).astype(bf16)


def part_kernel(s_ref, near_ref, far_ref, part_ref, lx_ref, lz_ref, plane_ref, m0_ref, m1_ref, m2_ref, m3_ref, w_high, w_low):
    k = pl.program_id(0)

    @pl.when(k == 0)
    def _():
        for i in range(4):
            for j in range(4):
                rows = pl.ds(row_of(s_ref, i, j), 16)
                for r in range(16):
                    plane_ref[r, rows] = near_ref[4 * i + j, r]
                    plane_ref[16 + r, rows] = far_ref[4 * i + j, r]
        line_z = lz_ref[...]

        def step(s, _):
            rows = pl.ds(pl.multiple_of(s * 32, 32), 32)
            w_high[rows], w_low[rows] = halves(nt(line_z, plane_ref[s]))
            return 0

        lax.fori_loop(0, 32, step, 0, unroll=4)

    kron = spread_x(lx_ref[...])
    total = part_ref[...].reshape(512, 256) - nn(kron, w_high[...]) - nn(kron, w_low[...])
    for which, ref in enumerate((m0_ref, m1_ref, m2_ref, m3_ref)):

        @pl.when(k == which)
        def _(ref=ref):
            ref[...] = total.reshape(16, 32, 256).astype(ref.dtype)


def xy_kernel(s_ref, inv_ref, old_ref, own_ref, g1_ref, g2_ref, g3_ref, new_ref):
    total = own_ref[...] + g1_ref[...].astype(f32) + g2_ref[...].astype(f32) + g3_ref[...].astype(f32)
    old = old_ref[...].astype(f32).reshape(512, 256)
    new = old + apply_inverse(inv_ref[...], total.reshape(512, 256) - old)
    new_ref[...] = new.astype(bf16).reshape(16, 32, 256)


def side_kernel(s_ref, plane_ref, low_ref, high_ref, q_ref, b_ref, xp_ref, yc_ref, zc_ref):
    k = pl.program_id(0)

    @pl.when(k == 0)
    def _():
        def step(s, carry):
            y_cross, z_cross = carry
            over_y = nn(jnp.concatenate(halves(b_ref[s]), axis=0), plane_ref[s])
            over_z = nt(jnp.concatenate(halves(q_ref[s]), axis=0), plane_ref[s])
            return y_cross + over_z[:32] + over_z[32:], z_cross + over_y[:32] + over_y[32:]

        zero = jnp.zeros((32, 256), f32)
        yc_ref[...], zc_ref[...] = lax.fori_loop(0, 32, step, (zero, zero), unroll=4)

    def parts(rho_ref):
        total = jnp.zeros((256, 512), f32)
        for first in range(0, 16, 8):
            rows = [slice(16 * j, 16 * j + 16) for j in range(first, first + 8)]
            left = jnp.concatenate([rho_ref[:, r, :].reshape(256, 256) for r in rows], axis=1)
            right = jnp.concatenate([plane_ref[:, r, :].reshape(512, 256) for r in rows], axis=1)
            total = total + nt(left, right)
        total = jnp.where(iota((256, 512), 0) % 16 == iota((256, 512), 1) % 16, total, 0.0)
        over_x = nn(one_where(iota((16, 256), 1) // 16 == iota((16, 256), 0)), total, precision=HIGH)
        xp_ref[...] = nn(over_x, one_where(iota((512, 32), 0) // 16 == iota((512, 32), 1)), precision=HIGH)

    @pl.when(k < 2)
    def _():
        parts(low_ref)

    @pl.when(k >= 2)
    def _():
        parts(high_ref)


def xz_kernel(s_ref, plane_ref, ty_ref, pz_ref, lx_ref, ly_ref, inv_ref, new_ref, u_high, u_low):
    @pl.when(pl.program_id(0) == 0)
    def _():
        line_y = ly_ref[...]

        def step(s, _):
            rows = pl.ds(pl.multiple_of(s * 32, 32), 32)
            u_high[rows], u_low[rows] = halves(nn(line_y, plane_ref[s]))
            return 0

        lax.fori_loop(0, 32, step, 0, unroll=4)

    kron = spread_x(lx_ref[...])
    total = ty_ref[...].reshape(512, 256) - nn(kron, u_high[...]) - nn(kron, u_low[...])
    old = pz_ref[...].astype(f32).reshape(512, 256)
    new_ref[...] = (old + apply_inverse(inv_ref[...], total - old)).astype(bf16).reshape(16, 32, 256)


def contract(form, left, right):
    return jnp.einsum(form, left, right, preferred_element_type=f32)


def exact(form, left, right):
    return jnp.einsum(form, left, right, precision=HIGH, preferred_element_type=f32)


def ordered(mine, other, second, axis):
    return jnp.concatenate([jnp.where(second, other, mine), jnp.where(second, mine, other)], axis=axis)


def all_sum(value, axis):
    total = value
    for shift in range(1, sizes[axis]):
        total = total + hop(value, axis, shift)
    return total


def pair_sum(value):
    return value + pair_hop(value, 1) + pair_hop(value, 2) + pair_hop(value, 3)


def update(inverse, part, old):
    old = old.astype(f32)
    shape = part.shape
    step = jnp.dot(inverse, (part - old).reshape(32, -1), precision=HIGH)
    return (old + step.reshape(shape)).astype(bf16)


def phase(*values):
    return lax.optimization_barrier(values)


def shards(target, plane_xy, plane_xz, plane_yz, line_x, line_y, line_z):
    at = {name: lax.axis_index(name) for name in sizes}
    scalars = jnp.stack([at["y"], at["x"], at["zl"], at["c"], at["gz"]]).astype(jnp.int32)
    second_c, second_z = at["c"] == 1, at["zl"] == 1
    shape = jax.ShapeDtypeStruct
    lines = [whole((32, 256))] * 2

    half = lambda value, which: lax.dynamic_slice_in_dim(value, which * 16, 16, 0)
    own, other = half(plane_yz, at["c"]), half(plane_yz, 1 - at["c"])
    here = ordered(own, pair_hop(other, 1), second_c, 1)
    there = ordered(pair_hop(own, 2), pair_hop(other, 3), second_c, 1)
    block = ordered(here, there, second_z, 1)
    px, pz = plane_xy.transpose(1, 0, 2), plane_xz.transpose(1, 0, 2)
    block, px, pz, target = phase(block, px, pz, target)

    def local(target, px, pz, which):
        blocks = lambda k, s: (k + 4 * which, 0, 0)
        outs = lambda k, s: (k, 0, 0)
        return call(
            rho_kernel, "rho", scalars, (4,),
            [pl.BlockSpec((8, 256, 256), blocks)] + [pl.BlockSpec((8, 32, 256), blocks)] * 2 + lines,
            [pl.BlockSpec((8, 256, 256), outs)] + [pl.BlockSpec((8, 32, 256), outs)] * 2 + lines,
            [shape((32, 256, 256), bf16)] + [shape((32, 32, 256), f32)] * 2 + [shape((32, 256), f32)] * 2,
            [], (target, px, pz, line_y, line_z),
        )

    got = [hop(block, "y", shift) for shift in range(1, 4)]
    low = local(target, px, pz, 0)
    got, low, target, px, pz, block = phase(got, low, target, px, pz, block)
    block = jnp.stack([block] + got)
    block, target, px, pz, low = phase(block, target, px, pz, low)
    got = [hop(block, "x", shift) for shift in range(1, 4)]
    high = local(target, px, pz, 1)

    back = jnp.roll(line_x, -16 * at["c"], axis=0)
    to_block = lambda j, s: ((j // 4 + 4 - s[0]) % 4, (j % 4 + 4 - s[1]) % 4, 0, 0, 0)
    keep, send = call(
        yz_kernel, "yz", scalars, (16,),
        [whole((32, 64))] + [pl.BlockSpec((32, 16, 256), lambda j, s: (0, j, 0))] * 2,
        [pl.BlockSpec((1, 1, 16, 16, 256), to_block)] * 2,
        [shape((4, 4, 16, 16, 256), bf16)] * 2,
        [pltpu.VMEM((512, 1024), bf16)], (back, low[0], high[0]),
    )
    got, keep, send, px, pz, block, high = phase(got, keep, send, px, pz, block, high)
    near = jnp.stack([block] + got).reshape(16, 16, 16, 256)
    far, came = hop(near, "c", 1), hop(send, "c", 1)
    sums, gram_z, gram_y = call(
        small_kernel, "small", scalars, (1,),
        [whole((64, 32, 256))] * 2 + [whole((4, 32, 256)), whole((32, 64))] + [whole((32, 256))] * 2,
        [whole((4, 32, 32))] + [whole((32, 32))] * 2,
        [shape((4, 32, 32), f32)] + [shape((32, 32), f32)] * 2,
        [], (px, pz, plane_yz.transpose(1, 0, 2), line_x, line_y, line_z), 30,
    )
    q_part = contract("sx,xrz->srz", back, pz)
    b_part = contract("sx,xry->sry", back, px)
    far, came, sums, gram_z, gram_y, q_part, b_part, near, keep = phase(far, came, sums, gram_z, gram_y, q_part, b_part, near, keep)
    pieces = [keep[i].astype(f32) + came[i].astype(f32) for i in range(4)]
    pieces = [pieces[0]] + [piece.astype(bf16) for piece in pieces[1:]]
    pieces, near, far, gram_z = phase(pieces, near, far, gram_z)
    sent = [hop(pieces[shift], "y", shift) for shift in range(1, 4)]
    gram_z = all_sum(gram_z, "gz")

    back_t = back.T
    xy_part = jnp.concatenate([low[2], high[2]])
    turned = lambda k, s: ((s[4] + k) % 4, 0, 0)
    plane, mine, *parts = call(
        part_kernel, "part", scalars, (4,),
        [whole((16, 16, 16, 256))] * 2
        + [pl.BlockSpec((16, 32, 256), turned), pl.BlockSpec((16, 32), lambda k, s: ((s[4] + k) % 4, 0)), whole((32, 256))],
        [whole((32, 256, 256))] + [whole((16, 32, 256))] * 4,
        [shape((32, 256, 256), bf16), shape((16, 32, 256), f32)] + [shape((16, 32, 256), bf16)] * 3,
        [pltpu.VMEM((1024, 256), bf16)] * 2, (near, far, xy_part, back_t, line_z),
    )
    early = inverses(scalars, jnp.stack([gram_z, gram_y]))
    plane, mine, parts, early = phase(plane, mine, parts, early)
    parts = [hop(part, "gz", shift) for shift, part in enumerate(parts, 1)]
    x_part, y_cross, z_cross = call(
        side_kernel, "side", scalars, (4,),
        [whole((32, 256, 256))]
        + [pl.BlockSpec((16, 256, 256), lambda k, s: (jnp.minimum(k, 1), 0, 0)), pl.BlockSpec((16, 256, 256), lambda k, s: (jnp.maximum(k, 2) - 2, 0, 0))]
        + [whole((32, 32, 256))] * 2,
        [pl.BlockSpec((16, 32), lambda k, s: (k, 0))] + lines,
        [shape((64, 32), f32)] + [shape((32, 256), f32)] * 2,
        [], (plane, low[0], high[0], q_part, b_part), 56,
    )
    blocks = lambda k, s: (k, 0, 0)
    solve_xz = lambda plane: call(
        xz_kernel, "xz", scalars, (4,),
        [whole((32, 256, 256))] + [pl.BlockSpec((16, 32, 256), blocks)] * 2
        + [pl.BlockSpec((16, 32), lambda k, s: (k, 0)), whole((32, 256)), whole((32, 32))],
        pl.BlockSpec((16, 32, 256), blocks),
        shape((64, 32, 256), bf16),
        [pltpu.VMEM((1024, 256), bf16)] * 2, (plane, jnp.concatenate([low[1], high[1]]), pz, back_t, line_y, early[1]),
    )
    sent, x_part, y_cross, z_cross, plane, pieces = phase(sent, x_part, y_cross, z_cross, plane, pieces)
    total = pieces[0]
    for piece in sent:
        total = total + piece.astype(f32)
    x_side = jnp.roll(x_part.T, 16 * at["c"], axis=0)
    both = jnp.concatenate([low[3] + high[3] - y_cross, x_side, sums[0], sums[1]], axis=1)
    sent = [hop(total[shift], "x", shift) for shift in range(1, 4)]
    both = all_sum(both, "gz")
    new_xz = solve_xz(plane).transpose(1, 0, 2)
    parts, total, sent, both, new_xz = phase(parts, total[0], sent, both, new_xz)
    mine = call(
        xy_kernel, "xy", scalars, (1,),
        [whole((32, 32)), pl.BlockSpec((16, 32, 256), lambda k, s: (s[4], 0, 0))] + [whole((16, 32, 256))] * 4,
        whole((16, 32, 256)),
        shape((16, 32, 256), bf16),
        [], (early[0], px, mine, *parts),
    )
    total = total + sent[0] + sent[1] + sent[2]
    x_side = both[:, 256:320]
    both = jnp.concatenate([both[:, :256], low[4] + high[4] - z_cross, both[:, 320:], sums[2], sums[3]], axis=1)
    mine, total, both = phase(mine, total, both)
    quarters = [mine] + [hop(mine, "gz", shift) for shift in range(1, 4)]
    region = lambda which: lax.dynamic_slice_in_dim(total, which * 8, 8, 1)
    total = region(at["zl"]) + hop(region(1 - at["zl"]), "zl", 1)
    region = lambda which: lax.dynamic_slice_in_dim(total, which * 4, 4, 1)
    yz_side = ordered(region(at["c"]), hop(region(1 - at["c"]), "c", 1), second_c, 0)
    for axis in ("c", "zl", "y", "x"):
        both = all_sum(both, axis)
    late = inverses(scalars, jnp.stack([both[:, 512 + 32 * i : 544 + 32 * i] for i in range(4)]))
    new_xy = jnp.zeros((32, 64, 256), bf16)
    for shift, piece in enumerate(quarters):
        new_xy = lax.dynamic_update_slice_in_dim(new_xy, piece.transpose(1, 0, 2), ((at["gz"] + 4 - shift) % 4) * 16, 1)
    gram_yz, gram_x = both[:, 544:576], both[:, 608:640]
    new_yz = update(late[3], yz_side - exact("rs,syz->ryz", gram_x, plane_yz.astype(f32)), plane_yz)
    new_x = update(late[1], x_side - exact("rs,sx->rx", gram_yz, line_x.astype(f32)), line_x)
    new_y = update(late[0], both[:, :256], line_y)
    new_z = update(late[2], both[:, 256:512], line_z)
    return (new_xy, new_xz, new_yz, new_x, new_y, new_z)


def solution(mesh):
    shape = tuple(sizes.values())
    mesh = Mesh(mesh.devices.reshape(shape), tuple(sizes))
    xy = ("y", "x", "zl", "c")
    outs = (
        P(None, xy, None),
        P(None, xy, "gz"),
        P(None, xy, "gz"),
        P(None, xy),
        P(),
        P(None, "gz"),
    )
    return jax.shard_map(
        shards,
        mesh=mesh,
        in_specs=(P(xy, None, "gz"),) + outs,
        out_specs=outs,
        check_vma=False,
    )
```

```python
import functools

import jax
import jax.numpy as jnp
from jax import lax
from jax.experimental import pallas as pl
from jax.experimental.pallas import tpu as pltpu
from jax.sharding import Mesh, PartitionSpec as P

ridge = 1.0
f32 = jnp.float32
bf16 = jnp.bfloat16
sizes = {"y": 4, "x": 4, "zl": 2, "c": 2, "gz": 4}
HIGH = lax.Precision.HIGHEST
MB = 2**20


def hop(value, axis, shift):
    count = sizes[axis]
    return lax.ppermute(value, axis, [(i, (i + shift) % count) for i in range(count)])


def pair_hop(value, flip):
    return lax.ppermute(value, ("zl", "c"), [(i, i ^ flip) for i in range(4)])


def nn(left, right, **kw):
    return lax.dot_general(left, right, (((1,), (0,)), ((), ())), preferred_element_type=f32, **kw)


def nt(left, right, **kw):
    return lax.dot_general(left, right, (((1,), (1,)), ((), ())), preferred_element_type=f32, **kw)


def tn(left, right):
    return lax.dot_general(left, right, (((0,), (0,)), ((), ())), preferred_element_type=f32)


def iota(shape, axis):
    return lax.broadcasted_iota(jnp.int32, shape, axis)


def one_where(mask, kind=f32):
    return jnp.where(mask, 1.0, 0.0).astype(kind)


def call(kernel, name, scalars, grid, in_specs, out_specs, out_shape, scratch, args, limit=50, aliases=None):
    return pl.pallas_call(
        kernel,
        name=name,
        input_output_aliases=aliases or {},
        out_shape=out_shape,
        grid_spec=pltpu.PrefetchScalarGridSpec(
            num_scalar_prefetch=1, grid=grid, in_specs=in_specs, out_specs=out_specs, scratch_shapes=scratch
        ),
        compiler_params=pltpu.CompilerParams(vmem_limit_bytes=limit * MB),
        cost_estimate=pl.CostEstimate(flops=1000, bytes_accessed=1000, transcendentals=0),
    )(scalars, *args)


def whole(shape):
    return pl.BlockSpec(shape, lambda *_: (0,) * len(shape))


def invert(work):
    shape = work.shape
    rows, cols = iota(shape, 1), iota(shape, 2)
    work = work + ridge * one_where(rows == cols)
    for k in range(shape[1]):
        row, col = work[:, k : k + 1, :], work[:, :, k : k + 1]
        pivot = 1.0 / work[:, k : k + 1, k : k + 1]
        scaled = row * pivot
        work = jnp.where(cols == k, 0.0, work) - col * jnp.where(cols == k, pivot, scaled)
        work = jnp.where(rows == k, jnp.where(cols == k, pivot, scaled), work)
    return work


def inverse_kernel(s_ref, gram_ref, out_ref):
    out_ref[...] = invert(gram_ref[...])


def inverses(scalars, grams):
    shape = grams.shape
    return call(
        inverse_kernel, "inverse", scalars, (1,), [whole(shape)], whole(shape), jax.ShapeDtypeStruct(shape, f32), [], (grams,), 16
    )


def small_kernel(s_ref, px_ref, pz_ref, own_ref, lx_ref, ly_ref, sums_ref, inv_ref):
    def step(x, carry):
        xy, xz = carry
        return xy + nt(px_ref[x], px_ref[x]), xz + nt(pz_ref[x], pz_ref[x])

    zero = jnp.zeros((32, 32), f32)
    gram_xy, gram_xz = lax.fori_loop(0, 64, step, (zero, zero), unroll=8)
    gram_yz = zero
    for y in range(4):
        gram_yz = gram_yz + nt(own_ref[y], own_ref[y])
    sums_ref[0] = gram_xz
    sums_ref[1] = gram_yz
    sums_ref[2] = gram_xy
    sums_ref[3] = nt(lx_ref[...], lx_ref[...])
    inv_ref[...] = invert(nt(ly_ref[...], ly_ref[...])[None])[0]


def rho_kernel(s_ref, t_ref, px_ref, pz_ref, ly_ref, lz_ref, *refs):
    rho_ref, ty_ref, xy_ref, yp_ref, zp_ref = refs[-5:]
    line_y, line_z = ly_ref[...], lz_ref[...]

    @pl.when(pl.program_id(0) == 0)
    def _():
        yp_ref[...] = refs[3][...] if len(refs) > 5 else jnp.zeros_like(yp_ref)
        zp_ref[...] = refs[4][...] if len(refs) > 5 else jnp.zeros_like(zp_ref)

    def step(x, _):
        over_y = jnp.concatenate([line_y, px_ref[x]], axis=0)
        over_z = jnp.concatenate([pz_ref[x], line_z], axis=0)
        rho = (t_ref[x].astype(f32) - tn(over_y, over_z)).astype(bf16)
        rho_ref[x] = rho
        from_z = nt(over_z, rho)
        from_y = nn(over_y, rho)
        ty_ref[x] = from_y[:32]
        zp_ref[...] += from_y[32:]
        yp_ref[...] += from_z[:32]
        xy_ref[x] = from_z[32:]
        return 0

    lax.fori_loop(0, 8, step, 0, unroll=8)


def yz_kernel(s_ref, lx_ref, rho_ref, keep_ref, send_ref, kron):
    @pl.when(pl.program_id(0) == 0)
    def _():
        spread = one_where(iota((64, 1024), 1) // 16 == iota((64, 1024), 0), bf16)
        wide = nn(lx_ref[...], spread)
        mask = iota((16, 1024), 1) % 16 == iota((16, 1024), 0)
        for r in range(32):
            kron[16 * r : 16 * r + 16] = jnp.where(mask, wide[r : r + 1], 0.0).astype(bf16)

    out = nn(kron[...], rho_ref[...].reshape(1024, 256)).astype(bf16)
    keep_ref[...] = out[:256].reshape(1, 1, 16, 16, 256)
    send_ref[...] = out[256:].reshape(1, 1, 16, 16, 256)


def spread_x(lines):
    count = lines.shape[0]
    wide = nn(lines, one_where(iota((32, 1024), 1) // 32 == iota((32, 1024), 0), bf16))
    mask = iota((32, 1024), 1) % 32 == iota((32, 1024), 0)
    return jnp.where(mask[None], wide[:, None, :], 0.0).astype(bf16).reshape(count * 32, 1024)


def apply_inverse(inverse, rows):
    tall = one_where(iota((256, 32), 0) % 32 == iota((256, 32), 1))
    wide = nt(nn(tall, inverse, precision=HIGH), tall, precision=HIGH)
    wide = jnp.where(iota((256, 256), 0) // 32 == iota((256, 256), 1) // 32, wide, 0.0)
    count = rows.shape[0] // 256
    return jnp.concatenate([nn(wide, rows[256 * i : 256 * i + 256], precision=HIGH) for i in range(count)], axis=0)


def row_of(s_ref, i, j):
    return pl.multiple_of((((s_ref[0] + 4 - j) % 4) * 4 + (s_ref[1] + 4 - i) % 4) * 16, 16)


def halves(value):
    high = value.astype(bf16)
    return high, (value - high.astype(f32)).astype(bf16)


def part_kernel(s_ref, n0, n1, n2, n3, f0, f1, f2, f3, part_ref, lx_ref, lz_ref, plane_ref, m0_ref, m1_ref, m2_ref, m3_ref, w_high, w_low):
    k = pl.program_id(0)

    @pl.when(k == 0)
    def _():
        for i in range(4):
            for j in range(4):
                rows = pl.ds(row_of(s_ref, i, j), 16)
                for r in range(16):
                    plane_ref[r, rows] = (n0, n1, n2, n3)[i][j, r]
                    plane_ref[16 + r, rows] = (f0, f1, f2, f3)[i][j, r]
        line_z = lz_ref[...]
        gram = nt(line_z, line_z)
        high, low = halves(gram)
        middle, low = halves(gram - high.astype(f32))
        tile = jnp.concatenate([high.astype(f32), middle.astype(f32), low.astype(f32), jnp.zeros((32, 160), f32)], axis=1)
        for ref in (m1_ref, m2_ref, m3_ref):
            ref[16] = tile.astype(bf16)

        def step(s, _):
            rows = pl.ds(pl.multiple_of(s * 32, 32), 32)
            w_high[rows], w_low[rows] = halves(nt(line_z, plane_ref[s]))
            return 0

        lax.fori_loop(0, 32, step, 0, unroll=4)

    kron = spread_x(lx_ref[...])
    total = part_ref[...].reshape(512, 256) - nn(kron, w_high[...]) - nn(kron, w_low[...])
    for which, ref in enumerate((m0_ref, m1_ref, m2_ref, m3_ref)):

        @pl.when(k == which)
        def _(ref=ref):
            ref[:16] = total.reshape(16, 32, 256).astype(ref.dtype)


def xy_kernel(s_ref, lz_ref, old_ref, own_ref, g1_ref, g2_ref, g3_ref, new_ref):
    total, gram = own_ref[...], nt(lz_ref[...], lz_ref[...])
    for ref in (g1_ref, g2_ref, g3_ref):
        total = total + ref[:16].astype(f32)
        tile = ref[16].astype(f32)
        gram = gram + (tile[:, :32] + (tile[:, 32:64] + tile[:, 64:96]))
    inverse = invert(gram[None])[0]
    old = old_ref[...].astype(f32).reshape(512, 256)
    new = old + apply_inverse(inverse, total.reshape(512, 256) - old)
    new_ref[...] = new.astype(bf16).reshape(16, 32, 256)


def side_kernel(s_ref, plane_ref, rho_ref, q_ref, b_ref, xp_ref, yc_ref, zc_ref):
    k = pl.program_id(0)

    @pl.when(k == 0)
    def _():
        def step(s, carry):
            y_cross, z_cross = carry
            over_y = nn(jnp.concatenate(halves(b_ref[s]), axis=0), plane_ref[s])
            over_z = nt(jnp.concatenate(halves(q_ref[s]), axis=0), plane_ref[s])
            return y_cross + over_z[:32] + over_z[32:], z_cross + over_y[:32] + over_y[32:]

        zero = jnp.zeros((32, 256), f32)
        yc_ref[...], zc_ref[...] = lax.fori_loop(0, 32, step, (zero, zero), unroll=4)

    total = jnp.zeros((256, 512), f32)
    for first in range(0, 16, 8):
        rows = [slice(16 * j, 16 * j + 16) for j in range(first, first + 8)]
        left = jnp.concatenate([rho_ref[:, r, :].reshape(256, 256) for r in rows], axis=1)
        right = jnp.concatenate([plane_ref[:, r, :].reshape(512, 256) for r in rows], axis=1)
        total = total + nt(left, right)
    total = jnp.where(iota((256, 512), 0) % 16 == iota((256, 512), 1) % 16, total, 0.0)
    over_x = nn(one_where(iota((16, 256), 1) // 16 == iota((16, 256), 0)), total, precision=HIGH)
    xp_ref[...] = nn(over_x, one_where(iota((512, 32), 0) // 16 == iota((512, 32), 1)), precision=HIGH)


def xz_kernel(s_ref, plane_ref, ty_ref, pz_ref, lx_ref, ly_ref, inv_ref, new_ref, u_high, u_low):
    @pl.when(pl.program_id(0) == 0)
    def _():
        line_y = ly_ref[...]

        def step(s, _):
            rows = pl.ds(pl.multiple_of(s * 32, 32), 32)
            u_high[rows], u_low[rows] = halves(nn(line_y, plane_ref[s]))
            return 0

        lax.fori_loop(0, 32, step, 0, unroll=4)

    kron = spread_x(lx_ref[...])
    total = ty_ref[...].reshape(512, 256) - nn(kron, u_high[...]) - nn(kron, u_low[...])
    old = pz_ref[...].astype(f32).reshape(512, 256)
    new_ref[...] = (old + apply_inverse(inv_ref[...], total - old)).astype(bf16).reshape(16, 32, 256)


def contract(form, left, right):
    return jnp.einsum(form, left, right, preferred_element_type=f32)


def exact(form, left, right):
    return jnp.einsum(form, left, right, precision=HIGH, preferred_element_type=f32)


def ordered(mine, other, second, axis):
    return jnp.concatenate([jnp.where(second, other, mine), jnp.where(second, mine, other)], axis=axis)


def all_sum(value, axis):
    return (value + hop(value, axis, 2)) + (hop(value, axis, 1) + hop(value, axis, 3))


def fold(value, axis):
    count = sizes[axis]
    for bit in (1, 2)[: count // 2]:
        value = value + lax.ppermute(value, axis, [(i, i ^ bit) for i in range(count)])
    return value


def update(inverse, part, old):
    old = old.astype(f32)
    shape = part.shape
    step = jnp.dot(inverse, (part - old).reshape(32, -1), precision=HIGH)
    return (old + step.reshape(shape)).astype(bf16)


def phase(*values):
    return lax.optimization_barrier(values)


def shards(target, plane_xy, plane_xz, plane_yz, line_x, line_y, line_z):
    at = {name: lax.axis_index(name) for name in sizes}
    scalars = jnp.stack([at["y"], at["x"], at["zl"], at["c"], at["gz"]]).astype(jnp.int32)
    second_c, second_z = at["c"] == 1, at["zl"] == 1
    shape = jax.ShapeDtypeStruct
    lines = [whole((32, 256))] * 2

    half = lambda value, which: lax.dynamic_slice_in_dim(value, which * 16, 16, 0)
    own, other = half(plane_yz, at["c"]), half(plane_yz, 1 - at["c"])
    here = ordered(own, pair_hop(other, 1), second_c, 1)
    there = ordered(pair_hop(own, 2), pair_hop(other, 3), second_c, 1)
    block = ordered(here, there, second_z, 1)
    px, pz = plane_xy.transpose(1, 0, 2), plane_xz.transpose(1, 0, 2)
    block, px, pz, target = phase(block, px, pz, target)

    def local(target, px, pz, first, count, before):
        blocks = lambda k, s: (k + first, 0, 0)
        sizes = [(8, 256, 256), (8, 32, 256), (8, 32, 256)]
        return call(
            rho_kernel, "rho", scalars, (count,),
            [pl.BlockSpec(size, blocks) for size in sizes] + lines + ([pl.BlockSpec(memory_space=pl.ANY)] * 3 + lines if before else []),
            [pl.BlockSpec(size, blocks) for size in sizes] + lines,
            [shape((64, 256, 256), bf16)] + [shape((64, 32, 256), f32)] * 2 + [shape((32, 256), f32)] * 2,
            [], (target, px, pz, line_y, line_z, *before), 16, {6: 0, 7: 1, 8: 2} if before else None,
        )

    got = [hop(block, "y", shift) for shift in range(1, 4)]
    first = local(target, px, pz, 0, 2, [])
    got, first, target, px, pz, block = phase(got, first, target, px, pz, block)
    block = jnp.stack([block] + got)
    block, target, px, pz, first = phase(block, target, px, pz, first)
    got = [hop(block, "x", shift) for shift in range(1, 4)]
    far = [hop(block, "c", 1)]
    rho, ty, xy_part, y_part, z_part = local(target, px, pz, 2, 6, list(first))

    back = jnp.roll(line_x, -16 * at["c"], axis=0)
    to_block = lambda j, s: ((j // 4 + 4 - s[0]) % 4, (j % 4) ^ s[1], 0, 0, 0)
    keep, send = call(
        yz_kernel, "yz", scalars, (16,),
        [whole((32, 64)), pl.BlockSpec((64, 16, 256), lambda j, s: (0, j, 0))],
        [pl.BlockSpec((1, 1, 16, 16, 256), to_block)] * 2,
        [shape((4, 4, 16, 16, 256), bf16)] * 2,
        [pltpu.VMEM((512, 1024), bf16)], (back, rho), 16,
    )
    got, far, keep, send, px, pz, block = phase(got, far, keep, send, px, pz, block)
    near = [block] + got
    came, far = hop(send, "c", 1), far + [hop(piece, "c", 1) for piece in got]
    q_part = contract("sx,xrz->srz", back, pz)
    b_part = contract("sx,xry->sry", back, px)
    far, came, q_part, b_part, near, keep = phase(far, came, q_part, b_part, near, keep)
    pieces = [keep[i].astype(f32) + came[i].astype(f32) for i in range(4)]
    sent = [pieces[2][:2].astype(bf16), pieces[2][2:].astype(bf16)]
    pieces = [pieces[0], pieces[1], pieces[3]]
    sent, pieces, near, far = phase(sent, pieces, near, far)
    sent = [hop(sent[0], "y", 1), hop(sent[1], "y", 3)]

    back_t = back.T
    turned = lambda k, s: ((s[4] + k) % 4, 0, 0)
    plane, mine, *parts = call(
        part_kernel, "part", scalars, (4,),
        [whole((4, 16, 16, 256))] * 8
        + [pl.BlockSpec((16, 32, 256), turned), pl.BlockSpec((16, 32), lambda k, s: ((s[4] + k) % 4, 0)), whole((32, 256))],
        [whole((32, 256, 256)), whole((16, 32, 256))] + [whole((17, 32, 256))] * 3,
        [shape((32, 256, 256), bf16), shape((16, 32, 256), f32)] + [shape((17, 32, 256), bf16)] * 3,
        [pltpu.VMEM((1024, 256), bf16)] * 2, (*near, *far, xy_part, back_t, line_z), 40,
    )
    plane, mine, parts, q_part, b_part, sent, pieces = phase(plane, mine, parts, q_part, b_part, sent, pieces)
    ahead = (pieces[1] + jnp.concatenate([sent[0].astype(f32), jnp.zeros((2, 16, 16, 256), f32)])).astype(bf16)
    behind = (pieces[2] + jnp.concatenate([jnp.zeros((2, 16, 16, 256), f32), sent[1].astype(f32)])).astype(bf16)
    total = pieces[0]
    plane, mine, parts, q_part, b_part, ahead, behind, total = phase(plane, mine, parts, q_part, b_part, ahead, behind, total)
    sent = [hop(ahead, "y", 1), hop(behind, "y", 3)]
    parts = [hop(part, "gz", shift) for shift, part in enumerate(parts, 1)]
    blocks = lambda k, s: (k, 0, 0)
    x_part, y_cross, z_cross = call(
        side_kernel, "side", scalars, (4,),
        [whole((32, 256, 256)), pl.BlockSpec((16, 256, 256), blocks)] + [whole((32, 32, 256))] * 2,
        [pl.BlockSpec((16, 32), lambda k, s: (k, 0))] + lines,
        [shape((64, 32), f32)] + [shape((32, 256), f32)] * 2,
        [], (plane, rho, q_part, b_part), 44,
    )
    sums, inv_y = call(
        small_kernel, "small", scalars, (1,),
        [whole((64, 32, 256))] * 2 + [whole((4, 32, 256)), whole((32, 64)), whole((32, 256))],
        [whole((4, 32, 32)), whole((32, 32))],
        [shape((4, 32, 32), f32), shape((32, 32), f32)],
        [], (px, pz, plane_yz.transpose(1, 0, 2), line_x, line_y), 20,
    )
    parts, sent, x_part, y_cross, z_cross, plane, sums, inv_y, total = phase(parts, sent, x_part, y_cross, z_cross, plane, sums, inv_y, total)

    x_side = jnp.roll(x_part.T, 16 * at["c"], axis=0)
    both = jnp.concatenate([y_part - y_cross, x_side, sums[0], sums[1]], axis=1)
    both = all_sum(both, "gz")
    mine = call(
        xy_kernel, "xy", scalars, (1,),
        [whole((32, 256)), pl.BlockSpec((16, 32, 256), lambda k, s: (s[4], 0, 0)), whole((16, 32, 256))] + [whole((17, 32, 256))] * 3,
        whole((16, 32, 256)),
        shape((16, 32, 256), bf16),
        [], (line_z, px, mine, *parts), 24,
    )
    total = total + sent[0].astype(f32) + sent[1].astype(f32)
    mine, both, plane, total = phase(mine, both, plane, total)
    x_side = both[:, 256:320]
    both = jnp.concatenate([both[:, :256], z_part - z_cross, both[:, 320:], sums[2], sums[3]], axis=1)

    quarters = [mine] + [hop(mine, "gz", shift) for shift in range(1, 4)]
    for axis in ("y", "x", "c", "zl"):
        both = fold(both, axis)
    sent = lax.ppermute(total[2:], "x", [(i, i ^ 2) for i in range(4)])
    new_xz = call(
        xz_kernel, "xz", scalars, (4,),
        [whole((32, 256, 256))] + [pl.BlockSpec((16, 32, 256), blocks)] * 2
        + [pl.BlockSpec((16, 32), lambda k, s: (k, 0)), whole((32, 256)), whole((32, 32))],
        pl.BlockSpec((16, 32, 256), blocks),
        shape((64, 32, 256), bf16),
        [pltpu.VMEM((1024, 256), bf16)] * 2, (plane, ty, pz, back_t, line_y, inv_y), 30,
    )
    total = total[:2] + sent
    total = total[0] + lax.ppermute(total[1], "x", [(i, i ^ 1) for i in range(4)])
    region = lambda which: lax.dynamic_slice_in_dim(total, which * 8, 8, 1)
    total = region(at["zl"]) + hop(region(1 - at["zl"]), "zl", 1)
    region = lambda which: lax.dynamic_slice_in_dim(total, which * 4, 4, 1)
    yz_side = ordered(region(at["c"]), hop(region(1 - at["c"]), "c", 1), second_c, 0)
    late = inverses(scalars, jnp.stack([both[:, 512 + 32 * i : 544 + 32 * i] for i in range(4)]))
    new_xy = jnp.zeros((32, 64, 256), bf16)
    for shift, piece in enumerate(quarters):
        new_xy = lax.dynamic_update_slice_in_dim(new_xy, piece.transpose(1, 0, 2), ((at["gz"] + 4 - shift) % 4) * 16, 1)
    gram_yz, gram_x = both[:, 544:576], both[:, 608:640]
    new_yz = update(late[3], yz_side - exact("rs,syz->ryz", gram_x, plane_yz.astype(f32)), plane_yz)
    new_x = update(late[1], x_side - exact("rs,sx->rx", gram_yz, line_x.astype(f32)), line_x)
    new_y = update(late[0], both[:, :256], line_y)
    new_z = update(late[2], both[:, 256:512], line_z)
    return (new_xy, new_xz.transpose(1, 0, 2), new_yz, new_x, new_y, new_z)


def solution(mesh):
    shape = tuple(sizes.values())
    mesh = Mesh(mesh.devices.reshape(shape), tuple(sizes))
    xy = ("y", "x", "zl", "c")
    outs = (
        P(None, xy, None),
        P(None, xy, "gz"),
        P(None, xy, "gz"),
        P(None, xy),
        P(),
        P(None, "gz"),
    )
    return jax.shard_map(
        shards,
        mesh=mesh,
        in_specs=(P(xy, None, "gz"),) + outs,
        out_specs=outs,
        check_vma=False,
    )
```

```python
import functools

import jax
import jax.numpy as jnp
from jax import lax
from jax.experimental import pallas as pl
from jax.experimental.pallas import tpu as pltpu
from jax.sharding import Mesh, PartitionSpec as P

ridge = 1.0
f32 = jnp.float32
bf16 = jnp.bfloat16
sizes = {"y": 4, "x": 4, "zl": 2, "c": 2, "gz": 4}
HIGH = lax.Precision.HIGHEST
MB = 2**20


def hop(value, axis, shift):
    count = sizes[axis]
    return lax.ppermute(value, axis, [(i, (i + shift) % count) for i in range(count)])


def pair_hop(value, flip):
    return lax.ppermute(value, ("zl", "c"), [(i, i ^ flip) for i in range(4)])


def nn(left, right, **kw):
    return lax.dot_general(left, right, (((1,), (0,)), ((), ())), preferred_element_type=f32, **kw)


def nt(left, right, **kw):
    return lax.dot_general(left, right, (((1,), (1,)), ((), ())), preferred_element_type=f32, **kw)


def tn(left, right):
    return lax.dot_general(left, right, (((0,), (0,)), ((), ())), preferred_element_type=f32)


def iota(shape, axis):
    return lax.broadcasted_iota(jnp.int32, shape, axis)


def one_where(mask, kind=f32):
    return jnp.where(mask, 1.0, 0.0).astype(kind)


def call(kernel, name, scalars, grid, in_specs, out_specs, out_shape, scratch, args, limit=50, aliases=None):
    return pl.pallas_call(
        kernel,
        name=name,
        input_output_aliases=aliases or {},
        out_shape=out_shape,
        grid_spec=pltpu.PrefetchScalarGridSpec(
            num_scalar_prefetch=1, grid=grid, in_specs=in_specs, out_specs=out_specs, scratch_shapes=scratch
        ),
        compiler_params=pltpu.CompilerParams(vmem_limit_bytes=limit * MB),
        cost_estimate=pl.CostEstimate(flops=1000, bytes_accessed=1000, transcendentals=0),
    )(scalars, *args)


def whole(shape):
    return pl.BlockSpec(shape, lambda *_: (0,) * len(shape))


def invert(work):
    shape = work.shape
    rows, cols = iota(shape, 1), iota(shape, 2)
    work = work + ridge * one_where(rows == cols)
    for k in range(shape[1]):
        row, col = work[:, k : k + 1, :], work[:, :, k : k + 1]
        pivot = 1.0 / work[:, k : k + 1, k : k + 1]
        scaled = row * pivot
        work = jnp.where(cols == k, 0.0, work) - col * jnp.where(cols == k, pivot, scaled)
        work = jnp.where(rows == k, jnp.where(cols == k, pivot, scaled), work)
    return work


def inverse_kernel(s_ref, gram_ref, out_ref):
    out_ref[...] = invert(gram_ref[...])


def inverses(scalars, grams):
    shape = grams.shape
    return call(
        inverse_kernel, "inverse", scalars, (1,), [whole(shape)], whole(shape), jax.ShapeDtypeStruct(shape, f32), [], (grams,), 16
    )


def small_kernel(s_ref, px_ref, pz_ref, own_ref, lx_ref, ly_ref, sums_ref, inv_ref):
    def step(x, carry):
        xy, xz = carry
        return xy + nt(px_ref[x], px_ref[x]), xz + nt(pz_ref[x], pz_ref[x])

    zero = jnp.zeros((32, 32), f32)
    gram_xy, gram_xz = lax.fori_loop(0, 64, step, (zero, zero), unroll=8)
    gram_yz = zero
    for y in range(4):
        gram_yz = gram_yz + nt(own_ref[y], own_ref[y])
    sums_ref[0] = gram_xz
    sums_ref[1] = gram_yz
    sums_ref[2] = gram_xy
    sums_ref[3] = nt(lx_ref[...], lx_ref[...])
    inv_ref[...] = invert(nt(ly_ref[...], ly_ref[...])[None])[0]


def rho_kernel(s_ref, t_ref, px_ref, pz_ref, ly_ref, lz_ref, rho_ref, ty_ref, xy_ref, yp_ref, zp_ref):
    line_y, line_z = ly_ref[...], lz_ref[...]

    @pl.when(pl.program_id(0) == 0)
    def _():
        yp_ref[...] = jnp.zeros_like(yp_ref)
        zp_ref[...] = jnp.zeros_like(zp_ref)

    def step(x, _):
        over_y = jnp.concatenate([line_y, px_ref[x]], axis=0)
        over_z = jnp.concatenate([pz_ref[x], line_z], axis=0)
        rho = (t_ref[x].astype(f32) - tn(over_y, over_z)).astype(bf16)
        rho_ref[x] = rho
        from_z = nt(over_z, rho)
        from_y = nn(over_y, rho)
        ty_ref[x] = from_y[:32]
        zp_ref[...] += from_y[32:]
        yp_ref[...] += from_z[:32]
        xy_ref[x] = from_z[32:]
        return 0

    lax.fori_loop(0, 8, step, 0, unroll=8)


def yz_kernel(s_ref, lx_ref, low_ref, high_ref, keep_ref, send_ref, kron):
    @pl.when(pl.program_id(0) == 0)
    def _():
        spread = one_where(iota((64, 1024), 1) // 16 == iota((64, 1024), 0), bf16)
        wide = nn(lx_ref[...], spread)
        mask = iota((16, 1024), 1) % 16 == iota((16, 1024), 0)
        for r in range(32):
            kron[16 * r : 16 * r + 16] = jnp.where(mask, wide[r : r + 1], 0.0).astype(bf16)

    rows = jnp.concatenate([low_ref[...].reshape(256, 256), high_ref[...].reshape(768, 256)], axis=0)
    out = nn(kron[...], rows).astype(bf16)
    keep_ref[...] = out[:256].reshape(1, 1, 16, 16, 256)
    send_ref[...] = out[256:].reshape(1, 1, 16, 16, 256)


def spread_x(lines):
    count = lines.shape[0]
    wide = nn(lines, one_where(iota((32, 1024), 1) // 32 == iota((32, 1024), 0), bf16))
    mask = iota((32, 1024), 1) % 32 == iota((32, 1024), 0)
    return jnp.where(mask[None], wide[:, None, :], 0.0).astype(bf16).reshape(count * 32, 1024)


def apply_inverse(inverse, rows):
    tall = one_where(iota((256, 32), 0) % 32 == iota((256, 32), 1))
    wide = nt(nn(tall, inverse, precision=HIGH), tall, precision=HIGH)
    wide = jnp.where(iota((256, 256), 0) // 32 == iota((256, 256), 1) // 32, wide, 0.0)
    count = rows.shape[0] // 256
    return jnp.concatenate([nn(wide, rows[256 * i : 256 * i + 256], precision=HIGH) for i in range(count)], axis=0)


def row_of(s_ref, i, j):
    return pl.multiple_of((((s_ref[0] + 4 - j) % 4) * 4 + (s_ref[1] + 4 - i) % 4) * 16, 16)


def halves(value):
    high = value.astype(bf16)
    return high, (value - high.astype(f32)).astype(bf16)


def part_kernel(s_ref, n0, n1, n2, n3, f0, f1, f2, f3, low_ref, high_ref, lx_ref, lz_ref, plane_ref, m0_ref, m1_ref, m2_ref, m3_ref, w_high, w_low):
    k = pl.program_id(0)

    @pl.when(k == 0)
    def _():
        for i in range(4):
            for j in range(4):
                rows = pl.ds(row_of(s_ref, i, j), 16)
                for r in range(16):
                    plane_ref[r, rows] = (n0, n1, n2, n3)[i][j, r]
                    plane_ref[16 + r, rows] = (f0, f1, f2, f3)[i][j, r]
        line_z = lz_ref[...]
        gram = nt(line_z, line_z)
        high, low = halves(gram)
        middle, low = halves(gram - high.astype(f32))
        tile = jnp.concatenate([high.astype(f32), middle.astype(f32), low.astype(f32), jnp.zeros((32, 160), f32)], axis=1)
        for ref in (m1_ref, m2_ref, m3_ref):
            ref[16] = tile.astype(bf16)

        def step(s, _):
            rows = pl.ds(pl.multiple_of(s * 32, 32), 32)
            w_high[rows], w_low[rows] = halves(nt(line_z, plane_ref[s]))
            return 0

        lax.fori_loop(0, 32, step, 0, unroll=4)

    kron = spread_x(lx_ref[...])
    part = jnp.where((s_ref[4] + k) % 4 == 0, low_ref[...], high_ref[...])
    total = part.reshape(512, 256) - nn(kron, w_high[...]) - nn(kron, w_low[...])
    for which, ref in enumerate((m0_ref, m1_ref, m2_ref, m3_ref)):

        @pl.when(k == which)
        def _(ref=ref):
            ref[:16] = total.reshape(16, 32, 256).astype(ref.dtype)


def xy_kernel(s_ref, lz_ref, old_ref, own_ref, g1_ref, g2_ref, g3_ref, new_ref):
    total, gram = own_ref[...], nt(lz_ref[...], lz_ref[...])
    for ref in (g1_ref, g2_ref, g3_ref):
        total = total + ref[:16].astype(f32)
        tile = ref[16].astype(f32)
        gram = gram + (tile[:, :32] + (tile[:, 32:64] + tile[:, 64:96]))
    inverse = invert(gram[None])[0]
    old = old_ref[...].astype(f32).reshape(512, 256)
    new = old + apply_inverse(inverse, total.reshape(512, 256) - old)
    new_ref[...] = new.astype(bf16).reshape(16, 32, 256)


def side_kernel(s_ref, plane_ref, low_ref, high_ref, q_ref, b_ref, xp_ref, yc_ref, zc_ref):
    k = pl.program_id(0)

    @pl.when(k == 0)
    def _():
        def step(s, carry):
            y_cross, z_cross = carry
            over_y = nn(jnp.concatenate(halves(b_ref[s]), axis=0), plane_ref[s])
            over_z = nt(jnp.concatenate(halves(q_ref[s]), axis=0), plane_ref[s])
            return y_cross + over_z[:32] + over_z[32:], z_cross + over_y[:32] + over_y[32:]

        zero = jnp.zeros((32, 256), f32)
        yc_ref[...], zc_ref[...] = lax.fori_loop(0, 32, step, (zero, zero), unroll=4)

    def parts(rho_ref):
        total = jnp.zeros((256, 512), f32)
        for first in range(0, 16, 8):
            rows = [slice(16 * j, 16 * j + 16) for j in range(first, first + 8)]
            left = jnp.concatenate([rho_ref[:, r, :].reshape(256, 256) for r in rows], axis=1)
            right = jnp.concatenate([plane_ref[:, r, :].reshape(512, 256) for r in rows], axis=1)
            total = total + nt(left, right)
        total = jnp.where(iota((256, 512), 0) % 16 == iota((256, 512), 1) % 16, total, 0.0)
        over_x = nn(one_where(iota((16, 256), 1) // 16 == iota((16, 256), 0)), total, precision=HIGH)
        xp_ref[...] = nn(over_x, one_where(iota((512, 32), 0) // 16 == iota((512, 32), 1)), precision=HIGH)

    @pl.when(k == 0)
    def _():
        parts(low_ref)

    @pl.when(k > 0)
    def _():
        parts(high_ref)


def xz_kernel(s_ref, plane_ref, low_ref, high_ref, pz_ref, lx_ref, ly_ref, inv_ref, new_ref, u_high, u_low):
    @pl.when(pl.program_id(0) == 0)
    def _():
        line_y = ly_ref[...]

        def step(s, _):
            rows = pl.ds(pl.multiple_of(s * 32, 32), 32)
            u_high[rows], u_low[rows] = halves(nn(line_y, plane_ref[s]))
            return 0

        lax.fori_loop(0, 32, step, 0, unroll=4)

    kron = spread_x(lx_ref[...])
    part = jnp.where(pl.program_id(0) == 0, low_ref[...], high_ref[...])
    total = part.reshape(512, 256) - nn(kron, u_high[...]) - nn(kron, u_low[...])
    old = pz_ref[...].astype(f32).reshape(512, 256)
    new_ref[...] = (old + apply_inverse(inv_ref[...], total - old)).astype(bf16).reshape(16, 32, 256)


def contract(form, left, right):
    return jnp.einsum(form, left, right, preferred_element_type=f32)


def exact(form, left, right):
    return jnp.einsum(form, left, right, precision=HIGH, preferred_element_type=f32)


def ordered(mine, other, second, axis):
    return jnp.concatenate([jnp.where(second, other, mine), jnp.where(second, mine, other)], axis=axis)


def all_sum(value, axis):
    return (value + hop(value, axis, 2)) + (hop(value, axis, 1) + hop(value, axis, 3))


def fold(value, axis):
    count = sizes[axis]
    for bit in (1, 2)[: count // 2]:
        value = value + lax.ppermute(value, axis, [(i, i ^ bit) for i in range(count)])
    return value


def update(inverse, part, old):
    old = old.astype(f32)
    shape = part.shape
    step = jnp.dot(inverse, (part - old).reshape(32, -1), precision=HIGH)
    return (old + step.reshape(shape)).astype(bf16)


def phase(*values):
    return lax.optimization_barrier(values)


def shards(target, plane_xy, plane_xz, plane_yz, line_x, line_y, line_z):
    at = {name: lax.axis_index(name) for name in sizes}
    scalars = jnp.stack([at["y"], at["x"], at["zl"], at["c"], at["gz"]]).astype(jnp.int32)
    second_c, second_z = at["c"] == 1, at["zl"] == 1
    shape = jax.ShapeDtypeStruct
    lines = [whole((32, 256))] * 2

    half = lambda value, which: lax.dynamic_slice_in_dim(value, which * 16, 16, 0)
    own, other = half(plane_yz, at["c"]), half(plane_yz, 1 - at["c"])
    here = ordered(own, pair_hop(other, 1), second_c, 1)
    there = ordered(pair_hop(own, 2), pair_hop(other, 3), second_c, 1)
    block = ordered(here, there, second_z, 1)
    px, pz = plane_xy.transpose(1, 0, 2), plane_xz.transpose(1, 0, 2)
    block, scalars = phase(block, scalars)

    def local(scalars, first, count):
        blocks = lambda k, s: (k + first, 0, 0)
        outs = lambda k, s: (k, 0, 0)
        sizes = [(8, 256, 256), (8, 32, 256), (8, 32, 256)]
        return call(
            rho_kernel, "rho", scalars, (count,),
            [pl.BlockSpec(size, blocks) for size in sizes] + lines,
            [pl.BlockSpec(size, outs) for size in sizes] + lines,
            [shape((8 * count, 256, 256), bf16)] + [shape((8 * count, 32, 256), f32)] * 2 + [shape((32, 256), f32)] * 2,
            [], (target, px, pz, line_y, line_z), 16,
        )

    got = [hop(block, "y", shift) for shift in range(1, 4)]
    low = local(scalars, 0, 2)
    got, y_part, scalars = phase(got, low[3], scalars)
    block = jnp.stack([block] + got)
    block, scalars = phase(block, scalars)
    got = [hop(block, "x", shift) for shift in range(1, 4)]
    far = [hop(block, "c", 1)]
    high = local(scalars, 2, 6)
    y_part, z_part = y_part + high[3], low[4] + high[4]

    back = jnp.roll(line_x, -16 * at["c"], axis=0)
    to_block = lambda j, s: ((j // 4 + 4 - s[0]) % 4, (j % 4) ^ s[1], 0, 0, 0)
    keep, send = call(
        yz_kernel, "yz", scalars, (16,),
        [whole((32, 64))] + [pl.BlockSpec((count, 16, 256), lambda j, s: (0, j, 0)) for count in (16, 48)],
        [pl.BlockSpec((1, 1, 16, 16, 256), to_block)] * 2,
        [shape((4, 4, 16, 16, 256), bf16)] * 2,
        [pltpu.VMEM((512, 1024), bf16)], (back, low[0], high[0]), 16,
    )
    got, far, send, scalars = phase(got, far, send, scalars)
    near = [block] + got
    came, far = hop(send, "c", 1), far + [hop(piece, "c", 1) for piece in got]
    q_part = contract("sx,xrz->srz", back, pz)
    b_part = contract("sx,xry->sry", back, px)
    far, came, q_part, b_part, scalars = phase(far, came, q_part, b_part, scalars)
    pieces = [keep[i].astype(f32) + came[i].astype(f32) for i in range(4)]
    sent = [pieces[2][:2].astype(bf16), pieces[2][2:].astype(bf16)]
    sent, scalars = phase(sent, scalars)
    sent = [hop(sent[0], "y", 1), hop(sent[1], "y", 3)]

    back_t = back.T
    turned = lambda k, s: (jnp.maximum((s[4] + k) % 4, 1) - 1, 0, 0)
    plane, mine, *parts = call(
        part_kernel, "part", scalars, (4,),
        [whole((4, 16, 16, 256))] * 8
        + [whole((16, 32, 256)), pl.BlockSpec((16, 32, 256), turned), pl.BlockSpec((16, 32), lambda k, s: ((s[4] + k) % 4, 0)), whole((32, 256))],
        [whole((32, 256, 256)), whole((16, 32, 256))] + [whole((17, 32, 256))] * 3,
        [shape((32, 256, 256), bf16), shape((16, 32, 256), f32)] + [shape((17, 32, 256), bf16)] * 3,
        [pltpu.VMEM((1024, 256), bf16)] * 2, (*near, *far, low[2], high[2], back_t, line_z), 40,
    )
    parts, sent, scalars = phase(parts, sent, scalars)
    ahead = (pieces[1] + jnp.concatenate([sent[0].astype(f32), jnp.zeros((2, 16, 16, 256), f32)])).astype(bf16)
    behind = (pieces[3] + jnp.concatenate([jnp.zeros((2, 16, 16, 256), f32), sent[1].astype(f32)])).astype(bf16)
    ahead, behind, scalars = phase(ahead, behind, scalars)
    sent = [hop(ahead, "y", 1), hop(behind, "y", 3)]
    parts = [hop(part, "gz", shift) for shift, part in enumerate(parts, 1)]
    blocks = lambda k, s: (k, 0, 0)
    later = lambda k, s: (jnp.maximum(k, 1) - 1, 0, 0)
    x_part, y_cross, z_cross = call(
        side_kernel, "side", scalars, (4,),
        [whole((32, 256, 256)), whole((16, 256, 256)), pl.BlockSpec((16, 256, 256), later)] + [whole((32, 32, 256))] * 2,
        [pl.BlockSpec((16, 32), lambda k, s: (k, 0))] + lines,
        [shape((64, 32), f32)] + [shape((32, 256), f32)] * 2,
        [], (plane, low[0], high[0], q_part, b_part), 44,
    )
    sums, inv_y = call(
        small_kernel, "small", scalars, (1,),
        [whole((64, 32, 256))] * 2 + [whole((4, 32, 256)), whole((32, 64)), whole((32, 256))],
        [whole((4, 32, 32)), whole((32, 32))],
        [shape((4, 32, 32), f32), shape((32, 32), f32)],
        [], (px, pz, plane_yz.transpose(1, 0, 2), line_x, line_y), 20,
    )
    parts, sent, x_part, y_cross, z_cross, sums, inv_y, scalars = phase(parts, sent, x_part, y_cross, z_cross, sums, inv_y, scalars)
    total = pieces[0] + sent[0].astype(f32) + sent[1].astype(f32)
    total, scalars = phase(total, scalars)
    yz_sum = total[:2] + lax.ppermute(total[2:], "x", [(i, i ^ 2) for i in range(4)])

    x_side = jnp.roll(x_part.T, 16 * at["c"], axis=0)
    both = jnp.concatenate([y_part - y_cross, x_side, sums[0], sums[1]], axis=1)
    both = all_sum(both, "gz")
    mine = call(
        xy_kernel, "xy", scalars, (1,),
        [whole((32, 256)), pl.BlockSpec((16, 32, 256), lambda k, s: (s[4], 0, 0)), whole((16, 32, 256))] + [whole((17, 32, 256))] * 3,
        whole((16, 32, 256)),
        shape((16, 32, 256), bf16),
        [], (line_z, px, mine, *parts), 24,
    )
    mine, both, yz_sum, scalars = phase(mine, both, yz_sum, scalars)
    x_side = both[:, 256:320]
    both = jnp.concatenate([both[:, :256], z_part - z_cross, both[:, 320:], sums[2], sums[3]], axis=1)

    quarters = [mine] + [hop(mine, "gz", shift) for shift in range(1, 4)]
    both = fold(both, "y")
    total = yz_sum[0] + lax.ppermute(yz_sum[1], "x", [(i, i ^ 1) for i in range(4)])
    both, total = phase(both, total)
    both = fold(both, "x")
    region = lambda which: lax.dynamic_slice_in_dim(total, which * 8, 8, 1)
    total = region(at["zl"]) + hop(region(1 - at["zl"]), "zl", 1)
    both, total = phase(both, total)
    both = fold(fold(both, "c"), "zl")
    region = lambda which: lax.dynamic_slice_in_dim(total, which * 4, 4, 1)
    yz_side = ordered(region(at["c"]), hop(region(1 - at["c"]), "c", 1), second_c, 0)
    new_xz = call(
        xz_kernel, "xz", scalars, (4,),
        [whole((32, 256, 256)), whole((16, 32, 256)), pl.BlockSpec((16, 32, 256), later), pl.BlockSpec((16, 32, 256), blocks)]
        + [pl.BlockSpec((16, 32), lambda k, s: (k, 0)), whole((32, 256)), whole((32, 32))],
        pl.BlockSpec((16, 32, 256), blocks),
        shape((64, 32, 256), bf16),
        [pltpu.VMEM((1024, 256), bf16)] * 2, (plane, low[1], high[1], pz, back_t, line_y, inv_y), 30,
    )
    late = inverses(scalars, jnp.stack([both[:, 512 + 32 * i : 544 + 32 * i] for i in range(4)]))
    new_xy = jnp.zeros((32, 64, 256), bf16)
    for shift, piece in enumerate(quarters):
        new_xy = lax.dynamic_update_slice_in_dim(new_xy, piece.transpose(1, 0, 2), ((at["gz"] + 4 - shift) % 4) * 16, 1)
    gram_yz, gram_x = both[:, 544:576], both[:, 608:640]
    new_yz = update(late[3], yz_side - exact("rs,syz->ryz", gram_x, plane_yz.astype(f32)), plane_yz)
    new_x = update(late[1], x_side - exact("rs,sx->rx", gram_yz, line_x.astype(f32)), line_x)
    new_y = update(late[0], both[:, :256], line_y)
    new_z = update(late[2], both[:, 256:512], line_z)
    return (new_xy, new_xz.transpose(1, 0, 2), new_yz, new_x, new_y, new_z)


def solution(mesh):
    shape = tuple(sizes.values())
    mesh = Mesh(mesh.devices.reshape(shape), tuple(sizes))
    xy = ("y", "x", "zl", "c")
    outs = (
        P(None, xy, None),
        P(None, xy, "gz"),
        P(None, xy, "gz"),
        P(None, xy),
        P(),
        P(None, "gz"),
    )
    return jax.shard_map(
        shards,
        mesh=mesh,
        in_specs=(P(xy, None, "gz"),) + outs,
        out_specs=outs,
        check_vma=False,
    )
```

```python
import functools

import jax
import jax.numpy as jnp
from jax import lax
from jax.experimental import pallas as pl
from jax.experimental.pallas import tpu as pltpu
from jax.sharding import Mesh, PartitionSpec as P

ridge = 1.0
f32 = jnp.float32
bf16 = jnp.bfloat16
sizes = {"y": 4, "x": 4, "zl": 2, "c": 2, "gz": 4}
HIGH = lax.Precision.HIGHEST
MB = 2**20


def hop(value, axis, shift):
    count = sizes[axis]
    return lax.ppermute(value, axis, [(i, (i + shift) % count) for i in range(count)])


def pair_hop(value, flip):
    return lax.ppermute(value, ("zl", "c"), [(i, i ^ flip) for i in range(4)])


def nn(left, right, **kw):
    return lax.dot_general(left, right, (((1,), (0,)), ((), ())), preferred_element_type=f32, **kw)


def nt(left, right, **kw):
    return lax.dot_general(left, right, (((1,), (1,)), ((), ())), preferred_element_type=f32, **kw)


def tn(left, right):
    return lax.dot_general(left, right, (((0,), (0,)), ((), ())), preferred_element_type=f32)


def iota(shape, axis):
    return lax.broadcasted_iota(jnp.int32, shape, axis)


def one_where(mask, kind=f32):
    return jnp.where(mask, 1.0, 0.0).astype(kind)


def call(kernel, name, scalars, grid, in_specs, out_specs, out_shape, scratch, args, limit=50, aliases=None):
    return pl.pallas_call(
        kernel,
        name=name,
        input_output_aliases=aliases or {},
        out_shape=out_shape,
        grid_spec=pltpu.PrefetchScalarGridSpec(
            num_scalar_prefetch=1, grid=grid, in_specs=in_specs, out_specs=out_specs, scratch_shapes=scratch
        ),
        compiler_params=pltpu.CompilerParams(vmem_limit_bytes=limit * MB),
        cost_estimate=pl.CostEstimate(flops=1000, bytes_accessed=1000, transcendentals=0),
    )(scalars, *args)


def whole(shape):
    return pl.BlockSpec(shape, lambda *_: (0,) * len(shape))


def invert(work):
    shape = work.shape
    rows, cols = iota(shape, 1), iota(shape, 2)
    work = work + ridge * one_where(rows == cols)
    for k in range(shape[1]):
        row, col = work[:, k : k + 1, :], work[:, :, k : k + 1]
        pivot = 1.0 / work[:, k : k + 1, k : k + 1]
        scaled = row * pivot
        work = jnp.where(cols == k, 0.0, work) - col * jnp.where(cols == k, pivot, scaled)
        work = jnp.where(rows == k, jnp.where(cols == k, pivot, scaled), work)
    return work


def inverse_kernel(s_ref, gram_ref, out_ref):
    out_ref[...] = invert(gram_ref[...])


def inverses(scalars, grams):
    shape = grams.shape
    return call(
        inverse_kernel, "inverse", scalars, (1,), [whole(shape)], whole(shape), jax.ShapeDtypeStruct(shape, f32), [], (grams,), 16
    )


def small_kernel(s_ref, px_ref, pz_ref, own_ref, lx_ref, sums_ref):
    def step(x, carry):
        xy, xz = carry
        return xy + nt(px_ref[x], px_ref[x]), xz + nt(pz_ref[x], pz_ref[x])

    zero = jnp.zeros((32, 32), f32)
    gram_xy, gram_xz = lax.fori_loop(0, 64, step, (zero, zero), unroll=8)
    gram_yz = zero
    for y in range(4):
        gram_yz = gram_yz + nt(own_ref[y], own_ref[y])
    sums_ref[0] = gram_xz
    sums_ref[1] = gram_yz
    sums_ref[2] = gram_xy
    sums_ref[3] = nt(lx_ref[...], lx_ref[...])


def rho_kernel(s_ref, t_ref, px_ref, pz_ref, ly_ref, lz_ref, rho_ref, ty_ref, xy_ref, yp_ref, zp_ref):
    line_y, line_z = ly_ref[...], lz_ref[...]

    @pl.when(pl.program_id(0) == 0)
    def _():
        yp_ref[...] = jnp.zeros_like(yp_ref)
        zp_ref[...] = jnp.zeros_like(zp_ref)

    def step(x, _):
        over_y = jnp.concatenate([line_y, px_ref[x]], axis=0)
        over_z = jnp.concatenate([pz_ref[x], line_z], axis=0)
        rho = (t_ref[x].astype(f32) - tn(over_y, over_z)).astype(bf16)
        rho_ref[x] = rho
        from_z = nt(over_z, rho)
        from_y = nn(over_y, rho)
        ty_ref[x] = from_y[:32]
        zp_ref[...] += from_y[32:]
        yp_ref[...] += from_z[:32]
        xy_ref[x] = from_z[32:]
        return 0

    lax.fori_loop(0, 8, step, 0, unroll=8)


def yz_kernel(s_ref, lx_ref, rho_ref, keep_ref, send_ref, kron):
    @pl.when(pl.program_id(0) == 0)
    def _():
        spread = one_where(iota((64, 1024), 1) // 16 == iota((64, 1024), 0), bf16)
        wide = nn(lx_ref[...], spread)
        mask = iota((16, 1024), 1) % 16 == iota((16, 1024), 0)
        for r in range(32):
            kron[16 * r : 16 * r + 16] = jnp.where(mask, wide[r : r + 1], 0.0).astype(bf16)

    out = nn(kron[...], rho_ref[...].reshape(1024, 256)).astype(bf16)
    keep_ref[...] = out[:256].reshape(1, 1, 16, 16, 256)
    send_ref[...] = out[256:].reshape(1, 1, 16, 16, 256)


def spread_x(lines):
    count = lines.shape[0]
    wide = nn(lines, one_where(iota((32, 1024), 1) // 32 == iota((32, 1024), 0), bf16))
    mask = iota((32, 1024), 1) % 32 == iota((32, 1024), 0)
    return jnp.where(mask[None], wide[:, None, :], 0.0).astype(bf16).reshape(count * 32, 1024)


def apply_inverse(inverse, rows):
    tall = one_where(iota((256, 32), 0) % 32 == iota((256, 32), 1))
    wide = nt(nn(tall, inverse, precision=HIGH), tall, precision=HIGH)
    wide = jnp.where(iota((256, 256), 0) // 32 == iota((256, 256), 1) // 32, wide, 0.0)
    count = rows.shape[0] // 256
    return jnp.concatenate([nn(wide, rows[256 * i : 256 * i + 256], precision=HIGH) for i in range(count)], axis=0)


def row_of(s_ref, i, j):
    return pl.multiple_of((((s_ref[0] + 4 - j) % 4) * 4 + (s_ref[1] + 4 - i) % 4) * 16, 16)


def halves(value):
    high = value.astype(bf16)
    return high, (value - high.astype(f32)).astype(bf16)


def part_kernel(s_ref, n0, n1, n2, n3, f0, f1, f2, f3, part_ref, lx_ref, lz_ref, plane_ref, m0_ref, m1_ref, m2_ref, m3_ref, w_high, w_low):
    k = pl.program_id(0)

    @pl.when(k == 0)
    def _():
        for i in range(4):
            for j in range(4):
                rows = pl.ds(row_of(s_ref, i, j), 16)
                for r in range(16):
                    plane_ref[r, rows] = (n0, n1, n2, n3)[i][j, r]
                    plane_ref[16 + r, rows] = (f0, f1, f2, f3)[i][j, r]
        line_z = lz_ref[...]
        gram = nt(line_z, line_z)
        high, low = halves(gram)
        middle, low = halves(gram - high.astype(f32))
        tile = jnp.concatenate([high.astype(f32), middle.astype(f32), low.astype(f32), jnp.zeros((32, 160), f32)], axis=1)
        for ref in (m1_ref, m2_ref, m3_ref):
            ref[16] = tile.astype(bf16)

        def step(s, _):
            rows = pl.ds(pl.multiple_of(s * 32, 32), 32)
            w_high[rows], w_low[rows] = halves(nt(line_z, plane_ref[s]))
            return 0

        lax.fori_loop(0, 32, step, 0, unroll=4)

    kron = spread_x(lx_ref[...])
    total = part_ref[...].reshape(512, 256) - nn(kron, w_high[...]) - nn(kron, w_low[...])
    for which, ref in enumerate((m0_ref, m1_ref, m2_ref, m3_ref)):

        @pl.when(k == which)
        def _(ref=ref):
            ref[:16] = total.reshape(16, 32, 256).astype(ref.dtype)


def xy_kernel(s_ref, ly_ref, lz_ref, old_ref, own_ref, g1_ref, g2_ref, g3_ref, new_ref, inv_ref):
    total, gram = own_ref[...], nt(lz_ref[...], lz_ref[...])
    for ref in (g1_ref, g2_ref, g3_ref):
        total = total + ref[:16].astype(f32)
        tile = ref[16].astype(f32)
        gram = gram + (tile[:, :32] + (tile[:, 32:64] + tile[:, 64:96]))
    both = invert(jnp.stack([gram, nt(ly_ref[...], ly_ref[...])]))
    inverse = both[0]
    inv_ref[...] = both[1]
    old = old_ref[...].astype(f32).reshape(512, 256)
    new = old + apply_inverse(inverse, total.reshape(512, 256) - old)
    new_ref[...] = new.astype(bf16).reshape(16, 32, 256)


def side_kernel(s_ref, plane_ref, rho_ref, q_ref, b_ref, xp_ref, yc_ref, zc_ref):
    k = pl.program_id(0)

    @pl.when(k == 0)
    def _():
        def step(s, carry):
            y_cross, z_cross = carry
            over_y = nn(jnp.concatenate(halves(b_ref[s]), axis=0), plane_ref[s])
            over_z = nt(jnp.concatenate(halves(q_ref[s]), axis=0), plane_ref[s])
            return y_cross + over_z[:32] + over_z[32:], z_cross + over_y[:32] + over_y[32:]

        zero = jnp.zeros((32, 256), f32)
        yc_ref[...], zc_ref[...] = lax.fori_loop(0, 32, step, (zero, zero), unroll=4)

    total = jnp.zeros((256, 512), f32)
    for first in range(0, 16, 8):
        rows = [slice(16 * j, 16 * j + 16) for j in range(first, first + 8)]
        left = jnp.concatenate([rho_ref[:, r, :].reshape(256, 256) for r in rows], axis=1)
        right = jnp.concatenate([plane_ref[:, r, :].reshape(512, 256) for r in rows], axis=1)
        total = total + nt(left, right)
    total = jnp.where(iota((256, 512), 0) % 16 == iota((256, 512), 1) % 16, total, 0.0)
    over_x = nn(one_where(iota((16, 256), 1) // 16 == iota((16, 256), 0)), total, precision=HIGH)
    xp_ref[...] = nn(over_x, one_where(iota((512, 32), 0) // 16 == iota((512, 32), 1)), precision=HIGH)


def xz_kernel(s_ref, plane_ref, ty_ref, pz_ref, lx_ref, ly_ref, inv_ref, new_ref, u_high, u_low):
    @pl.when(pl.program_id(0) == 0)
    def _():
        line_y = ly_ref[...]

        def step(s, _):
            rows = pl.ds(pl.multiple_of(s * 32, 32), 32)
            u_high[rows], u_low[rows] = halves(nn(line_y, plane_ref[s]))
            return 0

        lax.fori_loop(0, 32, step, 0, unroll=4)

    kron = spread_x(lx_ref[...])
    total = ty_ref[...].reshape(512, 256) - nn(kron, u_high[...]) - nn(kron, u_low[...])
    old = pz_ref[...].astype(f32).reshape(512, 256)
    new_ref[...] = (old + apply_inverse(inv_ref[...], total - old)).astype(bf16).reshape(16, 32, 256)


def contract(form, left, right):
    return jnp.einsum(form, left, right, preferred_element_type=f32)


def exact(form, left, right):
    return jnp.einsum(form, left, right, precision=HIGH, preferred_element_type=f32)


def ordered(mine, other, second, axis):
    return jnp.concatenate([jnp.where(second, other, mine), jnp.where(second, mine, other)], axis=axis)


def all_sum(value, axis):
    return (value + hop(value, axis, 2)) + (hop(value, axis, 1) + hop(value, axis, 3))


def fold(value, axis):
    count = sizes[axis]
    for bit in (1, 2)[: count // 2]:
        value = value + lax.ppermute(value, axis, [(i, i ^ bit) for i in range(count)])
    return value


def update(inverse, part, old):
    old = old.astype(f32)
    shape = part.shape
    step = jnp.dot(inverse, (part - old).reshape(32, -1), precision=HIGH)
    return (old + step.reshape(shape)).astype(bf16)


def phase(*values):
    return lax.optimization_barrier(values)


def shards(target, plane_xy, plane_xz, plane_yz, line_x, line_y, line_z):
    at = {name: lax.axis_index(name) for name in sizes}
    scalars = jnp.stack([at["y"], at["x"], at["zl"], at["c"], at["gz"]]).astype(jnp.int32)
    second_c, second_z = at["c"] == 1, at["zl"] == 1
    shape = jax.ShapeDtypeStruct
    lines = [whole((32, 256))] * 2

    half = lambda value, which: lax.dynamic_slice_in_dim(value, which * 16, 16, 0)
    own, other = half(plane_yz, at["c"]), half(plane_yz, 1 - at["c"])
    here = ordered(own, pair_hop(other, 1), second_c, 1)
    there = ordered(pair_hop(own, 2), pair_hop(other, 3), second_c, 1)
    block = ordered(here, there, second_z, 1)
    block, scalars = phase(block, scalars)

    got = [hop(block, "y", shift) for shift in range(1, 4)]
    px, pz = plane_xy.transpose(1, 0, 2), plane_xz.transpose(1, 0, 2)
    block = jnp.stack([block] + got)
    block, scalars = phase(block, scalars)
    got = [hop(block, "x", shift) for shift in range(1, 4)]
    far = [hop(block, "c", 1)]
    blocks = lambda k, s: (k, 0, 0)
    tiles = [pl.BlockSpec(size, blocks) for size in ((8, 256, 256), (8, 32, 256), (8, 32, 256))]
    rho, ty, xy_part, y_part, z_part = call(
        rho_kernel, "rho", scalars, (8,), tiles + lines, tiles + lines,
        [shape((64, 256, 256), bf16)] + [shape((64, 32, 256), f32)] * 2 + [shape((32, 256), f32)] * 2,
        [], (target, px, pz, line_y, line_z), 16,
    )

    back = jnp.roll(line_x, -16 * at["c"], axis=0)
    to_block = lambda j, s: ((j // 4 + 4 - s[0]) % 4, (j % 4) ^ s[1], 0, 0, 0)
    keep, send = call(
        yz_kernel, "yz", scalars, (16,),
        [whole((32, 64)), pl.BlockSpec((64, 16, 256), lambda j, s: (0, j, 0))],
        [pl.BlockSpec((1, 1, 16, 16, 256), to_block)] * 2,
        [shape((4, 4, 16, 16, 256), bf16)] * 2,
        [pltpu.VMEM((512, 1024), bf16)], (back, rho), 16,
    )
    got, far, send, scalars = phase(got, far, send, scalars)
    near = [block] + got
    came, far = hop(send, "c", 1), far + [hop(piece, "c", 1) for piece in got]
    q_part = contract("sx,xrz->srz", back, pz)
    b_part = contract("sx,xry->sry", back, px)
    far, came, q_part, b_part, scalars = phase(far, came, q_part, b_part, scalars)
    pieces = [keep[i].astype(f32) + came[i].astype(f32) for i in range(4)]
    sent = [pieces[2][:2].astype(bf16), pieces[2][2:].astype(bf16)]
    sent, scalars = phase(sent, scalars)
    sent = [hop(sent[0], "y", 1), hop(sent[1], "y", 3)]

    back_t = back.T
    resident = pl.BlockSpec(memory_space=pltpu.VMEM)
    turned = lambda k, s: ((s[4] + k) % 4, 0, 0)
    plane, mine, *parts = call(
        part_kernel, "part", scalars, (4,),
        [whole((4, 16, 16, 256))] * 8
        + [pl.BlockSpec((16, 32, 256), turned), pl.BlockSpec((16, 32), lambda k, s: ((s[4] + k) % 4, 0)), whole((32, 256))],
        [resident, whole((16, 32, 256))] + [whole((17, 32, 256))] * 3,
        [shape((32, 256, 256), bf16), shape((16, 32, 256), f32)] + [shape((17, 32, 256), bf16)] * 3,
        [pltpu.VMEM((1024, 256), bf16)] * 2, (*near, *far, xy_part, back_t, line_z), 28,
    )
    parts, sent, scalars = phase(parts, sent, scalars)
    ahead = (pieces[1] + jnp.concatenate([sent[0].astype(f32), jnp.zeros((2, 16, 16, 256), f32)])).astype(bf16)
    behind = (pieces[3] + jnp.concatenate([jnp.zeros((2, 16, 16, 256), f32), sent[1].astype(f32)])).astype(bf16)
    ahead, behind, scalars = phase(ahead, behind, scalars)
    sent = [hop(ahead, "y", 1), hop(behind, "y", 3)]
    parts = [hop(part, "gz", shift) for shift, part in enumerate(parts, 1)]
    x_part, y_cross, z_cross = call(
        side_kernel, "side", scalars, (4,),
        [resident, pl.BlockSpec((16, 256, 256), blocks), resident, resident],
        [pl.BlockSpec((16, 32), lambda k, s: (k, 0))] + lines,
        [shape((64, 32), f32)] + [shape((32, 256), f32)] * 2,
        [], (plane, rho, q_part, b_part), 24,
    )
    sums = call(
        small_kernel, "small", scalars, (1,),
        [whole((64, 32, 256))] * 2 + [whole((4, 32, 256)), whole((32, 64))],
        whole((4, 32, 32)),
        shape((4, 32, 32), f32),
        [], (px, pz, plane_yz.transpose(1, 0, 2), line_x), 16,
    )
    parts, sent, x_part, y_cross, z_cross, sums, scalars = phase(parts, sent, x_part, y_cross, z_cross, sums, scalars)
    here = pieces[0][:2] + sent[0][:2].astype(f32) + sent[1][:2].astype(f32)
    there = pieces[0][2:] + sent[0][2:].astype(f32) + sent[1][2:].astype(f32)
    there, scalars = phase(there, scalars)
    there = lax.ppermute(there, "x", [(i, i ^ 2) for i in range(4)])

    x_side = jnp.roll(x_part.T, 16 * at["c"], axis=0)
    both = jnp.concatenate([y_part - y_cross, x_side, sums[0], sums[1]], axis=1)
    both = all_sum(both, "gz")
    mine, inv_y = call(
        xy_kernel, "xy", scalars, (1,),
        lines + [pl.BlockSpec((16, 32, 256), lambda k, s: (s[4], 0, 0)), whole((16, 32, 256))] + [whole((17, 32, 256))] * 3,
        [whole((16, 32, 256)), whole((32, 32))],
        [shape((16, 32, 256), bf16), shape((32, 32), f32)],
        [], (line_y, line_z, px, mine, *parts), 20,
    )
    new_xz = call(
        xz_kernel, "xz", scalars, (4,),
        [resident, pl.BlockSpec((16, 32, 256), blocks), pl.BlockSpec((16, 32, 256), blocks)]
        + [pl.BlockSpec((16, 32), lambda k, s: (k, 0)), whole((32, 256)), whole((32, 32))],
        pl.BlockSpec((16, 32, 256), blocks),
        shape((64, 32, 256), bf16),
        [pltpu.VMEM((1024, 256), bf16)] * 2, (plane, ty, pz, back_t, line_y, inv_y), 20,
    )
    mine, both, there, new_xz = phase(mine, both, there, new_xz)
    x_side = both[:, 256:320]
    both = jnp.concatenate([both[:, :256], z_part - z_cross, both[:, 320:], sums[2], sums[3]], axis=1)

    quarters = [mine] + [hop(mine, "gz", shift) for shift in range(1, 4)]
    both = fold(both, "y")
    total = lax.ppermute(here[1] + there[1], "x", [(i, i ^ 1) for i in range(4)])
    total = here[0] + there[0] + total
    both, total = phase(both, total)
    both = fold(both, "x")
    region = lambda which: lax.dynamic_slice_in_dim(total, which * 8, 8, 1)
    total = region(at["zl"]) + hop(region(1 - at["zl"]), "zl", 1)
    both, total = phase(both, total)
    both = fold(fold(both, "c"), "zl")
    region = lambda which: lax.dynamic_slice_in_dim(total, which * 4, 4, 1)
    yz_side = ordered(region(at["c"]), hop(region(1 - at["c"]), "c", 1), second_c, 0)
    late = inverses(scalars, jnp.stack([both[:, 512 + 32 * i : 544 + 32 * i] for i in range(4)]))
    new_xy = jnp.zeros((32, 64, 256), bf16)
    for shift, piece in enumerate(quarters):
        new_xy = lax.dynamic_update_slice_in_dim(new_xy, piece.transpose(1, 0, 2), ((at["gz"] + 4 - shift) % 4) * 16, 1)
    gram_yz, gram_x = both[:, 544:576], both[:, 608:640]
    new_yz = update(late[3], yz_side - exact("rs,syz->ryz", gram_x, plane_yz.astype(f32)), plane_yz)
    new_x = update(late[1], x_side - exact("rs,sx->rx", gram_yz, line_x.astype(f32)), line_x)
    new_y = update(late[0], both[:, :256], line_y)
    new_z = update(late[2], both[:, 256:512], line_z)
    return (new_xy, new_xz.transpose(1, 0, 2), new_yz, new_x, new_y, new_z)


def solution(mesh):
    shape = tuple(sizes.values())
    mesh = Mesh(mesh.devices.reshape(shape), tuple(sizes))
    xy = ("y", "x", "zl", "c")
    outs = (
        P(None, xy, None),
        P(None, xy, "gz"),
        P(None, xy, "gz"),
        P(None, xy),
        P(),
        P(None, "gz"),
    )
    return jax.shard_map(
        shards,
        mesh=mesh,
        in_specs=(P(xy, None, "gz"),) + outs,
        out_specs=outs,
        check_vma=False,
    )
```

```python
import functools

import jax
import jax.numpy as jnp
from jax import lax
from jax.experimental import pallas as pl
from jax.experimental.layout import Layout, with_layout_constraint
from jax.experimental.pallas import tpu as pltpu
from jax.sharding import Mesh, PartitionSpec as P

ridge = 1.0
f32 = jnp.float32
bf16 = jnp.bfloat16
sizes = {"y": 4, "x": 4, "zl": 2, "c": 2, "gz": 4}
HIGH = lax.Precision.HIGHEST
MB = 2**20


def hop(value, axis, shift):
    count = sizes[axis]
    return lax.ppermute(value, axis, [(i, (i + shift) % count) for i in range(count)])


def pair_hop(value, flip):
    return lax.ppermute(value, ("zl", "c"), [(i, i ^ flip) for i in range(4)])


def nn(left, right, **kw):
    return lax.dot_general(left, right, (((1,), (0,)), ((), ())), preferred_element_type=f32, **kw)


def nt(left, right, **kw):
    return lax.dot_general(left, right, (((1,), (1,)), ((), ())), preferred_element_type=f32, **kw)


def tn(left, right):
    return lax.dot_general(left, right, (((0,), (0,)), ((), ())), preferred_element_type=f32)


def iota(shape, axis):
    return lax.broadcasted_iota(jnp.int32, shape, axis)


def one_where(mask, kind=f32):
    return jnp.where(mask, 1.0, 0.0).astype(kind)


def call(kernel, name, scalars, grid, in_specs, out_specs, out_shape, scratch, args, limit=50, aliases=None):
    return pl.pallas_call(
        kernel,
        name=name,
        input_output_aliases=aliases or {},
        out_shape=out_shape,
        grid_spec=pltpu.PrefetchScalarGridSpec(
            num_scalar_prefetch=1, grid=grid, in_specs=in_specs, out_specs=out_specs, scratch_shapes=scratch
        ),
        compiler_params=pltpu.CompilerParams(vmem_limit_bytes=limit * MB),
        cost_estimate=pl.CostEstimate(flops=1000, bytes_accessed=1000, transcendentals=0),
    )(scalars, *args)


def whole(shape):
    return pl.BlockSpec(shape, lambda *_: (0,) * len(shape))


def invert(work):
    shape = work.shape
    rows, cols = iota(shape, 1), iota(shape, 2)
    work = work + ridge * one_where(rows == cols)
    for k in range(shape[1]):
        row, col = work[:, k : k + 1, :], work[:, :, k : k + 1]
        pivot = 1.0 / work[:, k : k + 1, k : k + 1]
        scaled = row * pivot
        work = jnp.where(cols == k, 0.0, work) - col * jnp.where(cols == k, pivot, scaled)
        work = jnp.where(rows == k, jnp.where(cols == k, pivot, scaled), work)
    return work


def inverse_kernel(s_ref, gram_ref, out_ref):
    out_ref[...] = invert(gram_ref[...])


def inverses(scalars, grams):
    shape = grams.shape
    return call(
        inverse_kernel, "inverse", scalars, (1,), [whole(shape)], whole(shape), jax.ShapeDtypeStruct(shape, f32), [], (grams,), 16
    )


def small_kernel(s_ref, px_ref, pz_ref, own_ref, lx_ref, sums_ref):
    def step(x, carry):
        xy, xz = carry
        return xy + nt(px_ref[x], px_ref[x]), xz + nt(pz_ref[x], pz_ref[x])

    zero = jnp.zeros((32, 32), f32)
    gram_xy, gram_xz = lax.fori_loop(0, 64, step, (zero, zero), unroll=8)
    gram_yz = zero
    for y in range(4):
        gram_yz = gram_yz + nt(own_ref[y], own_ref[y])
    sums_ref[0] = gram_xz
    sums_ref[1] = gram_yz
    sums_ref[2] = gram_xy
    sums_ref[3] = nt(lx_ref[...], lx_ref[...])


def rho_kernel(s_ref, t_ref, px_ref, pz_ref, ly_ref, lz_ref, rho_ref, ty_ref, xy_ref, yp_ref, zp_ref):
    line_y, line_z = ly_ref[...], lz_ref[...]

    @pl.when(pl.program_id(0) == 0)
    def _():
        yp_ref[...] = jnp.zeros_like(yp_ref)
        zp_ref[...] = jnp.zeros_like(zp_ref)

    def step(x, _):
        over_y = jnp.concatenate([line_y, px_ref[x]], axis=0)
        over_z = jnp.concatenate([pz_ref[x], line_z], axis=0)
        rho = (t_ref[x].astype(f32) - tn(over_y, over_z)).astype(bf16)
        rho_ref[x] = rho
        from_z = nt(over_z, rho)
        from_y = nn(over_y, rho)
        ty_ref[x] = from_y[:32]
        zp_ref[...] += from_y[32:]
        yp_ref[...] += from_z[:32]
        xy_ref[x] = from_z[32:]
        return 0

    lax.fori_loop(0, 8, step, 0, unroll=8)


def yz_kernel(s_ref, lx_ref, rho_ref, keep_ref, send_ref, kron):
    @pl.when(pl.program_id(0) == 0)
    def _():
        spread = one_where(iota((64, 1024), 1) // 16 == iota((64, 1024), 0), bf16)
        wide = nn(lx_ref[...], spread)
        mask = iota((16, 1024), 1) % 16 == iota((16, 1024), 0)
        for r in range(32):
            kron[16 * r : 16 * r + 16] = jnp.where(mask, wide[r : r + 1], 0.0).astype(bf16)

    out = nn(kron[...], rho_ref[...].reshape(1024, 256)).astype(bf16)
    keep_ref[...] = out[:256].reshape(1, 1, 16, 16, 256)
    send_ref[...] = out[256:].reshape(1, 1, 16, 16, 256)


def spread_x(lines):
    count = lines.shape[0]
    wide = nn(lines, one_where(iota((32, 1024), 1) // 32 == iota((32, 1024), 0), bf16))
    mask = iota((32, 1024), 1) % 32 == iota((32, 1024), 0)
    return jnp.where(mask[None], wide[:, None, :], 0.0).astype(bf16).reshape(count * 32, 1024)


def apply_inverse(inverse, rows):
    tall = one_where(iota((256, 32), 0) % 32 == iota((256, 32), 1))
    wide = nt(nn(tall, inverse, precision=HIGH), tall, precision=HIGH)
    wide = jnp.where(iota((256, 256), 0) // 32 == iota((256, 256), 1) // 32, wide, 0.0)
    count = rows.shape[0] // 256
    return jnp.concatenate([nn(wide, rows[256 * i : 256 * i + 256], precision=HIGH) for i in range(count)], axis=0)


def row_of(s_ref, i, j):
    return pl.multiple_of((((s_ref[0] + 4 - j) % 4) * 4 + (s_ref[1] + 4 - i) % 4) * 16, 16)


def halves(value):
    high = value.astype(bf16)
    return high, (value - high.astype(f32)).astype(bf16)


def part_kernel(s_ref, n0, n1, n2, n3, f0, f1, f2, f3, part_ref, lx_ref, lz_ref, plane_ref, m0_ref, m1_ref, m2_ref, m3_ref, w_high, w_low):
    k = pl.program_id(0)

    @pl.when(k == 0)
    def _():
        for i in range(4):
            for j in range(4):
                rows = pl.ds(row_of(s_ref, i, j), 16)
                for r in range(16):
                    plane_ref[r, rows] = (n0, n1, n2, n3)[i][j, r]
                    plane_ref[16 + r, rows] = (f0, f1, f2, f3)[i][j, r]
        line_z = lz_ref[...]
        gram = nt(line_z, line_z)
        high, low = halves(gram)
        middle, low = halves(gram - high.astype(f32))
        tile = jnp.concatenate([high.astype(f32), middle.astype(f32), low.astype(f32), jnp.zeros((32, 160), f32)], axis=1)
        for ref in (m1_ref, m2_ref, m3_ref):
            ref[16] = tile.astype(bf16)

        def step(s, _):
            rows = pl.ds(pl.multiple_of(s * 32, 32), 32)
            w_high[rows], w_low[rows] = halves(nt(line_z, plane_ref[s]))
            return 0

        lax.fori_loop(0, 32, step, 0, unroll=4)

    kron = spread_x(lx_ref[...])
    total = part_ref[...].reshape(512, 256) - nn(kron, w_high[...]) - nn(kron, w_low[...])
    for which, ref in enumerate((m0_ref, m1_ref, m2_ref, m3_ref)):

        @pl.when(k == which)
        def _(ref=ref):
            ref[:16] = total.reshape(16, 32, 256).astype(ref.dtype)


def xy_kernel(s_ref, ly_ref, lz_ref, old_ref, own_ref, g1_ref, g2_ref, g3_ref, new_ref, inv_ref):
    total, gram = own_ref[...], nt(lz_ref[...], lz_ref[...])
    for ref in (g1_ref, g2_ref, g3_ref):
        total = total + ref[:16].astype(f32)
        tile = ref[16].astype(f32)
        gram = gram + (tile[:, :32] + (tile[:, 32:64] + tile[:, 64:96]))
    both = invert(jnp.stack([gram, nt(ly_ref[...], ly_ref[...])]))
    inverse = both[0]
    inv_ref[...] = both[1]
    old = old_ref[...].astype(f32).reshape(512, 256)
    new = old + apply_inverse(inverse, total.reshape(512, 256) - old)
    new_ref[...] = new.astype(bf16).reshape(16, 32, 256)


def side_kernel(s_ref, plane_ref, rho_ref, q_ref, b_ref, yp_ref, zp_ref, sums_ref, gz_ref, xy_ref):
    k = pl.program_id(0)

    @pl.when(k == 0)
    def _():
        def step(s, carry):
            y_cross, z_cross = carry
            over_y = nn(jnp.concatenate(halves(b_ref[s]), axis=0), plane_ref[s])
            over_z = nt(jnp.concatenate(halves(q_ref[s]), axis=0), plane_ref[s])
            return y_cross + over_z[:32] + over_z[32:], z_cross + over_y[:32] + over_y[32:]

        zero = jnp.zeros((32, 256), f32)
        y_cross, z_cross = lax.fori_loop(0, 32, step, (zero, zero), unroll=4)
        gz_ref[:, :256] = yp_ref[...] - y_cross
        gz_ref[:, 256:] = jnp.concatenate([sums_ref[0], sums_ref[1], jnp.zeros((32, 64), f32)], axis=1)
        xy_ref[:, :256] = zp_ref[...] - z_cross
        xy_ref[:, 256:] = jnp.concatenate([sums_ref[2], sums_ref[3], jnp.zeros((32, 64), f32)], axis=1)

    total = jnp.zeros((256, 512), f32)
    for first in range(0, 16, 8):
        rows = [slice(16 * j, 16 * j + 16) for j in range(first, first + 8)]
        left = jnp.concatenate([rho_ref[:, r, :].reshape(256, 256) for r in rows], axis=1)
        right = jnp.concatenate([plane_ref[:, r, :].reshape(512, 256) for r in rows], axis=1)
        total = total + nt(left, right)
    total = jnp.where(iota((256, 512), 0) % 16 == iota((256, 512), 1) % 16, total, 0.0)
    over_x = nn(one_where(iota((16, 256), 1) // 16 == iota((16, 256), 0)), total, precision=HIGH)
    turned = (iota((32, 512), 1) // 16 + 16 * s_ref[3]) % 32 == iota((32, 512), 0)
    over_x = nt(one_where(turned), over_x, precision=HIGH)
    placed = one_where(iota((16, 128), 1) == iota((16, 128), 0) + 16 * k + 64)
    gz_ref[:, 256:] += nn(over_x, placed, precision=HIGH)


def xz_kernel(s_ref, plane_ref, ty_ref, pz_ref, lx_ref, ly_ref, inv_ref, new_ref, u_high, u_low):
    @pl.when(pl.program_id(0) == 0)
    def _():
        line_y = ly_ref[...]

        def step(s, _):
            rows = pl.ds(pl.multiple_of(s * 32, 32), 32)
            u_high[rows], u_low[rows] = halves(nn(line_y, plane_ref[s]))
            return 0

        lax.fori_loop(0, 32, step, 0, unroll=4)

    kron = spread_x(lx_ref[...])
    total = ty_ref[...].reshape(512, 256) - nn(kron, u_high[...]) - nn(kron, u_low[...])
    old = pz_ref[...].astype(f32).reshape(512, 256)
    new_ref[...] = (old + apply_inverse(inv_ref[...], total - old)).astype(bf16).reshape(16, 32, 256)


def contract(form, left, right):
    return jnp.einsum(form, left, right, preferred_element_type=f32)


def exact(form, left, right):
    return jnp.einsum(form, left, right, precision=HIGH, preferred_element_type=f32)


def ordered(mine, other, second, axis):
    return jnp.concatenate([jnp.where(second, other, mine), jnp.where(second, mine, other)], axis=axis)


def all_sum(value, axis):
    return (value + hop(value, axis, 2)) + (hop(value, axis, 1) + hop(value, axis, 3))


def fold(value, axis):
    count = sizes[axis]
    for bit in (1, 2)[: count // 2]:
        value = value + lax.ppermute(value, axis, [(i, i ^ bit) for i in range(count)])
    return value


def update(inverse, part, old):
    old = old.astype(f32)
    shape = part.shape
    step = jnp.dot(inverse, (part - old).reshape(32, -1), precision=HIGH)
    return (old + step.reshape(shape)).astype(bf16)


def phase(*values):
    return lax.optimization_barrier(values)


def shards(target, plane_xy, plane_xz, plane_yz, line_x, line_y, line_z):
    at = {name: lax.axis_index(name) for name in sizes}
    scalars = jnp.stack([at["y"], at["x"], at["zl"], at["c"], at["gz"]]).astype(jnp.int32)
    second_c, second_z = at["c"] == 1, at["zl"] == 1
    shape = jax.ShapeDtypeStruct
    lines = [whole((32, 256))] * 2

    half = lambda value, which: lax.dynamic_slice_in_dim(value, which * 16, 16, 0)
    own, other = half(plane_yz, at["c"]), half(plane_yz, 1 - at["c"])
    here = ordered(own, pair_hop(other, 1), second_c, 1)
    there = ordered(pair_hop(own, 2), pair_hop(other, 3), second_c, 1)
    block = ordered(here, there, second_z, 1)
    block, scalars = phase(block, scalars)

    got = [hop(block, "y", shift) for shift in range(1, 4)]
    px, pz = plane_xy.transpose(1, 0, 2), plane_xz.transpose(1, 0, 2)
    block = jnp.stack([block] + got)
    block, px, pz, scalars = phase(block, px, pz, scalars)
    got = [hop(block, "x", shift) for shift in range(1, 4)]
    far = [hop(block, "c", 1)]
    blocks = lambda k, s: (k, 0, 0)
    tiles = [pl.BlockSpec(size, blocks) for size in ((8, 256, 256), (8, 32, 256), (8, 32, 256))]
    rho, ty, xy_part, y_part, z_part = call(
        rho_kernel, "rho", scalars, (8,), tiles + lines, tiles + lines,
        [shape((64, 256, 256), bf16)] + [shape((64, 32, 256), f32)] * 2 + [shape((32, 256), f32)] * 2,
        [], (target, px, pz, line_y, line_z), 44,
    )

    back = jnp.roll(line_x, -16 * at["c"], axis=0)
    to_block = lambda j, s: ((j // 4 + 4 - s[0]) % 4, (j % 4) ^ s[1], 0, 0, 0)
    keep, send = call(
        yz_kernel, "yz", scalars, (16,),
        [whole((32, 64)), pl.BlockSpec((64, 16, 256), lambda j, s: (0, j, 0))],
        [pl.BlockSpec((1, 1, 16, 16, 256), to_block)] * 2,
        [shape((4, 4, 16, 16, 256), bf16)] * 2,
        [pltpu.VMEM((512, 1024), bf16)], (back, rho), 16,
    )
    got, far, send, scalars = phase(got, far, send, scalars)
    near = [block] + got
    came, far = hop(send, "c", 1), far + [hop(piece, "c", 1) for piece in got]
    rows = Layout(major_to_minor=(0, 1, 2))
    q_part = with_layout_constraint(contract("sx,xrz->srz", back, pz), rows)
    b_part = with_layout_constraint(contract("sx,xry->sry", back, px), rows)
    far, came, q_part, b_part, scalars = phase(far, came, q_part, b_part, scalars)
    pieces = [keep[i].astype(f32) + came[i].astype(f32) for i in range(4)]
    sent = [pieces[2][:2].astype(bf16), pieces[2][2:].astype(bf16)]
    sent, scalars = phase(sent, scalars)
    sent = [hop(sent[0], "y", 1), hop(sent[1], "y", 3)]

    back_t = back.T
    resident = pl.BlockSpec(memory_space=pltpu.VMEM)
    turned = lambda k, s: ((s[4] + k) % 4, 0, 0)
    plane, mine, *parts = call(
        part_kernel, "part", scalars, (4,),
        [whole((4, 16, 16, 256))] * 8
        + [pl.BlockSpec((16, 32, 256), turned), pl.BlockSpec((16, 32), lambda k, s: ((s[4] + k) % 4, 0)), whole((32, 256))],
        [resident, whole((16, 32, 256))] + [whole((17, 32, 256))] * 3,
        [shape((32, 256, 256), bf16), shape((16, 32, 256), f32)] + [shape((17, 32, 256), bf16)] * 3,
        [pltpu.VMEM((1024, 256), bf16)] * 2, (*near, *far, xy_part, back_t, line_z), 28,
    )
    parts, sent, scalars = phase(parts, sent, scalars)
    ahead = (pieces[1] + jnp.concatenate([sent[0].astype(f32), jnp.zeros((2, 16, 16, 256), f32)])).astype(bf16)
    behind = (pieces[3] + jnp.concatenate([jnp.zeros((2, 16, 16, 256), f32), sent[1].astype(f32)])).astype(bf16)
    ahead, behind, scalars = phase(ahead, behind, scalars)
    sent = [hop(ahead, "y", 1), hop(behind, "y", 3)]
    parts = [hop(part, "gz", shift) for shift, part in enumerate(parts, 1)]
    sums = call(
        small_kernel, "small", scalars, (1,),
        [whole((64, 32, 256))] * 2 + [whole((4, 32, 256)), whole((32, 64))],
        whole((4, 32, 32)),
        shape((4, 32, 32), f32),
        [], (px, pz, plane_yz.transpose(1, 0, 2), line_x), 16,
    )
    both, rest = call(
        side_kernel, "side", scalars, (4,),
        [resident, pl.BlockSpec((16, 256, 256), blocks), resident, resident] + lines + [whole((4, 32, 32))],
        [whole((32, 384))] * 2,
        [shape((32, 384), f32)] * 2,
        [], (plane, rho, q_part, b_part, y_part, z_part, sums), 52,
    )
    parts, sent, both, rest, scalars = phase(parts, sent, both, rest, scalars)
    here = pieces[0][:2] + sent[0][:2].astype(f32) + sent[1][:2].astype(f32)
    there = pieces[0][2:] + sent[0][2:].astype(f32) + sent[1][2:].astype(f32)
    there, scalars = phase(there, scalars)
    there = lax.ppermute(there, "x", [(i, i ^ 2) for i in range(4)])

    both = all_sum(both, "gz")
    mine, inv_y = call(
        xy_kernel, "xy", scalars, (1,),
        lines + [pl.BlockSpec((16, 32, 256), lambda k, s: (s[4], 0, 0)), whole((16, 32, 256))] + [whole((17, 32, 256))] * 3,
        [whole((16, 32, 256)), whole((32, 32))],
        [shape((16, 32, 256), bf16), shape((32, 32), f32)],
        [], (line_y, line_z, px, mine, *parts), 20,
    )
    new_xz = call(
        xz_kernel, "xz", scalars, (4,),
        [resident, pl.BlockSpec((16, 32, 256), blocks), pl.BlockSpec((16, 32, 256), blocks)]
        + [pl.BlockSpec((16, 32), lambda k, s: (k, 0)), whole((32, 256)), whole((32, 32))],
        pl.BlockSpec((16, 32, 256), blocks),
        shape((64, 32, 256), bf16),
        [pltpu.VMEM((1024, 256), bf16)] * 2, (plane, ty, pz, back_t, line_y, inv_y), 20,
    )
    mine, both, there, new_xz = phase(mine, both, there, new_xz)
    x_side = both[:, 320:]
    both = jnp.concatenate([both, rest], axis=1)

    quarters = [mine] + [hop(mine, "gz", shift) for shift in range(1, 4)]
    both = fold(both, "y")
    total = lax.ppermute(here[1] + there[1], "x", [(i, i ^ 1) for i in range(4)])
    total = here[0] + there[0] + total
    both, total = phase(both, total)
    both = fold(both, "x")
    region = lambda which: lax.dynamic_slice_in_dim(total, which * 8, 8, 1)
    total = region(at["zl"]) + hop(region(1 - at["zl"]), "zl", 1)
    both, total = phase(both, total)
    both = fold(fold(both, "c"), "zl")
    region = lambda which: lax.dynamic_slice_in_dim(total, which * 4, 4, 1)
    yz_side = ordered(region(at["c"]), hop(region(1 - at["c"]), "c", 1), second_c, 0)
    both, quarters[3] = phase(both, quarters[3])
    at_gram = {"xz": 256, "yz": 288, "xy": 640, "x": 672}
    gram_xz, gram_yz, gram_xy, gram_x = (both[:, first : first + 32] for first in at_gram.values())
    late = inverses(scalars, jnp.stack([gram_xz, gram_yz, gram_xy, gram_x]))
    new_xy = jnp.zeros((32, 64, 256), bf16)
    for shift, piece in enumerate(quarters):
        new_xy = lax.dynamic_update_slice_in_dim(new_xy, piece.transpose(1, 0, 2), ((at["gz"] + 4 - shift) % 4) * 16, 1)
    new_yz = update(late[3], yz_side - exact("rs,syz->ryz", gram_x, plane_yz.astype(f32)), plane_yz)
    new_x = update(late[1], x_side - exact("rs,sx->rx", gram_yz, line_x.astype(f32)), line_x)
    new_y = update(late[0], both[:, :256], line_y)
    new_z = update(late[2], both[:, 384:640], line_z)
    return (new_xy, new_xz.transpose(1, 0, 2), new_yz, new_x, new_y, new_z)


def solution(mesh):
    shape = tuple(sizes.values())
    mesh = Mesh(mesh.devices.reshape(shape), tuple(sizes))
    xy = ("y", "x", "zl", "c")
    outs = (
        P(None, xy, None),
        P(None, xy, "gz"),
        P(None, xy, "gz"),
        P(None, xy),
        P(),
        P(None, "gz"),
    )
    return jax.shard_map(
        shards,
        mesh=mesh,
        in_specs=(P(xy, None, "gz"),) + outs,
        out_specs=outs,
        check_vma=False,
    )
```

```python
import functools

import jax
import jax.numpy as jnp
from jax import lax
from jax.experimental import pallas as pl
from jax.experimental.layout import Layout, with_layout_constraint
from jax.experimental.pallas import tpu as pltpu
from jax.sharding import Mesh, PartitionSpec as P

ridge = 1.0
f32 = jnp.float32
bf16 = jnp.bfloat16
sizes = {"y": 4, "x": 4, "zl": 2, "c": 2, "gz": 4}
HIGH = lax.Precision.HIGHEST
MB = 2**20


def hop(value, axis, shift):
    count = sizes[axis]
    return lax.ppermute(value, axis, [(i, (i + shift) % count) for i in range(count)])


def pair_hop(value, flip):
    return lax.ppermute(value, ("zl", "c"), [(i, i ^ flip) for i in range(4)])


def nn(left, right, **kw):
    return lax.dot_general(left, right, (((1,), (0,)), ((), ())), preferred_element_type=f32, **kw)


def nt(left, right, **kw):
    return lax.dot_general(left, right, (((1,), (1,)), ((), ())), preferred_element_type=f32, **kw)


def tn(left, right):
    return lax.dot_general(left, right, (((0,), (0,)), ((), ())), preferred_element_type=f32)


def iota(shape, axis):
    return lax.broadcasted_iota(jnp.int32, shape, axis)


def one_where(mask, kind=f32):
    return jnp.where(mask, 1.0, 0.0).astype(kind)


def call(kernel, name, scalars, grid, in_specs, out_specs, out_shape, scratch, args, limit=50, aliases=None):
    return pl.pallas_call(
        kernel,
        name=name,
        input_output_aliases=aliases or {},
        out_shape=out_shape,
        grid_spec=pltpu.PrefetchScalarGridSpec(
            num_scalar_prefetch=1, grid=grid, in_specs=in_specs, out_specs=out_specs, scratch_shapes=scratch
        ),
        compiler_params=pltpu.CompilerParams(vmem_limit_bytes=limit * MB),
        cost_estimate=pl.CostEstimate(flops=1000, bytes_accessed=1000, transcendentals=0),
    )(scalars, *args)


def whole(shape):
    return pl.BlockSpec(shape, lambda *_: (0,) * len(shape))


def invert(work):
    shape = work.shape
    rows, cols = iota(shape, 1), iota(shape, 2)
    work = work + ridge * one_where(rows == cols)
    for k in range(shape[1]):
        row, col = work[:, k : k + 1, :], work[:, :, k : k + 1]
        pivot = 1.0 / work[:, k : k + 1, k : k + 1]
        scaled = row * pivot
        work = jnp.where(cols == k, 0.0, work) - col * jnp.where(cols == k, pivot, scaled)
        work = jnp.where(rows == k, jnp.where(cols == k, pivot, scaled), work)
    return work


def small_kernel(s_ref, px_ref, pz_ref, own_ref, lx_ref, sums_ref):
    def step(x, carry):
        xy, xz = carry
        return xy + nt(px_ref[x], px_ref[x]), xz + nt(pz_ref[x], pz_ref[x])

    zero = jnp.zeros((32, 32), f32)
    gram_xy, gram_xz = lax.fori_loop(0, 64, step, (zero, zero), unroll=8)
    gram_yz = zero
    for y in range(4):
        gram_yz = gram_yz + nt(own_ref[y], own_ref[y])
    sums_ref[0] = gram_xz
    sums_ref[1] = gram_yz
    sums_ref[2] = gram_xy
    sums_ref[3] = nt(lx_ref[...], lx_ref[...])


def rho_kernel(s_ref, t_ref, px_ref, pz_ref, ly_ref, lz_ref, rho_ref, ty_ref, xy_ref, yp_ref, zp_ref):
    line_y, line_z = ly_ref[...], lz_ref[...]

    @pl.when(pl.program_id(0) == 0)
    def _():
        yp_ref[...] = jnp.zeros_like(yp_ref)
        zp_ref[...] = jnp.zeros_like(zp_ref)

    def step(x, _):
        over_y = jnp.concatenate([line_y, px_ref[x]], axis=0)
        over_z = jnp.concatenate([pz_ref[x], line_z], axis=0)
        rho = (t_ref[x].astype(f32) - tn(over_y, over_z)).astype(bf16)
        rho_ref[8 * pl.program_id(0) + x] = rho
        from_z = nt(over_z, rho)
        from_y = nn(over_y, rho)
        ty_ref[x] = from_y[:32]
        zp_ref[...] += from_y[32:]
        yp_ref[...] += from_z[:32]
        xy_ref[x] = from_z[32:]
        return 0

    lax.fori_loop(0, 8, step, 0, unroll=8)


def yz_kernel(s_ref, lx_ref, rho_ref, keep_ref, send_ref, kron):
    @pl.when(pl.program_id(0) == 0)
    def _():
        spread = one_where(iota((64, 1024), 1) // 16 == iota((64, 1024), 0), bf16)
        wide = nn(lx_ref[...], spread)
        mask = iota((16, 1024), 1) % 16 == iota((16, 1024), 0)
        for r in range(32):
            kron[16 * r : 16 * r + 16] = jnp.where(mask, wide[r : r + 1], 0.0).astype(bf16)

    rows = pl.ds(pl.multiple_of(16 * pl.program_id(0), 16), 16)
    out = nn(kron[...], rho_ref[:, rows, :].reshape(1024, 256)).astype(bf16)
    keep_ref[...] = out[:256].reshape(1, 1, 16, 16, 256)
    send_ref[...] = out[256:].reshape(1, 1, 16, 16, 256)


def spread_x(lines):
    count = lines.shape[0]
    wide = nn(lines, one_where(iota((32, 1024), 1) // 32 == iota((32, 1024), 0), bf16))
    mask = iota((32, 1024), 1) % 32 == iota((32, 1024), 0)
    return jnp.where(mask[None], wide[:, None, :], 0.0).astype(bf16).reshape(count * 32, 1024)


def apply_inverse(inverse, rows):
    tall = one_where(iota((256, 32), 0) % 32 == iota((256, 32), 1))
    wide = nt(nn(tall, inverse, precision=HIGH), tall, precision=HIGH)
    wide = jnp.where(iota((256, 256), 0) // 32 == iota((256, 256), 1) // 32, wide, 0.0)
    count = rows.shape[0] // 256
    return jnp.concatenate([nn(wide, rows[256 * i : 256 * i + 256], precision=HIGH) for i in range(count)], axis=0)


def row_of(s_ref, i, j):
    return pl.multiple_of((((s_ref[0] + 4 - j) % 4) * 4 + (s_ref[1] + 4 - i) % 4) * 16, 16)


def halves(value):
    high = value.astype(bf16)
    return high, (value - high.astype(f32)).astype(bf16)


def part_kernel(s_ref, n0, n1, n2, n3, f0, f1, f2, f3, part_ref, lx_ref, lz_ref, plane_ref, m0_ref, m1_ref, m2_ref, m3_ref, w_high, w_low):
    k = pl.program_id(0)

    @pl.when(k == 0)
    def _():
        for i in range(4):
            for j in range(4):
                rows = pl.ds(row_of(s_ref, i, j), 16)
                for r in range(16):
                    plane_ref[r, rows] = (n0, n1, n2, n3)[i][j, r]
                    plane_ref[16 + r, rows] = (f0, f1, f2, f3)[i][j, r]
        line_z = lz_ref[...]
        gram = nt(line_z, line_z)
        high, low = halves(gram)
        middle, low = halves(gram - high.astype(f32))
        tile = jnp.concatenate([high.astype(f32), middle.astype(f32), low.astype(f32), jnp.zeros((32, 160), f32)], axis=1)
        for ref in (m1_ref, m2_ref, m3_ref):
            ref[16] = tile.astype(bf16)

        def step(s, _):
            rows = pl.ds(pl.multiple_of(s * 32, 32), 32)
            w_high[rows], w_low[rows] = halves(nt(line_z, plane_ref[s]))
            return 0

        lax.fori_loop(0, 32, step, 0, unroll=4)

    kron = spread_x(lx_ref[...])
    total = part_ref[...].reshape(512, 256) - nn(kron, w_high[...]) - nn(kron, w_low[...])
    for which, ref in enumerate((m0_ref, m1_ref, m2_ref, m3_ref)):

        @pl.when(k == which)
        def _(ref=ref):
            ref[:16] = total.reshape(16, 32, 256).astype(ref.dtype)


def xy_kernel(s_ref, ly_ref, lz_ref, old_ref, own_ref, g1_ref, g2_ref, g3_ref, new_ref, inv_ref):
    total, gram = own_ref[...], nt(lz_ref[...], lz_ref[...])
    for ref in (g1_ref, g2_ref, g3_ref):
        total = total + ref[:16].astype(f32)
        tile = ref[16].astype(f32)
        gram = gram + (tile[:, :32] + (tile[:, 32:64] + tile[:, 64:96]))
    both = invert(jnp.stack([gram, nt(ly_ref[...], ly_ref[...])]))
    inverse = both[0]
    inv_ref[...] = both[1]
    old = old_ref[...].astype(f32).reshape(512, 256)
    new = old + apply_inverse(inverse, total.reshape(512, 256) - old)
    new_ref[...] = new.astype(bf16).reshape(16, 32, 256)


def side_kernel(s_ref, plane_ref, rho_ref, q_ref, b_ref, yp_ref, zp_ref, sums_ref, gz_ref, xy_ref):
    k = pl.program_id(0)

    @pl.when(k == 0)
    def _():
        def step(s, carry):
            y_cross, z_cross = carry
            over_y = nn(jnp.concatenate(halves(b_ref[s]), axis=0), plane_ref[s])
            over_z = nt(jnp.concatenate(halves(q_ref[s]), axis=0), plane_ref[s])
            return y_cross + over_z[:32] + over_z[32:], z_cross + over_y[:32] + over_y[32:]

        zero = jnp.zeros((32, 256), f32)
        y_cross, z_cross = lax.fori_loop(0, 32, step, (zero, zero), unroll=4)
        gz_ref[:, :256] = yp_ref[...] - y_cross
        gz_ref[:, 256:] = jnp.concatenate([sums_ref[0], sums_ref[1], jnp.zeros((32, 64), f32)], axis=1)
        xy_ref[:, :256] = zp_ref[...] - z_cross
        xy_ref[:, 256:] = jnp.concatenate([sums_ref[2], sums_ref[3], jnp.zeros((32, 64), f32)], axis=1)

    total = jnp.zeros((256, 512), f32)
    for first in range(0, 16, 8):
        rows = [slice(16 * j, 16 * j + 16) for j in range(first, first + 8)]
        left = jnp.concatenate([rho_ref[:, r, :].reshape(256, 256) for r in rows], axis=1)
        right = jnp.concatenate([plane_ref[:, r, :].reshape(512, 256) for r in rows], axis=1)
        total = total + nt(left, right)
    total = jnp.where(iota((256, 512), 0) % 16 == iota((256, 512), 1) % 16, total, 0.0)
    over_x = nn(one_where(iota((16, 256), 1) // 16 == iota((16, 256), 0)), total, precision=HIGH)
    turned = (iota((32, 512), 1) // 16 + 16 * s_ref[3]) % 32 == iota((32, 512), 0)
    over_x = nt(one_where(turned), over_x, precision=HIGH)
    placed = one_where(iota((16, 128), 1) == iota((16, 128), 0) + 16 * k + 64)
    gz_ref[:, 256:] += nn(over_x, placed, precision=HIGH)


def xz_kernel(s_ref, plane_ref, ty_ref, pz_ref, lx_ref, ly_ref, inv_ref, new_ref, u_high, u_low):
    @pl.when(pl.program_id(0) == 0)
    def _():
        line_y = ly_ref[...]

        def step(s, _):
            rows = pl.ds(pl.multiple_of(s * 32, 32), 32)
            u_high[rows], u_low[rows] = halves(nn(line_y, plane_ref[s]))
            return 0

        lax.fori_loop(0, 32, step, 0, unroll=4)

    kron = spread_x(lx_ref[...])
    total = ty_ref[...].reshape(512, 256) - nn(kron, u_high[...]) - nn(kron, u_low[...])
    old = pz_ref[...].astype(f32).reshape(512, 256)
    new_ref[...] = (old + apply_inverse(inv_ref[...], total - old)).astype(bf16).reshape(16, 32, 256)


def last_kernel(s_ref, sums_ref, side_ref, lx_ref, ly_ref, lz_ref, inv_ref, x_out, y_out, z_out):
    sums = sums_ref[...]
    gram_xz, gram_yz, gram_xy, gram_x = (sums[:, first : first + 32] for first in (256, 288, 640, 672))
    inverse = invert(jnp.stack([gram_xz, gram_yz, gram_xy, gram_x]))

    def solved(which, part, old):
        return old + nn(inverse[which], part - old, precision=HIGH)

    line_x = lx_ref[...].astype(f32)
    x_out[...] = solved(1, side_ref[...] - nn(gram_yz, line_x, precision=HIGH), line_x).astype(bf16)
    y_out[...] = solved(0, sums[:, :256], ly_ref[...].astype(f32)).astype(bf16)
    z_out[...] = solved(2, sums[:, 384:640], lz_ref[...].astype(f32)).astype(bf16)
    inv_ref[...] = inverse[3]


def contract(form, left, right):
    return jnp.einsum(form, left, right, preferred_element_type=f32)


def exact(form, left, right):
    return jnp.einsum(form, left, right, precision=HIGH, preferred_element_type=f32)


def ordered(mine, other, second, axis):
    return jnp.concatenate([jnp.where(second, other, mine), jnp.where(second, mine, other)], axis=axis)


def all_sum(value, axis):
    return (value + hop(value, axis, 2)) + (hop(value, axis, 1) + hop(value, axis, 3))


def fold(value, axis):
    count = sizes[axis]
    for bit in (1, 2)[: count // 2]:
        value = value + lax.ppermute(value, axis, [(i, i ^ bit) for i in range(count)])
    return value


def update(inverse, part, old):
    old = old.astype(f32)
    shape = part.shape
    step = jnp.dot(inverse, (part - old).reshape(32, -1), precision=HIGH)
    return (old + step.reshape(shape)).astype(bf16)


def phase(*values):
    return lax.optimization_barrier(values)


def shards(target, plane_xy, plane_xz, plane_yz, line_x, line_y, line_z):
    at = {name: lax.axis_index(name) for name in sizes}
    scalars = jnp.stack([at["y"], at["x"], at["zl"], at["c"], at["gz"]]).astype(jnp.int32)
    second_c, second_z = at["c"] == 1, at["zl"] == 1
    shape = jax.ShapeDtypeStruct
    lines = [whole((32, 256))] * 2

    half = lambda value, which: lax.dynamic_slice_in_dim(value, which * 16, 16, 0)
    own, other = half(plane_yz, at["c"]), half(plane_yz, 1 - at["c"])
    here = ordered(own, pair_hop(other, 1), second_c, 1)
    there = ordered(pair_hop(own, 2), pair_hop(other, 3), second_c, 1)
    block = ordered(here, there, second_z, 1)
    block, scalars = phase(block, scalars)

    got = [hop(block, "y", shift) for shift in range(1, 4)]
    px, pz = plane_xy.transpose(1, 0, 2), plane_xz.transpose(1, 0, 2)
    block = jnp.stack([block] + got)
    block, px, pz, scalars = phase(block, px, pz, scalars)
    got = [hop(block, "x", shift) for shift in range(1, 4)]
    far = [hop(block, "c", 1)]
    blocks = lambda k, s: (k, 0, 0)
    resident = pl.BlockSpec(memory_space=pltpu.VMEM)
    tiles = [pl.BlockSpec(size, blocks) for size in ((8, 256, 256), (8, 32, 256), (8, 32, 256))]
    rho, ty, xy_part, y_part, z_part = call(
        rho_kernel, "rho", scalars, (8,), tiles + lines, [resident] + tiles[1:] + lines,
        [shape((64, 256, 256), bf16)] + [shape((64, 32, 256), f32)] * 2 + [shape((32, 256), f32)] * 2,
        [], (target, px, pz, line_y, line_z), 24,
    )

    back = jnp.roll(line_x, -16 * at["c"], axis=0)
    to_block = lambda j, s: ((j // 4 + 4 - s[0]) % 4, (j % 4) ^ s[1], 0, 0, 0)
    keep, send = call(
        yz_kernel, "yz", scalars, (16,),
        [whole((32, 64)), resident],
        [pl.BlockSpec((1, 1, 16, 16, 256), to_block)] * 2,
        [shape((4, 4, 16, 16, 256), bf16)] * 2,
        [pltpu.VMEM((512, 1024), bf16)], (back, rho), 16,
    )
    got, far, send, scalars = phase(got, far, send, scalars)
    near = [block] + got
    came, far = hop(send, "c", 1), far + [hop(piece, "c", 1) for piece in got]
    rows = Layout(major_to_minor=(0, 1, 2))
    q_part = with_layout_constraint(contract("sx,xrz->srz", back, pz), rows)
    b_part = with_layout_constraint(contract("sx,xry->sry", back, px), rows)
    far, came, q_part, b_part, scalars = phase(far, came, q_part, b_part, scalars)
    pieces = [keep[i].astype(f32) + came[i].astype(f32) for i in range(4)]
    sent = [pieces[2][:2].astype(bf16), pieces[2][2:].astype(bf16)]
    sent, scalars = phase(sent, scalars)
    sent = [hop(sent[0], "y", 1), hop(sent[1], "y", 3)]

    back_t = back.T
    turned = lambda k, s: ((s[4] + k) % 4, 0, 0)
    plane, mine, *parts = call(
        part_kernel, "part", scalars, (4,),
        [whole((4, 16, 16, 256))] * 8
        + [pl.BlockSpec((16, 32, 256), turned), pl.BlockSpec((16, 32), lambda k, s: ((s[4] + k) % 4, 0)), whole((32, 256))],
        [resident, whole((16, 32, 256))] + [whole((17, 32, 256))] * 3,
        [shape((32, 256, 256), bf16), shape((16, 32, 256), f32)] + [shape((17, 32, 256), bf16)] * 3,
        [pltpu.VMEM((1024, 256), bf16)] * 2, (*near, *far, xy_part, back_t, line_z), 28,
    )
    parts, sent, scalars = phase(parts, sent, scalars)
    ahead = (pieces[1] + jnp.concatenate([sent[0].astype(f32), jnp.zeros((2, 16, 16, 256), f32)])).astype(bf16)
    behind = (pieces[3] + jnp.concatenate([jnp.zeros((2, 16, 16, 256), f32), sent[1].astype(f32)])).astype(bf16)
    ahead, behind, scalars = phase(ahead, behind, scalars)
    sent = [hop(ahead, "y", 1), hop(behind, "y", 3)]
    parts = [hop(part, "gz", shift) for shift, part in enumerate(parts, 1)]
    sums = call(
        small_kernel, "small", scalars, (1,),
        [whole((64, 32, 256))] * 2 + [whole((4, 32, 256)), whole((32, 64))],
        whole((4, 32, 32)),
        shape((4, 32, 32), f32),
        [], (px, pz, plane_yz.transpose(1, 0, 2), line_x), 16,
    )
    both, rest = call(
        side_kernel, "side", scalars, (4,),
        [resident, pl.BlockSpec((16, 256, 256), blocks), resident, resident] + lines + [whole((4, 32, 32))],
        [whole((32, 384))] * 2,
        [shape((32, 384), f32)] * 2,
        [], (plane, rho, q_part, b_part, y_part, z_part, sums), 52,
    )
    parts, sent, both, rest, scalars = phase(parts, sent, both, rest, scalars)
    here = pieces[0][:2] + sent[0][:2].astype(f32) + sent[1][:2].astype(f32)
    there = pieces[0][2:] + sent[0][2:].astype(f32) + sent[1][2:].astype(f32)
    there, scalars = phase(there, scalars)
    there = lax.ppermute(there, "x", [(i, i ^ 2) for i in range(4)])

    both = all_sum(both, "gz")
    mine, inv_y = call(
        xy_kernel, "xy", scalars, (1,),
        lines + [pl.BlockSpec((16, 32, 256), lambda k, s: (s[4], 0, 0)), whole((16, 32, 256))] + [whole((17, 32, 256))] * 3,
        [whole((16, 32, 256)), whole((32, 32))],
        [shape((16, 32, 256), bf16), shape((32, 32), f32)],
        [], (line_y, line_z, px, mine, *parts), 20,
    )
    new_xz = call(
        xz_kernel, "xz", scalars, (4,),
        [resident, pl.BlockSpec((16, 32, 256), blocks), pl.BlockSpec((16, 32, 256), blocks)]
        + [pl.BlockSpec((16, 32), lambda k, s: (k, 0)), whole((32, 256)), whole((32, 32))],
        pl.BlockSpec((16, 32, 256), blocks),
        shape((64, 32, 256), bf16),
        [pltpu.VMEM((1024, 256), bf16)] * 2, (plane, ty, pz, back_t, line_y, inv_y), 20,
    )
    mine, both, there, new_xz = phase(mine, both, there, new_xz)
    x_side = both[:, 320:]
    both = jnp.concatenate([both, rest], axis=1)

    quarters = [mine] + [hop(mine, "gz", shift) for shift in range(1, 4)]
    both = fold(fold(both, "zl"), "y")
    total = lax.ppermute(here[1] + there[1], "x", [(i, i ^ 1) for i in range(4)])
    total = here[0] + there[0] + total
    both, total = phase(both, total)
    both = fold(both, "x")
    region = lambda which: lax.dynamic_slice_in_dim(total, which * 8, 8, 1)
    total = region(at["zl"]) + hop(region(1 - at["zl"]), "zl", 1)
    both, total = phase(both, total)
    both = fold(both, "c")
    region = lambda which: lax.dynamic_slice_in_dim(total, which * 4, 4, 1)
    yz_side = ordered(region(at["c"]), hop(region(1 - at["c"]), "c", 1), second_c, 0)
    both, quarters[3] = phase(both, quarters[3])
    new_xy = jnp.zeros((32, 64, 256), bf16)
    for shift, piece in enumerate(quarters):
        new_xy = lax.dynamic_update_slice_in_dim(new_xy, piece.transpose(1, 0, 2), ((at["gz"] + 4 - shift) % 4) * 16, 1)
    inv_x, new_x, new_y, new_z = call(
        last_kernel, "last", scalars, (1,),
        [whole((32, 768))] + [whole((32, 64))] * 2 + lines, [whole((32, 32)), whole((32, 64))] + lines,
        [shape((32, 32), f32), shape((32, 64), bf16)] + [shape((32, 256), bf16)] * 2,
        [], (both, x_side, line_x, line_y, line_z), 16,
    )
    new_yz = update(inv_x, yz_side - exact("rs,syz->ryz", both[:, 672:704], plane_yz.astype(f32)), plane_yz)
    return (new_xy, new_xz.transpose(1, 0, 2), new_yz, new_x, new_y, new_z)


def solution(mesh):
    shape = tuple(sizes.values())
    mesh = Mesh(mesh.devices.reshape(shape), tuple(sizes))
    xy = ("y", "x", "zl", "c")
    outs = (
        P(None, xy, None),
        P(None, xy, "gz"),
        P(None, xy, "gz"),
        P(None, xy),
        P(),
        P(None, "gz"),
    )
    return jax.shard_map(
        shards,
        mesh=mesh,
        in_specs=(P(xy, None, "gz"),) + outs,
        out_specs=outs,
        check_vma=False,
    )
```

```python
import functools

import jax
import jax.numpy as jnp
from jax import lax
from jax.experimental import pallas as pl
from jax.experimental.layout import Layout, with_layout_constraint
from jax.experimental.pallas import tpu as pltpu
from jax.sharding import Mesh, PartitionSpec as P

ridge = 1.0
f32 = jnp.float32
bf16 = jnp.bfloat16
sizes = {"y": 4, "x": 4, "zl": 2, "c": 2, "gz": 4}
HIGH = lax.Precision.HIGHEST
MB = 2**20


def hop(value, axis, shift):
    count = sizes[axis]
    return lax.ppermute(value, axis, [(i, (i + shift) % count) for i in range(count)])


def pair_hop(value, flip):
    return lax.ppermute(value, ("zl", "c"), [(i, i ^ flip) for i in range(4)])


def nn(left, right, **kw):
    return lax.dot_general(left, right, (((1,), (0,)), ((), ())), preferred_element_type=f32, **kw)


def nt(left, right, **kw):
    return lax.dot_general(left, right, (((1,), (1,)), ((), ())), preferred_element_type=f32, **kw)


def tn(left, right):
    return lax.dot_general(left, right, (((0,), (0,)), ((), ())), preferred_element_type=f32)


def iota(shape, axis):
    return lax.broadcasted_iota(jnp.int32, shape, axis)


def one_where(mask, kind=f32):
    return jnp.where(mask, 1.0, 0.0).astype(kind)


def call(kernel, name, scalars, grid, in_specs, out_specs, out_shape, scratch, args, limit=50, aliases=None):
    return pl.pallas_call(
        kernel,
        name=name,
        input_output_aliases=aliases or {},
        out_shape=out_shape,
        grid_spec=pltpu.PrefetchScalarGridSpec(
            num_scalar_prefetch=1, grid=grid, in_specs=in_specs, out_specs=out_specs, scratch_shapes=scratch
        ),
        compiler_params=pltpu.CompilerParams(vmem_limit_bytes=limit * MB),
        cost_estimate=pl.CostEstimate(flops=1000, bytes_accessed=1000, transcendentals=0),
    )(scalars, *args)


def whole(shape):
    return pl.BlockSpec(shape, lambda *_: (0,) * len(shape))


def invert(work):
    shape = work.shape
    rows, cols = iota(shape, 1), iota(shape, 2)
    work = work + ridge * one_where(rows == cols)
    for k in range(shape[1]):
        row, col = work[:, k : k + 1, :], work[:, :, k : k + 1]
        pivot = 1.0 / work[:, k : k + 1, k : k + 1]
        scaled = row * pivot
        work = jnp.where(cols == k, 0.0, work) - col * jnp.where(cols == k, pivot, scaled)
        work = jnp.where(rows == k, jnp.where(cols == k, pivot, scaled), work)
    return work


def small_kernel(s_ref, px_ref, pz_ref, own_ref, lx_ref, sums_ref):
    def step(x, carry):
        xy, xz = carry
        return xy + nt(px_ref[x], px_ref[x]), xz + nt(pz_ref[x], pz_ref[x])

    zero = jnp.zeros((32, 32), f32)
    gram_xy, gram_xz = lax.fori_loop(0, 64, step, (zero, zero), unroll=8)
    gram_yz = zero
    for y in range(4):
        gram_yz = gram_yz + nt(own_ref[y], own_ref[y])
    sums_ref[0] = gram_xz
    sums_ref[1] = gram_yz
    sums_ref[2] = gram_xy
    sums_ref[3] = nt(lx_ref[...], lx_ref[...])


def rho_kernel(s_ref, t_ref, px_ref, pz_ref, ly_ref, lz_ref, rho_ref, ty_ref, xy_ref, yp_ref, zp_ref):
    line_y, line_z = ly_ref[...], lz_ref[...]

    @pl.when(pl.program_id(0) == 0)
    def _():
        yp_ref[...] = jnp.zeros_like(yp_ref)
        zp_ref[...] = jnp.zeros_like(zp_ref)

    def step(x, _):
        over_y = jnp.concatenate([line_y, px_ref[x]], axis=0)
        over_z = jnp.concatenate([pz_ref[x], line_z], axis=0)
        rho = (t_ref[x].astype(f32) - tn(over_y, over_z)).astype(bf16)
        rho_ref[8 * pl.program_id(0) + x] = rho
        from_z = nt(over_z, rho)
        from_y = nn(over_y, rho)
        ty_ref[x] = from_y[:32]
        zp_ref[...] += from_y[32:]
        yp_ref[...] += from_z[:32]
        xy_ref[x] = from_z[32:]
        return 0

    lax.fori_loop(0, 8, step, 0, unroll=8)


def yz_kernel(s_ref, lx_ref, rho_ref, keep_ref, send_ref, kron):
    @pl.when(pl.program_id(0) == 0)
    def _():
        spread = one_where(iota((64, 1024), 1) // 16 == iota((64, 1024), 0), bf16)
        wide = nn(lx_ref[...], spread)
        mask = iota((16, 1024), 1) % 16 == iota((16, 1024), 0)
        for r in range(32):
            kron[16 * r : 16 * r + 16] = jnp.where(mask, wide[r : r + 1], 0.0).astype(bf16)

    rows = pl.ds(pl.multiple_of(16 * pl.program_id(0), 16), 16)
    out = nn(kron[...], rho_ref[:, rows, :].reshape(1024, 256)).astype(bf16)
    keep_ref[...] = out[:256].reshape(1, 1, 16, 16, 256)
    send_ref[...] = out[256:].reshape(1, 1, 16, 16, 256)


def spread_x(lines):
    count = lines.shape[0]
    wide = nn(lines, one_where(iota((32, 1024), 1) // 32 == iota((32, 1024), 0), bf16))
    mask = iota((32, 1024), 1) % 32 == iota((32, 1024), 0)
    return jnp.where(mask[None], wide[:, None, :], 0.0).astype(bf16).reshape(count * 32, 1024)


def apply_inverse(inverse, rows):
    tall = one_where(iota((256, 32), 0) % 32 == iota((256, 32), 1))
    wide = nt(nn(tall, inverse, precision=HIGH), tall, precision=HIGH)
    wide = jnp.where(iota((256, 256), 0) // 32 == iota((256, 256), 1) // 32, wide, 0.0)
    count = rows.shape[0] // 256
    return jnp.concatenate([nn(wide, rows[256 * i : 256 * i + 256], precision=HIGH) for i in range(count)], axis=0)


def row_of(s_ref, i, j):
    return pl.multiple_of((((s_ref[0] + 4 - j) % 4) * 4 + (s_ref[1] + 4 - i) % 4) * 16, 16)


def halves(value):
    high = value.astype(bf16)
    return high, (value - high.astype(f32)).astype(bf16)


def part_kernel(s_ref, n0, n1, n2, n3, f0, f1, f2, f3, part_ref, lx_ref, lz_ref, plane_ref, m0_ref, m1_ref, m2_ref, m3_ref, w_high, w_low):
    k = pl.program_id(0)

    @pl.when(k == 0)
    def _():
        for i in range(4):
            for j in range(4):
                rows = pl.ds(row_of(s_ref, i, j), 16)
                for r in range(16):
                    plane_ref[r, rows] = (n0, n1, n2, n3)[i][j, r]
                    plane_ref[16 + r, rows] = (f0, f1, f2, f3)[i][j, r]
        line_z = lz_ref[...]
        gram = nt(line_z, line_z)
        high, low = halves(gram)
        middle, low = halves(gram - high.astype(f32))
        tile = jnp.concatenate([high.astype(f32), middle.astype(f32), low.astype(f32), jnp.zeros((32, 160), f32)], axis=1)
        for ref in (m1_ref, m2_ref, m3_ref):
            ref[16] = tile.astype(bf16)

        def step(s, _):
            rows = pl.ds(pl.multiple_of(s * 32, 32), 32)
            w_high[rows], w_low[rows] = halves(nt(line_z, plane_ref[s]))
            return 0

        lax.fori_loop(0, 32, step, 0, unroll=4)

    kron = spread_x(lx_ref[...])
    total = part_ref[...].reshape(512, 256) - nn(kron, w_high[...]) - nn(kron, w_low[...])
    for which, ref in enumerate((m0_ref, m1_ref, m2_ref, m3_ref)):

        @pl.when(k == which)
        def _(ref=ref):
            ref[:16] = total.reshape(16, 32, 256).astype(ref.dtype)


def xy_kernel(s_ref, ly_ref, lz_ref, old_ref, own_ref, g1_ref, g2_ref, g3_ref, new_ref, inv_ref):
    total, gram = own_ref[...], nt(lz_ref[...], lz_ref[...])
    for ref in (g1_ref, g2_ref, g3_ref):
        total = total + ref[:16].astype(f32)
        tile = ref[16].astype(f32)
        gram = gram + (tile[:, :32] + (tile[:, 32:64] + tile[:, 64:96]))
    both = invert(jnp.stack([gram, nt(ly_ref[...], ly_ref[...])]))
    inverse = both[0]
    inv_ref[...] = both[1]
    old = old_ref[...].astype(f32).reshape(512, 256)
    new = old + apply_inverse(inverse, total.reshape(512, 256) - old)
    new_ref[...] = new.astype(bf16).reshape(16, 32, 256)


def side_kernel(s_ref, plane_ref, rho_ref, q_ref, b_ref, yp_ref, zp_ref, sums_ref, gz_ref, xy_ref):
    k = pl.program_id(0)

    @pl.when(k == 0)
    def _():
        def step(s, carry):
            y_cross, z_cross = carry
            over_y = nn(jnp.concatenate(halves(b_ref[s]), axis=0), plane_ref[s])
            over_z = nt(jnp.concatenate(halves(q_ref[s]), axis=0), plane_ref[s])
            return y_cross + over_z[:32] + over_z[32:], z_cross + over_y[:32] + over_y[32:]

        zero = jnp.zeros((32, 256), f32)
        y_cross, z_cross = lax.fori_loop(0, 32, step, (zero, zero), unroll=4)
        gz_ref[:, :256] = yp_ref[...] - y_cross
        gz_ref[:, 256:] = jnp.concatenate([sums_ref[0], sums_ref[1], jnp.zeros((32, 64), f32)], axis=1)
        xy_ref[:, :256] = zp_ref[...] - z_cross
        xy_ref[:, 256:] = jnp.concatenate([sums_ref[2], sums_ref[3], jnp.zeros((32, 64), f32)], axis=1)

    total = jnp.zeros((256, 512), f32)
    for first in range(0, 16, 8):
        rows = [slice(16 * j, 16 * j + 16) for j in range(first, first + 8)]
        left = jnp.concatenate([rho_ref[:, r, :].reshape(256, 256) for r in rows], axis=1)
        right = jnp.concatenate([plane_ref[:, r, :].reshape(512, 256) for r in rows], axis=1)
        total = total + nt(left, right)
    total = jnp.where(iota((256, 512), 0) % 16 == iota((256, 512), 1) % 16, total, 0.0)
    over_x = nn(one_where(iota((16, 256), 1) // 16 == iota((16, 256), 0)), total, precision=HIGH)
    turned = (iota((32, 512), 1) // 16 + 16 * s_ref[3]) % 32 == iota((32, 512), 0)
    over_x = nt(one_where(turned), over_x, precision=HIGH)
    placed = one_where(iota((16, 128), 1) == iota((16, 128), 0) + 16 * k + 64)
    gz_ref[:, 256:] += nn(over_x, placed, precision=HIGH)


def xz_kernel(s_ref, plane_ref, ty_ref, pz_ref, lx_ref, ly_ref, inv_ref, new_ref, u_high, u_low):
    @pl.when(pl.program_id(0) == 0)
    def _():
        line_y = ly_ref[...]

        def step(s, _):
            rows = pl.ds(pl.multiple_of(s * 32, 32), 32)
            u_high[rows], u_low[rows] = halves(nn(line_y, plane_ref[s]))
            return 0

        lax.fori_loop(0, 32, step, 0, unroll=4)

    kron = spread_x(lx_ref[...])
    total = ty_ref[...].reshape(512, 256) - nn(kron, u_high[...]) - nn(kron, u_low[...])
    old = pz_ref[...].astype(f32).reshape(512, 256)
    new_ref[...] = (old + apply_inverse(inv_ref[...], total - old)).astype(bf16).reshape(16, 32, 256)


def last_kernel(s_ref, sums_ref, side_ref, lx_ref, ly_ref, lz_ref, inv_ref, x_out, y_out, z_out):
    sums = sums_ref[...]
    gram_xz, gram_yz, gram_xy, gram_x = (sums[:, first : first + 32] for first in (256, 288, 640, 672))
    inverse = invert(jnp.stack([gram_xz, gram_yz, gram_xy, gram_x]))

    def solved(which, part, old):
        return old + nn(inverse[which], part - old, precision=HIGH)

    line_x = lx_ref[...].astype(f32)
    x_out[...] = solved(1, side_ref[...] - nn(gram_yz, line_x, precision=HIGH), line_x).astype(bf16)
    y_out[...] = solved(0, sums[:, :256], ly_ref[...].astype(f32)).astype(bf16)
    z_out[...] = solved(2, sums[:, 384:640], lz_ref[...].astype(f32)).astype(bf16)
    inv_ref[...] = inverse[3]


def contract(form, left, right):
    return jnp.einsum(form, left, right, preferred_element_type=f32)


def exact(form, left, right):
    return jnp.einsum(form, left, right, precision=HIGH, preferred_element_type=f32)


def ordered(mine, other, second, axis):
    return jnp.concatenate([jnp.where(second, other, mine), jnp.where(second, mine, other)], axis=axis)


def all_sum(value, axis):
    return (value + hop(value, axis, 2)) + (hop(value, axis, 1) + hop(value, axis, 3))


def fold(value, axis):
    count = sizes[axis]
    for bit in (1, 2)[: count // 2]:
        value = value + lax.ppermute(value, axis, [(i, i ^ bit) for i in range(count)])
    return value


def update(inverse, part, old):
    old = old.astype(f32)
    shape = part.shape
    step = jnp.dot(inverse, (part - old).reshape(32, -1), precision=HIGH)
    return (old + step.reshape(shape)).astype(bf16)


def phase(*values):
    return lax.optimization_barrier(values)


def shards(target, plane_xy, plane_xz, plane_yz, line_x, line_y, line_z):
    at = {name: lax.axis_index(name) for name in sizes}
    scalars = jnp.stack([at["y"], at["x"], at["zl"], at["c"], at["gz"]]).astype(jnp.int32)
    second_c, second_z = at["c"] == 1, at["zl"] == 1
    shape = jax.ShapeDtypeStruct
    lines = [whole((32, 256))] * 2

    half = lambda value, which: lax.dynamic_slice_in_dim(value, which * 16, 16, 0)
    own, other = half(plane_yz, at["c"]), half(plane_yz, 1 - at["c"])
    here = ordered(own, pair_hop(other, 1), second_c, 1)
    there = ordered(pair_hop(own, 2), pair_hop(other, 3), second_c, 1)
    block = ordered(here, there, second_z, 1)
    block, scalars = phase(block, scalars)

    got = [hop(block, "y", shift) for shift in range(1, 4)]
    px, pz = plane_xy.transpose(1, 0, 2), plane_xz.transpose(1, 0, 2)
    block = jnp.stack([block] + got)
    block, px, pz, scalars = phase(block, px, pz, scalars)
    got = [hop(block, "x", shift) for shift in range(1, 4)]
    far = [hop(block, "c", 1)]
    blocks = lambda k, s: (k, 0, 0)
    resident = pl.BlockSpec(memory_space=pltpu.VMEM)
    tiles = [pl.BlockSpec(size, blocks) for size in ((8, 256, 256), (8, 32, 256), (8, 32, 256))]
    rho, ty, xy_part, y_part, z_part = call(
        rho_kernel, "rho", scalars, (8,), tiles + lines, [resident] + tiles[1:] + lines,
        [shape((64, 256, 256), bf16)] + [shape((64, 32, 256), f32)] * 2 + [shape((32, 256), f32)] * 2,
        [], (target, px, pz, line_y, line_z), 24,
    )

    back = jnp.roll(line_x, -16 * at["c"], axis=0)
    to_block = lambda j, s: ((j // 4 + 4 - s[0]) % 4, (j % 4) ^ s[1], 0, 0, 0)
    keep, send = call(
        yz_kernel, "yz", scalars, (16,),
        [whole((32, 64)), resident],
        [pl.BlockSpec((1, 1, 16, 16, 256), to_block)] * 2,
        [shape((4, 4, 16, 16, 256), bf16)] * 2,
        [pltpu.VMEM((512, 1024), bf16)], (back, rho), 16,
    )
    got, far, send, scalars = phase(got, far, send, scalars)
    near = [block] + got
    came, far = hop(send, "c", 1), far + [hop(piece, "c", 1) for piece in got]
    rows = Layout(major_to_minor=(0, 1, 2))
    q_part = with_layout_constraint(contract("sx,xrz->srz", back, pz), rows)
    b_part = with_layout_constraint(contract("sx,xry->sry", back, px), rows)
    far, came, q_part, b_part, scalars = phase(far, came, q_part, b_part, scalars)
    pieces = [keep[i].astype(f32) + came[i].astype(f32) for i in range(4)]
    sent = [pieces[2][:2].astype(bf16), pieces[2][2:].astype(bf16)]
    sent, scalars = phase(sent, scalars)
    sent = [hop(sent[0], "y", 1), hop(sent[1], "y", 3)]

    back_t = back.T
    turned = lambda k, s: ((s[4] + k) % 4, 0, 0)
    plane, mine, *parts = call(
        part_kernel, "part", scalars, (4,),
        [whole((4, 16, 16, 256))] * 8
        + [pl.BlockSpec((16, 32, 256), turned), pl.BlockSpec((16, 32), lambda k, s: ((s[4] + k) % 4, 0)), whole((32, 256))],
        [resident, whole((16, 32, 256))] + [whole((17, 32, 256))] * 3,
        [shape((32, 256, 256), bf16), shape((16, 32, 256), f32)] + [shape((17, 32, 256), bf16)] * 3,
        [pltpu.VMEM((1024, 256), bf16)] * 2, (*near, *far, xy_part, back_t, line_z), 28,
    )
    parts, sent, scalars = phase(parts, sent, scalars)
    ahead = (pieces[1] + jnp.concatenate([sent[0].astype(f32), jnp.zeros((2, 16, 16, 256), f32)])).astype(bf16)
    behind = (pieces[3] + jnp.concatenate([jnp.zeros((2, 16, 16, 256), f32), sent[1].astype(f32)])).astype(bf16)
    ahead, behind, scalars = phase(ahead, behind, scalars)
    sent = [hop(ahead, "y", 1), hop(behind, "y", 3)]
    parts = [hop(part, "gz", shift) for shift, part in enumerate(parts, 1)]
    sums = call(
        small_kernel, "small", scalars, (1,),
        [whole((64, 32, 256))] * 2 + [whole((4, 32, 256)), whole((32, 64))],
        whole((4, 32, 32)),
        shape((4, 32, 32), f32),
        [], (px, pz, plane_yz.transpose(1, 0, 2), line_x), 16,
    )
    both, rest = call(
        side_kernel, "side", scalars, (4,),
        [resident, pl.BlockSpec((16, 256, 256), blocks), resident, resident] + lines + [whole((4, 32, 32))],
        [whole((32, 384))] * 2,
        [shape((32, 384), f32)] * 2,
        [], (plane, rho, q_part, b_part, y_part, z_part, sums), 52,
    )
    parts, sent, both, rest, scalars = phase(parts, sent, both, rest, scalars)
    here = pieces[0][:2] + sent[0][:2].astype(f32) + sent[1][:2].astype(f32)
    there = pieces[0][2:] + sent[0][2:].astype(f32) + sent[1][2:].astype(f32)
    there, scalars = phase(there, scalars)
    there = lax.ppermute(there, "x", [(i, i ^ 2) for i in range(4)])

    both = all_sum(both, "gz")
    mine, inv_y = call(
        xy_kernel, "xy", scalars, (1,),
        lines + [pl.BlockSpec((16, 32, 256), lambda k, s: (s[4], 0, 0)), whole((16, 32, 256))] + [whole((17, 32, 256))] * 3,
        [whole((16, 32, 256)), whole((32, 32))],
        [shape((16, 32, 256), bf16), shape((32, 32), f32)],
        [], (line_y, line_z, px, mine, *parts), 20,
    )
    mine, both, there, scalars = phase(mine, both, there, scalars)
    x_side = both[:, 320:]
    both = jnp.concatenate([both, rest], axis=1)

    quarters = [mine] + [hop(mine, "gz", shift) for shift in range(1, 4)]
    both = fold(both, "zl")
    both, scalars = phase(both, scalars)
    new_xz = call(
        xz_kernel, "xz", scalars, (4,),
        [resident, pl.BlockSpec((16, 32, 256), blocks), pl.BlockSpec((16, 32, 256), blocks)]
        + [pl.BlockSpec((16, 32), lambda k, s: (k, 0)), whole((32, 256)), whole((32, 32))],
        pl.BlockSpec((16, 32, 256), blocks),
        shape((64, 32, 256), bf16),
        [pltpu.VMEM((1024, 256), bf16)] * 2, (plane, ty, pz, back_t, line_y, inv_y), 20,
    )
    both = fold(both, "y")
    total = lax.ppermute(here[1] + there[1], "x", [(i, i ^ 1) for i in range(4)])
    total = here[0] + there[0] + total
    both, total = phase(both, total)
    both = fold(both, "x")
    region = lambda which: lax.dynamic_slice_in_dim(total, which * 8, 8, 1)
    total = region(at["zl"]) + hop(region(1 - at["zl"]), "zl", 1)
    both, total = phase(both, total)
    both = fold(both, "c")
    region = lambda which: lax.dynamic_slice_in_dim(total, which * 4, 4, 1)
    yz_side = ordered(region(at["c"]), hop(region(1 - at["c"]), "c", 1), second_c, 0)
    both, quarters[3] = phase(both, quarters[3])
    new_xy = jnp.zeros((32, 64, 256), bf16)
    for shift, piece in enumerate(quarters):
        new_xy = lax.dynamic_update_slice_in_dim(new_xy, piece.transpose(1, 0, 2), ((at["gz"] + 4 - shift) % 4) * 16, 1)
    inv_x, new_x, new_y, new_z = call(
        last_kernel, "last", scalars, (1,),
        [whole((32, 768))] + [whole((32, 64))] * 2 + lines, [whole((32, 32)), whole((32, 64))] + lines,
        [shape((32, 32), f32), shape((32, 64), bf16)] + [shape((32, 256), bf16)] * 2,
        [], (both, x_side, line_x, line_y, line_z), 16,
    )
    new_yz = update(inv_x, yz_side - exact("rs,syz->ryz", both[:, 672:704], plane_yz.astype(f32)), plane_yz)
    return (new_xy, new_xz.transpose(1, 0, 2), new_yz, new_x, new_y, new_z)


def solution(mesh):
    shape = tuple(sizes.values())
    mesh = Mesh(mesh.devices.reshape(shape), tuple(sizes))
    xy = ("y", "x", "zl", "c")
    outs = (
        P(None, xy, None),
        P(None, xy, "gz"),
        P(None, xy, "gz"),
        P(None, xy),
        P(),
        P(None, "gz"),
    )
    return jax.shard_map(
        shards,
        mesh=mesh,
        in_specs=(P(xy, None, "gz"),) + outs,
        out_specs=outs,
        check_vma=False,
    )
```

```python
import functools

import jax
import jax.numpy as jnp
from jax import lax
from jax.experimental import pallas as pl
from jax.experimental.layout import Layout, with_layout_constraint
from jax.experimental.pallas import tpu as pltpu
from jax.sharding import Mesh, PartitionSpec as P

ridge = 1.0
f32 = jnp.float32
bf16 = jnp.bfloat16
sizes = {"y": 4, "x": 4, "zl": 2, "c": 2, "gz": 4}
HIGH = lax.Precision.HIGHEST
MB = 2**20


def hop(value, axis, shift):
    count = sizes[axis]
    return lax.ppermute(value, axis, [(i, (i + shift) % count) for i in range(count)])


def pair_hop(value, flip):
    return lax.ppermute(value, ("zl", "c"), [(i, i ^ flip) for i in range(4)])


def nn(left, right, **kw):
    return lax.dot_general(left, right, (((1,), (0,)), ((), ())), preferred_element_type=f32, **kw)


def nt(left, right, **kw):
    return lax.dot_general(left, right, (((1,), (1,)), ((), ())), preferred_element_type=f32, **kw)


def tn(left, right):
    return lax.dot_general(left, right, (((0,), (0,)), ((), ())), preferred_element_type=f32)


def iota(shape, axis):
    return lax.broadcasted_iota(jnp.int32, shape, axis)


def one_where(mask, kind=f32):
    return jnp.where(mask, 1.0, 0.0).astype(kind)


def call(kernel, name, scalars, grid, in_specs, out_specs, out_shape, scratch, args, limit=50, aliases=None):
    return pl.pallas_call(
        kernel,
        name=name,
        input_output_aliases=aliases or {},
        out_shape=out_shape,
        grid_spec=pltpu.PrefetchScalarGridSpec(
            num_scalar_prefetch=1, grid=grid, in_specs=in_specs, out_specs=out_specs, scratch_shapes=scratch
        ),
        compiler_params=pltpu.CompilerParams(vmem_limit_bytes=limit * MB),
        cost_estimate=pl.CostEstimate(flops=1000, bytes_accessed=1000, transcendentals=0),
    )(scalars, *args)


def whole(shape):
    return pl.BlockSpec(shape, lambda *_: (0,) * len(shape))


def invert(work):
    shape = work.shape
    rows, cols = iota(shape, 1), iota(shape, 2)
    work = work + ridge * one_where(rows == cols)
    for k in range(shape[1]):
        row, col = work[:, k : k + 1, :], work[:, :, k : k + 1]
        pivot = 1.0 / work[:, k : k + 1, k : k + 1]
        scaled = row * pivot
        work = jnp.where(cols == k, 0.0, work) - col * jnp.where(cols == k, pivot, scaled)
        work = jnp.where(rows == k, jnp.where(cols == k, pivot, scaled), work)
    return work


def small_kernel(s_ref, px_ref, pz_ref, own_ref, lx_ref, sums_ref):
    def step(x, carry):
        xy, xz = carry
        return xy + nt(px_ref[x], px_ref[x]), xz + nt(pz_ref[x], pz_ref[x])

    zero = jnp.zeros((32, 32), f32)
    gram_xy, gram_xz = lax.fori_loop(0, 64, step, (zero, zero), unroll=8)
    gram_yz = zero
    for y in range(4):
        gram_yz = gram_yz + nt(own_ref[y], own_ref[y])
    sums_ref[0] = gram_xz
    sums_ref[1] = gram_yz
    sums_ref[2] = gram_xy
    sums_ref[3] = nt(lx_ref[...], lx_ref[...])


def rho_kernel(s_ref, t_ref, px_ref, pz_ref, ly_ref, lz_ref, rho_ref, ty_ref, xy_ref, yp_ref, zp_ref):
    line_y, line_z = ly_ref[...], lz_ref[...]

    @pl.when(pl.program_id(0) == 0)
    def _():
        yp_ref[...] = jnp.zeros_like(yp_ref)
        zp_ref[...] = jnp.zeros_like(zp_ref)

    def step(x, _):
        over_y = jnp.concatenate([line_y, px_ref[x]], axis=0)
        over_z = jnp.concatenate([pz_ref[x], line_z], axis=0)
        rho = (t_ref[x].astype(f32) - tn(over_y, over_z)).astype(bf16)
        rho_ref[8 * pl.program_id(0) + x] = rho
        from_z = nt(over_z, rho)
        from_y = nn(over_y, rho)
        ty_ref[x] = from_y[:32]
        zp_ref[...] += from_y[32:]
        yp_ref[...] += from_z[:32]
        xy_ref[x] = from_z[32:]
        return 0

    lax.fori_loop(0, 8, step, 0, unroll=8)


def yz_kernel(s_ref, lx_ref, rho_ref, keep_ref, send_ref, kron):
    @pl.when(pl.program_id(0) == 0)
    def _():
        spread = one_where(iota((64, 1024), 1) // 16 == iota((64, 1024), 0), bf16)
        wide = nn(lx_ref[...], spread)
        mask = iota((16, 1024), 1) % 16 == iota((16, 1024), 0)
        for r in range(32):
            kron[16 * r : 16 * r + 16] = jnp.where(mask, wide[r : r + 1], 0.0).astype(bf16)

    rows = pl.ds(pl.multiple_of(16 * pl.program_id(0), 16), 16)
    out = nn(kron[...], rho_ref[:, rows, :].reshape(1024, 256)).astype(bf16)
    keep_ref[...] = out[:256].reshape(1, 1, 16, 16, 256)
    send_ref[...] = out[256:].reshape(1, 1, 16, 16, 256)


def spread_x(lines):
    count = lines.shape[0]
    wide = nn(lines, one_where(iota((32, 1024), 1) // 32 == iota((32, 1024), 0), bf16))
    mask = iota((32, 1024), 1) % 32 == iota((32, 1024), 0)
    return jnp.where(mask[None], wide[:, None, :], 0.0).astype(bf16).reshape(count * 32, 1024)


def wide_inverse(inverse):
    tall = one_where(iota((256, 32), 0) % 32 == iota((256, 32), 1))
    wide = nt(nn(tall, inverse, precision=HIGH), tall, precision=HIGH)
    return jnp.where(iota((256, 256), 0) // 32 == iota((256, 256), 1) // 32, wide, 0.0)


def apply_wide(wide, rows):
    count = rows.shape[0] // 256
    return jnp.concatenate([nn(wide, rows[256 * i : 256 * i + 256], precision=HIGH) for i in range(count)], axis=0)


def row_of(s_ref, i, j):
    return pl.multiple_of((((s_ref[0] + 4 - j) % 4) * 4 + (s_ref[1] + 4 - i) % 4) * 16, 16)


def halves(value):
    high = value.astype(bf16)
    return high, (value - high.astype(f32)).astype(bf16)


def part_kernel(s_ref, n0, n1, n2, n3, f0, f1, f2, f3, part_ref, lx_ref, lz_ref, plane_ref, m0_ref, m1_ref, m2_ref, m3_ref, w_high, w_low):
    k = pl.program_id(0)

    @pl.when(k == 0)
    def _():
        for i in range(4):
            for j in range(4):
                rows = pl.ds(row_of(s_ref, i, j), 16)
                for r in range(16):
                    plane_ref[r, rows] = (n0, n1, n2, n3)[i][j, r]
                    plane_ref[16 + r, rows] = (f0, f1, f2, f3)[i][j, r]
        line_z = lz_ref[...]
        gram = nt(line_z, line_z)
        high, low = halves(gram)
        middle, low = halves(gram - high.astype(f32))
        tile = jnp.concatenate([high.astype(f32), middle.astype(f32), low.astype(f32), jnp.zeros((32, 160), f32)], axis=1)
        for ref in (m1_ref, m2_ref, m3_ref):
            ref[16] = tile.astype(bf16)

        def step(s, _):
            rows = pl.ds(pl.multiple_of(s * 32, 32), 32)
            w_high[rows], w_low[rows] = halves(nt(line_z, plane_ref[s]))
            return 0

        lax.fori_loop(0, 32, step, 0, unroll=4)

    kron = spread_x(lx_ref[...])
    total = part_ref[...].reshape(512, 256) - nn(kron, w_high[...]) - nn(kron, w_low[...])
    for which, ref in enumerate((m0_ref, m1_ref, m2_ref, m3_ref)):

        @pl.when(k == which)
        def _(ref=ref):
            ref[:16] = total.reshape(16, 32, 256).astype(ref.dtype)


def xy_kernel(s_ref, ly_ref, lz_ref, old_ref, own_ref, g1_ref, g2_ref, g3_ref, new_ref, inv_ref):
    total, gram = own_ref[...], nt(lz_ref[...], lz_ref[...])
    for ref in (g1_ref, g2_ref, g3_ref):
        total = total + ref[:16].astype(f32)
        tile = ref[16].astype(f32)
        gram = gram + (tile[:, :32] + (tile[:, 32:64] + tile[:, 64:96]))
    both = invert(jnp.stack([gram, nt(ly_ref[...], ly_ref[...])]))
    inverse = both[0]
    inv_ref[...] = both[1]
    old = old_ref[...].astype(f32).reshape(512, 256)
    new = old + apply_wide(wide_inverse(inverse), total.reshape(512, 256) - old)
    new_ref[...] = new.astype(bf16).reshape(16, 32, 256)


def side_kernel(s_ref, plane_ref, rho_ref, q_ref, b_ref, yp_ref, zp_ref, sums_ref, gz_ref, xy_ref):
    k = pl.program_id(0)

    @pl.when(k == 0)
    def _():
        def step(s, carry):
            y_cross, z_cross = carry
            over_y = nn(jnp.concatenate(halves(b_ref[s]), axis=0), plane_ref[s])
            over_z = nt(jnp.concatenate(halves(q_ref[s]), axis=0), plane_ref[s])
            return y_cross + over_z[:32] + over_z[32:], z_cross + over_y[:32] + over_y[32:]

        zero = jnp.zeros((32, 256), f32)
        y_cross, z_cross = lax.fori_loop(0, 32, step, (zero, zero), unroll=4)
        gz_ref[:, :256] = yp_ref[...] - y_cross
        gz_ref[:, 256:] = jnp.concatenate([sums_ref[0], sums_ref[1], jnp.zeros((32, 64), f32)], axis=1)
        xy_ref[:, :256] = zp_ref[...] - z_cross
        xy_ref[:, 256:] = jnp.concatenate([sums_ref[2], sums_ref[3], jnp.zeros((32, 64), f32)], axis=1)

    total = jnp.zeros((256, 512), f32)
    for first in range(0, 16, 8):
        rows = [slice(16 * j, 16 * j + 16) for j in range(first, first + 8)]
        left = jnp.concatenate([rho_ref[:, r, :].reshape(256, 256) for r in rows], axis=1)
        right = jnp.concatenate([plane_ref[:, r, :].reshape(512, 256) for r in rows], axis=1)
        total = total + nt(left, right)
    total = jnp.where(iota((256, 512), 0) % 16 == iota((256, 512), 1) % 16, total, 0.0)
    over_x = nn(one_where(iota((16, 256), 1) // 16 == iota((16, 256), 0)), total, precision=HIGH)
    turned = (iota((32, 512), 1) // 16 + 16 * s_ref[3]) % 32 == iota((32, 512), 0)
    over_x = nt(one_where(turned), over_x, precision=HIGH)
    placed = one_where(iota((16, 128), 1) == iota((16, 128), 0) + 16 * k + 64)
    gz_ref[:, 256:] += nn(over_x, placed, precision=HIGH)


def xz_kernel(s_ref, plane_ref, ty_ref, pz_ref, lx_ref, ly_ref, inv_ref, new_ref, u_high, u_low, wide):
    @pl.when(pl.program_id(0) == 0)
    def _():
        wide[...] = wide_inverse(inv_ref[...])
        line_y = ly_ref[...]

        def step(s, _):
            rows = pl.ds(pl.multiple_of(s * 32, 32), 32)
            u_high[rows], u_low[rows] = halves(nn(line_y, plane_ref[s]))
            return 0

        lax.fori_loop(0, 32, step, 0, unroll=4)

    kron = spread_x(lx_ref[...])
    total = ty_ref[...].reshape(512, 256) - nn(kron, u_high[...]) - nn(kron, u_low[...])
    old = pz_ref[...].astype(f32).reshape(512, 256)
    new_ref[...] = (old + apply_wide(wide[...], total - old)).astype(bf16).reshape(16, 32, 256)


def last_kernel(s_ref, sums_ref, side_ref, lx_ref, ly_ref, lz_ref, inv_ref, x_out, y_out, z_out):
    sums = sums_ref[...]
    gram_xz, gram_yz, gram_xy, gram_x = (sums[:, first : first + 32] for first in (256, 288, 640, 672))
    inverse = invert(jnp.stack([gram_xz, gram_yz, gram_xy, gram_x]))

    def solved(which, part, old):
        return old + nn(inverse[which], part - old, precision=HIGH)

    line_x = lx_ref[...].astype(f32)
    x_out[...] = solved(1, side_ref[...] - nn(gram_yz, line_x, precision=HIGH), line_x).astype(bf16)
    y_out[...] = solved(0, sums[:, :256], ly_ref[...].astype(f32)).astype(bf16)
    z_out[...] = solved(2, sums[:, 384:640], lz_ref[...].astype(f32)).astype(bf16)
    inv_ref[...] = inverse[3]


def contract(form, left, right):
    return jnp.einsum(form, left, right, preferred_element_type=f32)


def exact(form, left, right):
    return jnp.einsum(form, left, right, precision=HIGH, preferred_element_type=f32)


def ordered(mine, other, second, axis):
    return jnp.concatenate([jnp.where(second, other, mine), jnp.where(second, mine, other)], axis=axis)


def all_sum(value, axis):
    return (value + hop(value, axis, 2)) + (hop(value, axis, 1) + hop(value, axis, 3))


def fold(value, axis):
    count = sizes[axis]
    for bit in (1, 2)[: count // 2]:
        value = value + lax.ppermute(value, axis, [(i, i ^ bit) for i in range(count)])
    return value


def update(inverse, part, old):
    old = old.astype(f32)
    shape = part.shape
    step = jnp.dot(inverse, (part - old).reshape(32, -1), precision=HIGH)
    return (old + step.reshape(shape)).astype(bf16)


def phase(*values):
    return lax.optimization_barrier(values)


def shards(target, plane_xy, plane_xz, plane_yz, line_x, line_y, line_z):
    at = {name: lax.axis_index(name) for name in sizes}
    scalars = jnp.stack([at["y"], at["x"], at["zl"], at["c"], at["gz"]]).astype(jnp.int32)
    second_c, second_z = at["c"] == 1, at["zl"] == 1
    shape = jax.ShapeDtypeStruct
    lines = [whole((32, 256))] * 2

    half = lambda value, which: lax.dynamic_slice_in_dim(value, which * 16, 16, 0)
    own, other = half(plane_yz, at["c"]), half(plane_yz, 1 - at["c"])
    here = ordered(own, pair_hop(other, 1), second_c, 1)
    there = ordered(pair_hop(own, 2), pair_hop(other, 3), second_c, 1)
    block = ordered(here, there, second_z, 1)
    block, scalars = phase(block, scalars)

    got = [hop(block, "y", shift) for shift in range(1, 4)]
    px, pz = plane_xy.transpose(1, 0, 2), plane_xz.transpose(1, 0, 2)
    block = jnp.stack([block] + got)
    block, px, pz, scalars = phase(block, px, pz, scalars)
    got = [hop(block, "x", shift) for shift in range(1, 4)]
    far = [hop(block, "c", 1)]
    blocks = lambda k, s: (k, 0, 0)
    resident = pl.BlockSpec(memory_space=pltpu.VMEM)
    tiles = [pl.BlockSpec(size, blocks) for size in ((8, 256, 256), (8, 32, 256), (8, 32, 256))]
    rho, ty, xy_part, y_part, z_part = call(
        rho_kernel, "rho", scalars, (8,), tiles + lines, [resident] + tiles[1:] + lines,
        [shape((64, 256, 256), bf16)] + [shape((64, 32, 256), f32)] * 2 + [shape((32, 256), f32)] * 2,
        [], (target, px, pz, line_y, line_z), 24,
    )

    back = jnp.roll(line_x, -16 * at["c"], axis=0)
    to_block = lambda j, s: ((j // 4 + 4 - s[0]) % 4, (j % 4) ^ s[1], 0, 0, 0)
    keep, send = call(
        yz_kernel, "yz", scalars, (16,),
        [whole((32, 64)), resident],
        [pl.BlockSpec((1, 1, 16, 16, 256), to_block)] * 2,
        [shape((4, 4, 16, 16, 256), bf16)] * 2,
        [pltpu.VMEM((512, 1024), bf16)], (back, rho), 16,
    )
    got, far, send, scalars = phase(got, far, send, scalars)
    near = [block] + got
    came, far = hop(send, "c", 1), far + [hop(piece, "c", 1) for piece in got]
    rows = Layout(major_to_minor=(0, 1, 2))
    q_part = with_layout_constraint(contract("sx,xrz->srz", back, pz), rows)
    b_part = with_layout_constraint(contract("sx,xry->sry", back, px), rows)
    far, came, q_part, b_part, scalars = phase(far, came, q_part, b_part, scalars)
    pieces = [keep[i].astype(f32) + came[i].astype(f32) for i in range(4)]
    sent = [pieces[2][:2].astype(bf16), pieces[2][2:].astype(bf16)]
    sent, scalars = phase(sent, scalars)
    sent = [hop(sent[0], "y", 1), hop(sent[1], "y", 3)]

    back_t = back.T
    turned = lambda k, s: ((s[4] + k) % 4, 0, 0)
    plane, mine, *parts = call(
        part_kernel, "part", scalars, (4,),
        [whole((4, 16, 16, 256))] * 8
        + [pl.BlockSpec((16, 32, 256), turned), pl.BlockSpec((16, 32), lambda k, s: ((s[4] + k) % 4, 0)), whole((32, 256))],
        [resident, whole((16, 32, 256))] + [whole((17, 32, 256))] * 3,
        [shape((32, 256, 256), bf16), shape((16, 32, 256), f32)] + [shape((17, 32, 256), bf16)] * 3,
        [pltpu.VMEM((1024, 256), bf16)] * 2, (*near, *far, xy_part, back_t, line_z), 28,
    )
    parts, sent, scalars = phase(parts, sent, scalars)
    ahead = (pieces[1] + jnp.concatenate([sent[0].astype(f32), jnp.zeros((2, 16, 16, 256), f32)])).astype(bf16)
    behind = (pieces[3] + jnp.concatenate([jnp.zeros((2, 16, 16, 256), f32), sent[1].astype(f32)])).astype(bf16)
    ahead, behind, scalars = phase(ahead, behind, scalars)
    sent = [hop(ahead, "y", 1), hop(behind, "y", 3)]
    parts = [hop(part, "gz", shift) for shift, part in enumerate(parts, 1)]
    sums = call(
        small_kernel, "small", scalars, (1,),
        [whole((64, 32, 256))] * 2 + [whole((4, 32, 256)), whole((32, 64))],
        whole((4, 32, 32)),
        shape((4, 32, 32), f32),
        [], (px, pz, plane_yz.transpose(1, 0, 2), line_x), 16,
    )
    both, rest = call(
        side_kernel, "side", scalars, (4,),
        [resident, pl.BlockSpec((16, 256, 256), blocks), resident, resident] + lines + [whole((4, 32, 32))],
        [whole((32, 384))] * 2,
        [shape((32, 384), f32)] * 2,
        [], (plane, rho, q_part, b_part, y_part, z_part, sums), 52,
    )
    parts, sent, both, rest, scalars = phase(parts, sent, both, rest, scalars)
    here = pieces[0][:2] + sent[0][:2].astype(f32) + sent[1][:2].astype(f32)
    there = pieces[0][2:] + sent[0][2:].astype(f32) + sent[1][2:].astype(f32)
    there, scalars = phase(there, scalars)
    there = lax.ppermute(there, "x", [(i, i ^ 2) for i in range(4)])

    both = all_sum(both, "gz")
    mine, inv_y = call(
        xy_kernel, "xy", scalars, (1,),
        lines + [pl.BlockSpec((16, 32, 256), lambda k, s: (s[4], 0, 0)), whole((16, 32, 256))] + [whole((17, 32, 256))] * 3,
        [whole((16, 32, 256)), whole((32, 32))],
        [shape((16, 32, 256), bf16), shape((32, 32), f32)],
        [], (line_y, line_z, px, mine, *parts), 20,
    )
    new_xz = call(
        xz_kernel, "xz", scalars, (4,),
        [resident, pl.BlockSpec((16, 32, 256), blocks), pl.BlockSpec((16, 32, 256), blocks)]
        + [pl.BlockSpec((16, 32), lambda k, s: (k, 0)), whole((32, 256)), whole((32, 32))],
        pl.BlockSpec((16, 32, 256), blocks),
        shape((64, 32, 256), bf16),
        [pltpu.VMEM((1024, 256), bf16)] * 2 + [pltpu.VMEM((256, 256), f32)], (plane, ty, pz, back_t, line_y, inv_y), 20,
    )
    mine, both, there, new_xz = phase(mine, both, there, new_xz)
    x_side = both[:, 320:]
    both = jnp.concatenate([both, rest], axis=1)

    quarters = [mine] + [hop(mine, "gz", shift) for shift in range(1, 4)]
    both = fold(fold(both, "zl"), "y")
    total = lax.ppermute(here[1] + there[1], "x", [(i, i ^ 1) for i in range(4)])
    total = here[0] + there[0] + total
    both, total = phase(both, total)
    both = fold(both, "x")
    region = lambda which: lax.dynamic_slice_in_dim(total, which * 8, 8, 1)
    total = region(at["zl"]) + hop(region(1 - at["zl"]), "zl", 1)
    both, total = phase(both, total)
    both = fold(both, "c")
    region = lambda which: lax.dynamic_slice_in_dim(total, which * 4, 4, 1)
    yz_side = ordered(region(at["c"]), hop(region(1 - at["c"]), "c", 1), second_c, 0)
    both, quarters[3] = phase(both, quarters[3])
    new_xy = jnp.zeros((32, 64, 256), bf16)
    for shift, piece in enumerate(quarters):
        new_xy = lax.dynamic_update_slice_in_dim(new_xy, piece.transpose(1, 0, 2), ((at["gz"] + 4 - shift) % 4) * 16, 1)
    inv_x, new_x, new_y, new_z = call(
        last_kernel, "last", scalars, (1,),
        [whole((32, 768))] + [whole((32, 64))] * 2 + lines, [whole((32, 32)), whole((32, 64))] + lines,
        [shape((32, 32), f32), shape((32, 64), bf16)] + [shape((32, 256), bf16)] * 2,
        [], (both, x_side, line_x, line_y, line_z), 16,
    )
    new_yz = update(inv_x, yz_side - exact("rs,syz->ryz", both[:, 672:704], plane_yz.astype(f32)), plane_yz)
    return (new_xy, new_xz.transpose(1, 0, 2), new_yz, new_x, new_y, new_z)


def solution(mesh):
    shape = tuple(sizes.values())
    mesh = Mesh(mesh.devices.reshape(shape), tuple(sizes))
    xy = ("y", "x", "zl", "c")
    outs = (
        P(None, xy, None),
        P(None, xy, "gz"),
        P(None, xy, "gz"),
        P(None, xy),
        P(),
        P(None, "gz"),
    )
    return jax.shard_map(
        shards,
        mesh=mesh,
        in_specs=(P(xy, None, "gz"),) + outs,
        out_specs=outs,
        check_vma=False,
    )
```
